32 devices in a mesh: row: 8 (over y, x, core), col: 4 (over z).
Axes of the slice: x: 2, y: 2, z: 4, core: 2. Of those that a mesh axis runs over, the one named last changes fastest.
Arguments:
- tokens: bfloat16 [2, 16384, 768], P(None, ('row', 'col')), may hold values from -6 to 6
- seg_ids: int32 [2, 16384], P(None, ('row', 'col')), may hold values from 0 to 3, as said below
- pad_mask: int32 [2, 16384], P(None, ('row', 'col')), may hold values from 0 to 1, as said below
- rand_blocks: int32 [2, 256, 3], P(None, ('row', 'col')), may hold values from 0 to 15
- w_qkv: bfloat16 [2, 768, 2304], P(None, 'row', 'col'), may hold values from -0.21875 to 0.21875
- w_out: bfloat16 [2, 768, 768], P(None, 'row', 'col'), may hold values from -2.5 to 2.5
- w_up: bfloat16 [2, 768, 3072], P(None, 'row', 'col'), may hold values from -0.21875 to 0.21875
- w_down: bfloat16 [2, 3072, 768], P(None, 'row', 'col'), may hold values from -0.109375 to 0.109375
- layer_vectors: bfloat16 [2, 8, 768], P(None, None, 'col'), may hold values from -1.5 to 1.5, as said below
- bias_up: bfloat16 [2, 3072], P(None, 'col'), may hold values from -1.5 to 1.5
- d_out: bfloat16 [2, 16384, 768], P(None, ('row', 'col')), may hold values from -6 to 6
Outputs:
- output: bfloat16 [2, 16384, 768], P(None, ('row', 'col'))
- d_tokens: float32 [2, 16384, 768], P(None, ('row', 'col'))
- grad_qkv: float32 [2, 768, 2304], P(None, 'row', 'col')
- grad_out: float32 [2, 768, 768], P(None, 'row', 'col')
- grad_up: float32 [2, 768, 3072], P(None, 'row', 'col')
- grad_down: float32 [2, 3072, 768], P(None, 'row', 'col')
- grad_vectors: float32 [2, 8, 768], P(None, None, 'col')
- grad_bias_up: float32 [2, 3072], P(None, 'col')
The draws below stay inside these ranges and needn't reach their ends.
Inputs may be any that keep to these rules, and one draw needn't show every extreme that they name: `seg_ids`: within each aligned sequence of 1024 tokens the numbers never fall, start at 0 and end at 3, each step by one; every document has at least 204 tokens. `pad_mask`: within each aligned sequence of 1024 tokens the ones come first, followed by 1 to 256 zeros. `layer_vectors`: gains near 1, biases near 0.
All inputs are finite; a program needn't handle non-finite values.
Results may differ from the reference program's by a relative error of at most 0.02.
Values may be sent and summed in bfloat16 or wider, within the bound.
A program may use at most 256 MiB of HBM per device.

```python
import jax
import jax.numpy as jnp
from jax import lax

D = 768
HEADS = 12
FF = 3072
BLOCK = 64
RANDB = 3
LAYERS = 2
MB = 2
DOCS = 4
HEAD = 64
SEQ_LEN = 1024
TOKENS = 16384


def draw_seg_ids(key, part):
    seq_count = TOKENS // SEQ_LEN
    least_doc = SEQ_LEN // 5
    extra = jax.random.randint(jax.random.fold_in(key, 11), (MB, seq_count, DOCS - 1), 0, SEQ_LEN // 20 + 1)
    steps_in = jnp.arange(1, DOCS, dtype=jnp.int32)
    cut_points = least_doc * steps_in[None, None, :] + jnp.cumsum(extra, axis=-1).astype(jnp.int32)
    places = jnp.arange(SEQ_LEN, dtype=jnp.int32)
    doc_ids = jnp.sum((places[None, None, :, None] >= cut_points[:, :, None, :]).astype(jnp.int32), axis=-1)
    return doc_ids.reshape(MB, TOKENS).astype(jnp.int32)


def draw_pad_mask(key, part):
    seq_count = TOKENS // SEQ_LEN
    padding = jax.random.randint(jax.random.fold_in(key, 23), (MB, seq_count, 1), 1, SEQ_LEN // 4 + 1)
    places = jnp.arange(SEQ_LEN, dtype=jnp.int32)
    return (places[None, None, :] < SEQ_LEN - padding).astype(jnp.int32).reshape(MB, TOKENS)


def draw_layer_vectors(key, part):
    inner = jax.random.fold_in(key, 37)
    base_draw = jnp.clip(jax.random.normal(inner, (LAYERS, 8, D), jnp.float32), -5.0, 5.0)
    spread = jnp.array([0.3, 0.3, 0.3, 0.3, 0.1, 0.3, 0.1, 0.3], jnp.float32)
    centre = jnp.array([0.0, 0.0, 0.0, 0.0, 1.0, 0.0, 1.0, 0.0], jnp.float32)
    return (base_draw * spread[None, :, None] + centre[None, :, None]).astype(jnp.bfloat16)


def place_ends(values, stream_key, least, top_value):
    dims = values.shape
    index_at = [jax.random.randint(jax.random.fold_in(stream_key, axis), (), 0, dims[axis]) for axis in range(len(dims))]
    values = values.at[tuple(index_at)].set(least)
    longest = dims.index(max(dims))
    index_at[longest] = (index_at[longest] + 1) % dims[longest]
    return values.at[tuple(index_at)].set(top_value)


def levels(own_key, extent, cuts, low, high):
    gain = 1.0
    for dim, shards_of in cuts:
        heights = jax.random.uniform(jax.random.fold_in(jax.random.fold_in(own_key, 6), dim), (shards_of,), jnp.float32, low / len(cuts), high / len(cuts))
        gain = gain * jnp.repeat(jnp.exp(heights), extent[dim] // shards_of).reshape((-1,) + (1,) * (len(extent) - 1 - dim))
    return gain


def normal_values(own_key, dims, deviation, bound, split=(), kind=jnp.bfloat16):
    entries = jax.random.normal(own_key, dims, jnp.float32) * deviation
    if len(split) > 0:
        entries = levels(own_key, dims, split, -0.22, 0.18) * entries
    return jnp.clip(entries, min=-bound, max=bound).astype(kind)


def setup_inputs(seed: int = 0) -> dict:
    seeds = jax.random.split(jax.random.key(seed), 12)
    return {
        "tokens": normal_values(seeds[0], (MB, TOKENS, D), 1.0, 6.0, ((1, 32),)),
        "seg_ids": draw_seg_ids(jax.random.fold_in(seeds[11], 71), 0),
        "pad_mask": draw_pad_mask(jax.random.fold_in(seeds[11], 71), 0),
        "rand_blocks": place_ends(jax.random.randint(seeds[3], (MB, TOKENS // BLOCK, RANDB), 0, SEQ_LEN // BLOCK), jax.random.fold_in(seeds[3], 1), 0, (SEQ_LEN // BLOCK) - 1).astype(jnp.int32),
        "w_qkv": normal_values(seeds[4], (LAYERS, D, 3 * D), D ** -0.5, 0.21875, ((1, 8), (2, 4))),
        "w_out": normal_values(seeds[5], (LAYERS, D, D), 6 ** -0.5, 2.5, ((1, 8), (2, 4))),
        "w_up": normal_values(seeds[6], (LAYERS, D, FF), D ** -0.5, 0.21875, ((1, 8), (2, 4))),
        "w_down": normal_values(seeds[7], (LAYERS, FF, D), FF ** -0.5, 0.109375, ((1, 8), (2, 4))),
        "layer_vectors": draw_layer_vectors(jax.random.fold_in(seeds[11], 71), 0),
        "bias_up": normal_values(seeds[9], (LAYERS, FF), 0.3, 1.5, ((1, 4),)),
        "d_out": normal_values(seeds[10], (MB, TOKENS, D), 1.0, 6.0, ((1, 32),)),
    }


@jax.custom_vjp
def low(v):
    return lax.optimization_barrier(v.astype(jnp.bfloat16)).astype(jnp.float32)

@jax.custom_vjp
def low_back(v):
    return v

def low_keep(v):
    return (low(v), None)

def low_pass(kept, grad):
    return (grad,)

def back_keep(v):
    return (v, None)

def back_low(kept, grad):
    return (low(grad),)
low.defvjp(low_keep, low_pass)
low_back.defvjp(back_keep, back_low)
NEG_FILL = -1e+30
EPS = 1e-06
ROOT_HALF = 0.7071067811865476

def multiply(left_mat, right_mat):
    return jnp.dot(left_mat, right_mat, precision=lax.Precision.HIGHEST, preferred_element_type=jnp.float32)

def gelu_value(pre_act):
    return 0.5 * pre_act * (1.0 + lax.erf(pre_act * ROOT_HALF))

def norm_forward(residual, norm_gain, norm_shift):
    center = residual - lax.optimization_barrier(jnp.mean(residual, axis=-1, keepdims=True))
    return center * lax.rsqrt(lax.optimization_barrier(jnp.mean(center * center, axis=-1, keepdims=True)) + EPS) * norm_gain + norm_shift

def pattern(segment, padding, chosen):
    length = segment.shape[0]
    places = jnp.arange(length, dtype=jnp.int32)
    starts_at = jnp.concatenate([jnp.ones((1,), jnp.int32), (segment[1:] != segment[:-1]).astype(jnp.int32)])
    starts = lax.cummax(places * starts_at, axis=0)
    global_tok = places - starts < 2 * BLOCK
    block_num = places // BLOCK
    near_block = jnp.abs(block_num[:, None] - block_num[None, :]) <= 1
    blocks_all = length // BLOCK
    hit_table = jnp.any(chosen[:, :, None] == jnp.arange(blocks_all, dtype=jnp.int32)[None, None, :], axis=1)
    random_hit = jnp.broadcast_to(hit_table[:, None, :, None], (blocks_all, BLOCK, blocks_all, BLOCK)).reshape(length, length)
    same_doc = segment[:, None] == segment[None, :]
    allowed = same_doc & (padding[None, :] > 0) & (global_tok[:, None] | global_tok[None, :] | near_block | random_hit)
    return allowed | (places[:, None] == places[None, :])

def attend(inputs):
    queries, key_rows, values, allowed = inputs
    length = queries.shape[0]
    query_heads = queries.reshape(length, HEADS, HEAD)
    key_heads = key_rows.reshape(length, HEADS, HEAD)
    value_heads = values.reshape(length, HEADS, HEAD)
    scores = low_back(jnp.einsum('qhe,khe->hqk', query_heads, key_heads, precision=lax.Precision.HIGHEST) * HEAD ** (-0.5))
    scores = jnp.where(allowed[None], scores, NEG_FILL)
    exponent = jnp.exp(scores - lax.optimization_barrier(jnp.max(scores, axis=-1, keepdims=True)))
    prob_low = low(exponent / lax.optimization_barrier(jnp.sum(exponent, axis=-1, keepdims=True)))
    mixture = jnp.einsum('hqk,khe->qhe', prob_low, value_heads, precision=lax.Precision.HIGHEST)
    return mixture.reshape(length, HEADS * HEAD)

def block_forward(params, tokens_in, allowed):
    mat_qkv, mat_out, mat_up, mat_down, vectors, up_bias = params
    hidden = tokens_in
    seq_shape = (TOKENS // SEQ_LEN, SEQ_LEN, D)
    for layer_idx in range(LAYERS):
        if layer_idx > 0:
            hidden = low(hidden)
        vector_set = vectors[layer_idx]
        projected = multiply(hidden, mat_qkv[layer_idx])
        queries = low(low_back(projected[:, :D] + vector_set[0]))
        key_rows = low(low_back(projected[:, D:2 * D]))
        values = low(low_back(projected[:, 2 * D:] + vector_set[1]))
        mixture = lax.map(jax.checkpoint(attend), (queries.reshape(seq_shape), key_rows.reshape(seq_shape), values.reshape(seq_shape), allowed))
        mixture = low(low_back(mixture.reshape(TOKENS, D)))
        branch = low_back(multiply(mixture, mat_out[layer_idx]) + vector_set[2])
        first_out = low(norm_forward(hidden + branch, vector_set[4], vector_set[5]))
        pre_act = low_back(multiply(first_out, mat_up[layer_idx]) + up_bias[layer_idx])
        act_low = low(gelu_value(pre_act))
        down_out = low_back(multiply(act_low, mat_down[layer_idx]) + vector_set[3])
        hidden = norm_forward(first_out + down_out, vector_set[6], vector_set[7])
    return hidden

def reference(tokens, seg_ids, pad_mask, rand_blocks, w_qkv, w_out, w_up, w_down, layer_vectors, bias_up, d_out):
    params = (w_qkv.astype(jnp.float32), w_out.astype(jnp.float32), w_up.astype(jnp.float32), w_down.astype(jnp.float32), layer_vectors.astype(jnp.float32), bias_up.astype(jnp.float32))
    seq_count = TOKENS // SEQ_LEN
    outputs = []
    input_grads = []
    totals = None
    for micro_idx in range(MB):
        allowed = jax.vmap(pattern)(seg_ids[micro_idx].reshape(seq_count, SEQ_LEN), pad_mask[micro_idx].reshape(seq_count, SEQ_LEN), rand_blocks[micro_idx].reshape(seq_count, SEQ_LEN // BLOCK, RANDB))

        def forward(param_set, tokens_in):
            return block_forward(param_set, tokens_in, allowed)
        result, pullback = jax.vjp(forward, params, tokens[micro_idx].astype(jnp.float32))
        grad_params, grad_tokens = pullback(d_out[micro_idx].astype(jnp.float32))
        outputs.append(result.astype(jnp.bfloat16))
        input_grads.append(grad_tokens)
        totals = grad_params if totals is None else jax.tree.map(jnp.add, totals, grad_params)
    return (jnp.stack(outputs), jnp.stack(input_grads), totals[0], totals[1], totals[2], totals[3], totals[4], totals[5])
```

```python
import functools
import jax
import jax.numpy as jnp
from jax import lax
from jax.experimental import pallas as pl
from jax.experimental.pallas import tpu as pltpu
from jax.sharding import PartitionSpec as P

HEAD = 64
PAIR = 2 * HEAD
TILE = 128
UNROLL = 6
UNROLL_BACK = 6
WIDTHS = (3, 4, 5, 6, 8)
SCALE = HEAD ** (-0.5)
NT = (((1,), (1,)), ((), ()))
F32 = jnp.float32
BF16 = jnp.bfloat16


def stack_heads(rows):
    first = lax.broadcasted_iota(jnp.int32, rows.shape, 1) < HEAD
    zero = jnp.zeros_like(rows)
    return jnp.concatenate([jnp.where(first, rows, zero), jnp.where(first, zero, rows)], axis=0)


def unstack_heads(both):
    half = both.shape[1] // 2
    first = lax.broadcasted_iota(jnp.int32, (both.shape[0], half), 0) < HEAD
    return jnp.where(first, both[:, :half], both[:, half:])


def by_width(count, blocks, run):
    low = 0
    for width in WIDTHS:
        width = min(width, blocks)
        if width == low:
            continue
        pl.when((count > low) & (count <= width))(functools.partial(run, width))
        low = width


def attend_kernel(first_ref, count_ref, qkv_ref, bias_ref, mix_ref, lse_ref, vt_ref):
    length, width3 = qkv_ref.shape
    model = width3 // 3
    blocks = length // TILE
    pairs = model // PAIR
    vt_ref[...] = qkv_ref[:, 2 * model :].T

    def one_tile(tile, carry):
        rows = pl.ds(pl.multiple_of(tile * TILE, TILE), TILE)

        def run(width):
            begin = jnp.minimum(first_ref[tile], blocks - width)
            keys = pl.ds(pl.multiple_of(begin * TILE, TILE), width * TILE)

            def one_pair(pair):
                cols = pl.ds(pl.multiple_of(pair * PAIR, PAIR), PAIR)
                k_cols = pl.ds(pl.multiple_of(model + pair * PAIR, PAIR), PAIR)
                both_q = stack_heads(qkv_ref[rows, cols] * SCALE)
                bias = bias_ref[keys, rows]
                scores = lax.dot_general(
                    qkv_ref[keys, k_cols], both_q, NT, preferred_element_type=F32
                ) + jnp.concatenate([bias, bias], axis=1)
                peak = jnp.max(scores, axis=0, keepdims=True)
                exponent = jnp.exp(scores - peak)
                total = jnp.sum(exponent, axis=0, keepdims=True)
                mixed = jnp.dot(
                    vt_ref[cols, keys], exponent.astype(BF16), preferred_element_type=F32
                )
                mixed = unstack_heads(mixed / total)
                mix_ref[rows, cols] = mixed.T.astype(BF16)
                lse_ref[pair, pl.ds(tile, 1), :] = peak + jnp.log(total)

            def some_pairs(step, carry):
                for offset in range(UNROLL):
                    one_pair(step * UNROLL + offset)
                return carry

            lax.fori_loop(0, pairs // UNROLL, some_pairs, 0)

        by_width(count_ref[tile], blocks, run)
        return carry

    lax.fori_loop(0, blocks, one_tile, 0)


def attend_back_kernel(
    first_ref, count_ref, qkv_ref, grad_ref, bias_ref, lse_ref, out_ref, kt_ref, dk_ref, dv_ref
):
    length, width3 = qkv_ref.shape
    model = width3 // 3
    blocks = length // TILE
    pairs = model // PAIR
    kt_ref[...] = qkv_ref[:, model : 2 * model].T
    dk_ref[...] = jnp.zeros_like(dk_ref)
    dv_ref[...] = jnp.zeros_like(dv_ref)

    def one_tile(tile, carry):
        rows = pl.ds(pl.multiple_of(tile * TILE, TILE), TILE)

        def run(width):
            begin = jnp.minimum(first_ref[tile], blocks - width)
            keys = pl.ds(pl.multiple_of(begin * TILE, TILE), width * TILE)

            def one_pair(pair):
                cols, k_cols, v_cols = (
                    pl.ds(pl.multiple_of(part * model + pair * PAIR, PAIR), PAIR)
                    for part in range(3)
                )
                both_q = stack_heads(qkv_ref[rows, cols] * SCALE)
                both_g = stack_heads(grad_ref[rows, cols])
                lse = lse_ref[pair, pl.ds(tile, 1), :]
                bias = bias_ref[keys, rows]
                scores = lax.dot_general(
                    qkv_ref[keys, k_cols], both_q, NT, preferred_element_type=F32
                ) + jnp.concatenate([bias, bias], axis=1)
                prob = jnp.exp(scores - lse)
                grad_p = lax.dot_general(
                    qkv_ref[keys, v_cols], both_g, NT, preferred_element_type=F32
                )
                delta = jnp.sum(grad_p * prob, axis=0, keepdims=True)
                grad_s = (prob * (grad_p - delta)).astype(BF16)
                dv = jnp.dot(prob.astype(BF16), both_g, preferred_element_type=F32)
                dk = jnp.dot(grad_s, both_q, preferred_element_type=F32)
                grad_q = jnp.dot(kt_ref[cols, keys], grad_s, preferred_element_type=F32)
                return (cols, dv, dk, (unstack_heads(grad_q) * SCALE).T.astype(BF16))

            def some_pairs(step, carry):
                done = [one_pair(step * UNROLL_BACK + offset) for offset in range(UNROLL_BACK)]
                for cols, dv, dk, dq in done:
                    dv_ref[keys, cols] += dv
                    dk_ref[keys, cols] += dk
                    out_ref[rows, cols] = dq
                return carry

            lax.fori_loop(0, pairs // UNROLL_BACK, some_pairs, 0)

        by_width(count_ref[tile], blocks, run)
        return carry

    lax.fori_loop(0, blocks, one_tile, 0)
    out_ref[:, model : 2 * model] = dk_ref[...].astype(BF16)
    out_ref[:, 2 * model :] = dv_ref[...].astype(BF16)


VMEM_SPEC = pl.BlockSpec(memory_space=pltpu.VMEM)
SMEM_SPEC = pl.BlockSpec(memory_space=pltpu.SMEM)


def attend(first, count, qkv, bias):
    length, width3 = qkv.shape
    model = width3 // 3
    pairs, blocks = model // PAIR, length // TILE
    return pl.pallas_call(
        attend_kernel,
        out_shape=(
            jax.ShapeDtypeStruct((length, model), BF16),
            jax.ShapeDtypeStruct((pairs, blocks, 2 * TILE), F32),
        ),
        in_specs=[SMEM_SPEC, SMEM_SPEC, VMEM_SPEC, VMEM_SPEC],
        out_specs=(VMEM_SPEC, VMEM_SPEC),
        scratch_shapes=[pltpu.VMEM((model, length), BF16)],
        compiler_params=pltpu.CompilerParams(vmem_limit_bytes=40 << 20),
    )(first, count, qkv, bias)


def attend_back(first, count, qkv, grad_mix, bias, lse):
    length, width3 = qkv.shape
    model = width3 // 3
    return pl.pallas_call(
        attend_back_kernel,
        out_shape=jax.ShapeDtypeStruct((length, width3), BF16),
        in_specs=[SMEM_SPEC, SMEM_SPEC] + [VMEM_SPEC] * 4,
        out_specs=VMEM_SPEC,
        scratch_shapes=[
            pltpu.VMEM((model, length), BF16),
            pltpu.VMEM((length, model), F32),
            pltpu.VMEM((length, model), F32),
        ],
        compiler_params=pltpu.CompilerParams(vmem_limit_bytes=48 << 20),
    )(first, count, qkv, grad_mix, bias, lse)

NEG_FILL = -1e30
EPS = 1e-06
ROOT_HALF = 0.7071067811865476
INV_ROOT_TAU = 0.3989422804014327
BLOCK = 64


def norm_forward(residual, norm_gain, norm_shift):
    center = residual - jnp.mean(residual, axis=-1, keepdims=True)
    scale_inv = lax.rsqrt(jnp.mean(center * center, axis=-1, keepdims=True) + EPS)
    normed = center * scale_inv
    return (normed * norm_gain + norm_shift, normed, scale_inv)


def norm_backward(grad_y, normed, scale_inv, norm_gain):
    grad_n = grad_y * norm_gain
    return scale_inv * (
        grad_n
        - jnp.mean(grad_n, axis=-1, keepdims=True)
        - normed * jnp.mean(grad_n * normed, axis=-1, keepdims=True)
    )


def gelu_value(pre_act):
    return 0.5 * pre_act * (1.0 + lax.erf(pre_act * ROOT_HALF))


def gelu_slope(pre_act):
    return 0.5 * (1.0 + lax.erf(pre_act * ROOT_HALF)) + pre_act * INV_ROOT_TAU * jnp.exp(
        -0.5 * pre_act * pre_act
    )


def swapped(block):
    count = lax.axis_size("col")
    return lax.ppermute(block, "col", [(i, i ^ 1) for i in range(count)])


def pick(array, index):
    return lax.dynamic_index_in_dim(array, index, 0, keepdims=False)


def to_sequence(halves, parity):
    own = pick(halves, parity)
    other = swapped(pick(halves, 1 - parity))
    first = parity == 0
    return jnp.concatenate([jnp.where(first, own, other), jnp.where(first, other, own)])


def from_sequence(whole, parity, narrow):
    halves = whole.reshape((2, -1) + whole.shape[1:])
    own = pick(halves, parity)
    other = swapped(pick(halves, 1 - parity).astype(narrow)).astype(whole.dtype)
    first = parity == 0
    return jnp.stack([jnp.where(first, own, other), jnp.where(first, other, own)])


def key_pattern(seg, pad, rand):
    length = seg.shape[0]
    places = jnp.arange(length, dtype=jnp.int32)
    starts = jnp.sum((seg[None, :] < seg[:, None]).astype(jnp.int32), axis=1)
    ends = jnp.sum((seg[None, :] <= seg[:, None]).astype(jnp.int32), axis=1)
    whole = places - starts < 2 * BLOCK
    block = places // BLOCK
    chosen = jnp.repeat(rand, BLOCK, axis=0)
    near = jnp.abs(block[:, None] - block[None, :]) <= 1
    hit = jnp.zeros((length, length), bool)
    for slot in range(rand.shape[1]):
        hit = hit | (block[:, None] == chosen[None, :, slot])
    allowed = (
        (seg[:, None] == seg[None, :])
        & (pad[:, None] > 0)
        & (whole[:, None] | whole[None, :] | near | hit)
    )
    allowed = allowed | (places[:, None] == places[None, :])
    bias = jnp.where(allowed, 0.0, NEG_FILL).astype(F32)
    first = starts[::TILE] // TILE
    count = (ends[TILE - 1 :: TILE] + TILE - 1) // TILE - first
    return bias, first, count


def layer_forward(hidden, weights, pattern):
    mat_qkv, mat_out, mat_up, mat_down, vectors, up_bias = weights
    bias, first, count = pattern
    qkv_bias = jnp.concatenate([vectors[0], jnp.zeros_like(vectors[0]), vectors[1]])
    qkv = (jnp.dot(hidden, mat_qkv, preferred_element_type=F32) + qkv_bias).astype(BF16)
    mixture, lse = attend(first, count, qkv, bias)
    branch = jnp.dot(mixture, mat_out, preferred_element_type=F32) + vectors[2]
    first_norm, normed_one, inv_one = norm_forward(
        hidden.astype(F32) + branch, vectors[4], vectors[5]
    )
    first_out = first_norm.astype(BF16)
    pre_act = jnp.dot(first_out, mat_up, preferred_element_type=F32) + up_bias
    act_low = gelu_value(pre_act).astype(BF16)
    down_out = jnp.dot(act_low, mat_down, preferred_element_type=F32) + vectors[3]
    final_out, normed_two, inv_two = norm_forward(
        first_out.astype(F32) + down_out, vectors[6], vectors[7]
    )
    saved = (
        hidden, qkv, lse, mixture, normed_one, inv_one, first_out, pre_act, act_low, normed_two, inv_two,
    )
    return final_out.astype(BF16), saved


def layer_backward(grad_y, weights, saved, pattern):
    mat_qkv, mat_out, mat_up, mat_down, vectors, up_bias = weights
    (
        hidden, qkv, lse, mixture, normed_one, inv_one, first_out, pre_act, act_low, normed_two, inv_two,
    ) = saved
    bias, first, count = pattern
    width = hidden.shape[1]
    grad_gain_two = jnp.sum(grad_y * normed_two, axis=0)
    grad_shift_two = jnp.sum(grad_y, axis=0)
    grad_two = norm_backward(grad_y, normed_two, inv_two, vectors[6])
    grad_down_low = grad_two.astype(BF16)
    grad_bias_down = jnp.sum(grad_down_low.astype(F32), axis=0)
    grad_mat_down = jnp.einsum("tf,td->fd", act_low, grad_down_low, preferred_element_type=F32)
    grad_act = jnp.einsum("td,fd->tf", grad_down_low, mat_down, preferred_element_type=F32)
    grad_pre = (grad_act * gelu_slope(pre_act)).astype(BF16)
    grad_bias_hidden = jnp.sum(grad_pre.astype(F32), axis=0)
    grad_mat_up = jnp.einsum("td,tf->df", first_out, grad_pre, preferred_element_type=F32)
    grad_first = grad_two + jnp.einsum("tf,df->td", grad_pre, mat_up, preferred_element_type=F32)
    grad_gain_one = jnp.sum(grad_first * normed_one, axis=0)
    grad_shift_one = jnp.sum(grad_first, axis=0)
    grad_one = norm_backward(grad_first, normed_one, inv_one, vectors[4])
    grad_branch = grad_one.astype(BF16)
    grad_bias_out = jnp.sum(grad_branch.astype(F32), axis=0)
    grad_mat_out = jnp.einsum("td,te->de", mixture, grad_branch, preferred_element_type=F32)
    grad_mix = jnp.einsum("te,de->td", grad_branch, mat_out, preferred_element_type=F32)
    grad_qkv = attend_back(first, count, qkv, grad_mix.astype(BF16), bias, lse)
    grad_mat_qkv = jnp.einsum("td,te->de", hidden, grad_qkv, preferred_element_type=F32)
    grad_hidden = grad_one + jnp.einsum("te,de->td", grad_qkv, mat_qkv, preferred_element_type=F32)
    bias_qkv = jnp.sum(grad_qkv.astype(F32), axis=0)
    grad_rows = jnp.stack(
        [
            bias_qkv[:width], bias_qkv[2 * width :], grad_bias_out, grad_bias_down,
            grad_gain_one, grad_shift_one, grad_gain_two, grad_shift_two,
        ]
    )
    return grad_hidden, (grad_mat_qkv, grad_mat_out, grad_mat_up, grad_mat_down), grad_rows, grad_bias_hidden


def shards(
    tokens, seg_ids, pad_mask, rand_blocks, w_qkv, w_out, w_up, w_down, layer_vectors, bias_up, d_out
):
    layers = w_qkv.shape[0]
    parity = lax.axis_index("col") % 2
    marks = jnp.concatenate(
        [seg_ids, pad_mask, rand_blocks.reshape(rand_blocks.shape[0], -1)], axis=1
    )
    half = seg_ids.shape[1]
    marks = to_sequence(marks[:, None], parity)
    seg, pad = marks[:, :half].reshape(-1), marks[:, half : 2 * half].reshape(-1)
    rand = marks[:, 2 * half :].reshape(-1, rand_blocks.shape[2])
    pattern = key_pattern(seg, pad, rand)

    def fetch(layer):
        mats = tuple(
            lax.all_gather(
                lax.all_gather(w[layer], "col", axis=1, tiled=True), "row", axis=0, tiled=True
            )
            for w in (w_qkv, w_out, w_up, w_down)
        )
        return mats + (
            lax.all_gather(layer_vectors[layer], "col", axis=1, tiled=True).astype(F32),
            lax.all_gather(bias_up[layer], "col", axis=0, tiled=True).astype(F32),
        )

    weights = [fetch(layer) for layer in range(layers)]
    hidden = to_sequence(tokens, parity)
    kept = []
    for layer in range(layers):
        hidden, saved = layer_forward(hidden, weights[layer], pattern)
        kept.append(saved)
    output = from_sequence(hidden, parity, BF16)
    flow = to_sequence(d_out, parity).astype(F32)
    grads, vec_grads, up_grads = [None] * layers, [None] * layers, [None] * layers
    for layer in reversed(range(layers)):
        flow, mats, vec_grads[layer], up_grads[layer] = layer_backward(
            flow, weights[layer], kept[layer], pattern
        )
        grads[layer] = [
            lax.psum_scatter(
                lax.psum_scatter(m.astype(BF16), "row", scatter_dimension=0, tiled=True),
                "col", scatter_dimension=1, tiled=True,
            ).astype(F32)
            for m in mats
        ]
    d_tokens = from_sequence(flow, parity, BF16)
    vec = lax.psum_scatter(jnp.stack(vec_grads), "col", scatter_dimension=2, tiled=True)
    ups = lax.psum_scatter(jnp.stack(up_grads), "col", scatter_dimension=1, tiled=True)
    vec, ups = lax.psum((vec, ups), "row")
    mats = [jnp.stack([grads[layer][i] for layer in range(layers)]) for i in range(4)]
    return output, d_tokens, *mats, vec, ups


def solution(mesh):
    in_specs = (
        P(None, ("row", "col"), None),
        P(None, ("row", "col")),
        P(None, ("row", "col")),
        P(None, ("row", "col"), None),
        P(None, "row", "col"),
        P(None, "row", "col"),
        P(None, "row", "col"),
        P(None, "row", "col"),
        P(None, None, "col"),
        P(None, "col"),
        P(None, ("row", "col"), None),
    )
    out_specs = (
        P(None, ("row", "col"), None),
        P(None, ("row", "col"), None),
        P(None, "row", "col"),
        P(None, "row", "col"),
        P(None, "row", "col"),
        P(None, "row", "col"),
        P(None, None, "col"),
        P(None, "col"),
    )
    return jax.shard_map(shards, mesh=mesh, in_specs=in_specs, out_specs=out_specs, check_vma=False)
```

```python
import functools
import jax
import jax.numpy as jnp
from jax import lax
from jax.experimental import pallas as pl
from jax.experimental.pallas import tpu as pltpu
from jax.sharding import PartitionSpec as P

HEAD = 64
PAIR = 2 * HEAD
TILE = 128
VMEM_SPEC = pl.BlockSpec(memory_space=pltpu.VMEM)
UNROLL = 6
UNROLL_BACK = 6
WIDTHS = (3, 4, 5, 6, 8)
SCALE = HEAD ** (-0.5)
NT = (((1,), (1,)), ((), ()))
F32 = jnp.float32
BF16 = jnp.bfloat16


def stack_heads(rows):
    first = lax.broadcasted_iota(jnp.int32, rows.shape, 1) < HEAD
    zero = jnp.zeros_like(rows)
    return jnp.concatenate([jnp.where(first, rows, zero), jnp.where(first, zero, rows)], axis=0)


def unstack_heads(both):
    half = both.shape[1] // 2
    first = lax.broadcasted_iota(jnp.int32, (both.shape[0], half), 0) < HEAD
    return jnp.where(first, both[:, :half], both[:, half:])


def by_width(count, blocks, run):
    low = 0
    for width in WIDTHS:
        width = min(width, blocks)
        if width == low:
            continue
        pl.when((count > low) & (count <= width))(functools.partial(run, width))
        low = width


def attend_kernel(first_ref, count_ref, qkv_ref, bias_ref, mix_ref, lse_ref, vt_ref):
    length, width3 = qkv_ref.shape
    model = width3 // 3
    blocks = length // TILE
    pairs = model // PAIR
    vt_ref[...] = qkv_ref[:, 2 * model :].T

    def one_tile(tile, carry):
        rows = pl.ds(pl.multiple_of(tile * TILE, TILE), TILE)

        def run(width):
            begin = jnp.minimum(first_ref[tile], blocks - width)
            keys = pl.ds(pl.multiple_of(begin * TILE, TILE), width * TILE)

            def one_pair(pair):
                cols = pl.ds(pl.multiple_of(pair * PAIR, PAIR), PAIR)
                k_cols = pl.ds(pl.multiple_of(model + pair * PAIR, PAIR), PAIR)
                both_q = stack_heads(qkv_ref[rows, cols] * SCALE)
                bias = bias_ref[keys, rows]
                scores = lax.dot_general(
                    qkv_ref[keys, k_cols], both_q, NT, preferred_element_type=F32
                ) + jnp.concatenate([bias, bias], axis=1)
                peak = jnp.max(scores, axis=0, keepdims=True)
                exponent = jnp.exp(scores - peak)
                total = jnp.sum(exponent, axis=0, keepdims=True)
                mixed = jnp.dot(
                    vt_ref[cols, keys], exponent.astype(BF16), preferred_element_type=F32
                )
                mixed = unstack_heads(mixed / total)
                mix_ref[rows, cols] = mixed.T.astype(BF16)
                lse_ref[pair, pl.ds(tile, 1), :] = peak + jnp.log(total)

            def some_pairs(step, carry):
                for offset in range(UNROLL):
                    one_pair(step * UNROLL + offset)
                return carry

            lax.fori_loop(0, pairs // UNROLL, some_pairs, 0)

        by_width(count_ref[tile], blocks, run)
        return carry

    lax.fori_loop(0, blocks, one_tile, 0)


def attend_back_kernel(
    first_ref, count_ref, qkv_ref, grad_ref, bias_ref, lse_ref, out_ref, kt_ref, dk_ref, dv_ref
):
    length, width3 = qkv_ref.shape
    model = width3 // 3
    blocks = length // TILE
    pairs = model // PAIR
    kt_ref[...] = qkv_ref[:, model : 2 * model].T
    dk_ref[...] = jnp.zeros_like(dk_ref)
    dv_ref[...] = jnp.zeros_like(dv_ref)

    def one_tile(tile, carry):
        rows = pl.ds(pl.multiple_of(tile * TILE, TILE), TILE)

        def run(width):
            begin = jnp.minimum(first_ref[tile], blocks - width)
            keys = pl.ds(pl.multiple_of(begin * TILE, TILE), width * TILE)

            def one_pair(pair):
                cols, k_cols, v_cols = (
                    pl.ds(pl.multiple_of(part * model + pair * PAIR, PAIR), PAIR)
                    for part in range(3)
                )
                both_q = stack_heads(qkv_ref[rows, cols] * SCALE)
                both_g = stack_heads(grad_ref[rows, cols])
                lse = lse_ref[pair, pl.ds(tile, 1), :]
                bias = bias_ref[keys, rows]
                scores = lax.dot_general(
                    qkv_ref[keys, k_cols], both_q, NT, preferred_element_type=F32
                ) + jnp.concatenate([bias, bias], axis=1)
                prob = jnp.exp(scores - lse)
                grad_p = lax.dot_general(
                    qkv_ref[keys, v_cols], both_g, NT, preferred_element_type=F32
                )
                delta = jnp.sum(grad_p * prob, axis=0, keepdims=True)
                grad_s = (prob * (grad_p - delta)).astype(BF16)
                dv = jnp.dot(prob.astype(BF16), both_g, preferred_element_type=F32)
                dk = jnp.dot(grad_s, both_q, preferred_element_type=F32)
                grad_q = jnp.dot(kt_ref[cols, keys], grad_s, preferred_element_type=F32)
                return (cols, dv, dk, (unstack_heads(grad_q) * SCALE).T.astype(BF16))

            def some_pairs(step, carry):
                done = [one_pair(step * UNROLL_BACK + offset) for offset in range(UNROLL_BACK)]
                for cols, dv, dk, dq in done:
                    dv_ref[keys, cols] += dv
                    dk_ref[keys, cols] += dk
                    out_ref[rows, cols] = dq
                return carry

            lax.fori_loop(0, pairs // UNROLL_BACK, some_pairs, 0)

        by_width(count_ref[tile], blocks, run)
        return carry

    lax.fori_loop(0, blocks, one_tile, 0)
    out_ref[:, model : 2 * model] = dk_ref[...].astype(BF16)
    out_ref[:, 2 * model :] = dv_ref[...].astype(BF16)


SMEM_SPEC = pl.BlockSpec(memory_space=pltpu.SMEM)


def attend(first, count, qkv, bias):
    length, width3 = qkv.shape
    model = width3 // 3
    pairs, blocks = model // PAIR, length // TILE
    return pl.pallas_call(
        attend_kernel,
        out_shape=(
            jax.ShapeDtypeStruct((length, model), BF16),
            jax.ShapeDtypeStruct((pairs, blocks, 2 * TILE), F32),
        ),
        in_specs=[SMEM_SPEC, SMEM_SPEC, VMEM_SPEC, VMEM_SPEC],
        out_specs=(VMEM_SPEC, VMEM_SPEC),
        scratch_shapes=[pltpu.VMEM((model, length), BF16)],
        compiler_params=pltpu.CompilerParams(vmem_limit_bytes=40 << 20),
    )(first, count, qkv, bias)


def attend_back(first, count, qkv, grad_mix, bias, lse):
    length, width3 = qkv.shape
    model = width3 // 3
    return pl.pallas_call(
        attend_back_kernel,
        out_shape=jax.ShapeDtypeStruct((length, width3), BF16),
        in_specs=[SMEM_SPEC, SMEM_SPEC] + [VMEM_SPEC] * 4,
        out_specs=VMEM_SPEC,
        scratch_shapes=[
            pltpu.VMEM((model, length), BF16),
            pltpu.VMEM((length, model), F32),
            pltpu.VMEM((length, model), F32),
        ],
        compiler_params=pltpu.CompilerParams(vmem_limit_bytes=48 << 20),
    )(first, count, qkv, grad_mix, bias, lse)

NEG_FILL = -1e30
EPS = 1e-06
ROOT_HALF = 0.7071067811865476
INV_ROOT_TAU = 0.3989422804014327
BLOCK = 64


def norm_forward(residual, norm_gain, norm_shift):
    center = residual - jnp.mean(residual, axis=-1, keepdims=True)
    scale_inv = lax.rsqrt(jnp.mean(center * center, axis=-1, keepdims=True) + EPS)
    normed = center * scale_inv
    return (normed * norm_gain + norm_shift, normed, scale_inv)


def norm_backward(grad_y, normed, scale_inv, norm_gain):
    grad_n = grad_y * norm_gain
    return scale_inv * (
        grad_n
        - jnp.mean(grad_n, axis=-1, keepdims=True)
        - normed * jnp.mean(grad_n * normed, axis=-1, keepdims=True)
    )


def gelu_value(pre_act):
    return 0.5 * pre_act * (1.0 + lax.erf(pre_act * ROOT_HALF))


def gelu_slope(pre_act):
    return 0.5 * (1.0 + lax.erf(pre_act * ROOT_HALF)) + pre_act * INV_ROOT_TAU * jnp.exp(
        -0.5 * pre_act * pre_act
    )


def swapped(block):
    count = lax.axis_size("col")
    return lax.ppermute(block, "col", [(i, i ^ 1) for i in range(count)])


def pick(array, index):
    return lax.dynamic_index_in_dim(array, index, 0, keepdims=False)


def to_sequence(halves, parity):
    own = pick(halves, parity)
    other = swapped(pick(halves, 1 - parity))
    first = parity == 0
    return jnp.concatenate([jnp.where(first, own, other), jnp.where(first, other, own)])


def from_sequence(whole, parity, narrow):
    halves = whole.reshape((2, -1) + whole.shape[1:])
    own = pick(halves, parity)
    other = swapped(pick(halves, 1 - parity).astype(narrow)).astype(whole.dtype)
    first = parity == 0
    return jnp.stack([jnp.where(first, own, other), jnp.where(first, other, own)])


def key_pattern(seg, pad, rand):
    length = seg.shape[0]
    places = jnp.arange(length, dtype=jnp.int32)
    starts = jnp.sum((seg[None, :] < seg[:, None]).astype(jnp.int32), axis=1)
    ends = jnp.sum((seg[None, :] <= seg[:, None]).astype(jnp.int32), axis=1)
    whole = places - starts < 2 * BLOCK
    block = places // BLOCK
    chosen = jnp.repeat(rand, BLOCK, axis=0)
    near = jnp.abs(block[:, None] - block[None, :]) <= 1
    hit = jnp.zeros((length, length), bool)
    for slot in range(rand.shape[1]):
        hit = hit | (block[:, None] == chosen[None, :, slot])
    allowed = (
        (seg[:, None] == seg[None, :])
        & (pad[:, None] > 0)
        & (whole[:, None] | whole[None, :] | near | hit)
    )
    allowed = allowed | (places[:, None] == places[None, :])
    bias = jnp.where(allowed, 0.0, NEG_FILL).astype(F32)
    first = starts[::TILE] // TILE
    count = (ends[TILE - 1 :: TILE] + TILE - 1) // TILE - first
    return bias, first, count


def layer_forward(hidden, weights, pattern):
    mat_qkv, mat_out, mat_up, mat_down, vectors, up_bias = weights
    bias, first, count = pattern
    qkv_bias = jnp.concatenate([vectors[0], jnp.zeros_like(vectors[0]), vectors[1]])
    qkv = (jnp.dot(hidden, mat_qkv, preferred_element_type=F32) + qkv_bias).astype(BF16)
    mixture, lse = attend(first, count, qkv, bias)
    branch = jnp.dot(mixture, mat_out, preferred_element_type=F32) + vectors[2]
    first_norm, normed_one, inv_one = norm_forward(
        hidden.astype(F32) + branch, vectors[4], vectors[5]
    )
    first_out = first_norm.astype(BF16)
    pre_act = jnp.dot(first_out, mat_up, preferred_element_type=F32) + up_bias
    act_low = gelu_value(pre_act).astype(BF16)
    down_out = jnp.dot(act_low, mat_down, preferred_element_type=F32) + vectors[3]
    final_out, normed_two, inv_two = norm_forward(
        first_out.astype(F32) + down_out, vectors[6], vectors[7]
    )
    saved = (
        hidden, qkv, lse, mixture, normed_one, inv_one, first_out, pre_act, act_low, normed_two, inv_two,
    )
    return final_out.astype(BF16), saved


def layer_backward(grad_y, weights, saved, pattern):
    mat_qkv, mat_out, mat_up, mat_down, vectors, up_bias = weights
    (
        hidden, qkv, lse, mixture, normed_one, inv_one, first_out, pre_act, act_low, normed_two, inv_two,
    ) = saved
    bias, first, count = pattern
    width = hidden.shape[1]
    grad_gain_two = jnp.sum(grad_y * normed_two, axis=0)
    grad_shift_two = jnp.sum(grad_y, axis=0)
    grad_two = norm_backward(grad_y, normed_two, inv_two, vectors[6])
    grad_down_low = grad_two.astype(BF16)
    grad_bias_down = jnp.sum(grad_down_low.astype(F32), axis=0)
    grad_mat_down = jnp.einsum("tf,td->fd", act_low, grad_down_low, preferred_element_type=F32)
    grad_act = jnp.einsum("td,fd->tf", grad_down_low, mat_down, preferred_element_type=F32)
    grad_pre = (grad_act * gelu_slope(pre_act)).astype(BF16)
    grad_bias_hidden = jnp.sum(grad_pre.astype(F32), axis=0)
    grad_mat_up = jnp.einsum("td,tf->df", first_out, grad_pre, preferred_element_type=F32)
    grad_first = grad_two + jnp.einsum("tf,df->td", grad_pre, mat_up, preferred_element_type=F32)
    grad_gain_one = jnp.sum(grad_first * normed_one, axis=0)
    grad_shift_one = jnp.sum(grad_first, axis=0)
    grad_one = norm_backward(grad_first, normed_one, inv_one, vectors[4])
    grad_branch = grad_one.astype(BF16)
    grad_bias_out = jnp.sum(grad_branch.astype(F32), axis=0)
    grad_mat_out = jnp.einsum("td,te->de", mixture, grad_branch, preferred_element_type=F32)
    grad_mix = jnp.einsum("te,de->td", grad_branch, mat_out, preferred_element_type=F32)
    grad_qkv = attend_back(first, count, qkv, grad_mix.astype(BF16), bias, lse)
    grad_mat_qkv = jnp.einsum("td,te->de", hidden, grad_qkv, preferred_element_type=F32)
    grad_hidden = grad_one + jnp.einsum("te,de->td", grad_qkv, mat_qkv, preferred_element_type=F32)
    bias_qkv = jnp.sum(grad_qkv.astype(F32), axis=0)
    grad_rows = jnp.stack(
        [
            bias_qkv[:width], bias_qkv[2 * width :], grad_bias_out, grad_bias_down,
            grad_gain_one, grad_shift_one, grad_gain_two, grad_shift_two,
        ]
    )
    return grad_hidden, (grad_mat_qkv, grad_mat_out, grad_mat_up, grad_mat_down), grad_rows, grad_bias_hidden


ANY_SPEC = pl.BlockSpec(memory_space=pl.ANY)
DMA = pltpu.SemaphoreType.DMA


class Place:
    def __init__(self, rows, cols):
        self.rows, self.cols = rows, cols
        self.row, self.col = lax.axis_index("row"), lax.axis_index("col")
        self.core = self.row % 2
        self.bits = list(range(1, rows.bit_length() - 1))
        self.orders = (self.bits, self.bits[::-1])

    def flipped(self, row, bit):
        return row + (1 - 2 * ((row // 2**bit) % 2)) * 2**bit

    def partner(self, bit):
        return (self.flipped(self.row, bit), self.col)

    def others(self, bits):
        found = [self.row]
        for bit in bits:
            found += [self.flipped(row, bit) for row in found]
        return found

    def greet(self):
        barrier = pltpu.get_barrier_semaphore()

        def signal(row, col):
            pl.semaphore_signal(
                barrier, inc=1, device_id=(row, col), device_id_type=pl.DeviceIdType.MESH
            )

        for bit in [0, *self.bits]:
            signal(*self.partner(bit))
        pl.when(self.col > 0)(lambda: signal(self.row, self.col - 1))
        pl.when(self.col < self.cols - 1)(lambda: signal(self.row, self.col + 1))
        inside = jnp.where((self.col > 0) & (self.col < self.cols - 1), 1, 0)
        pl.semaphore_wait(barrier, len(self.bits) + 2 + inside)


def remote(src, dst, send, recv, target):
    return pltpu.make_async_remote_copy(
        src_ref=src,
        dst_ref=dst,
        send_sem=send,
        recv_sem=recv,
        device_id=target,
        device_id_type=pl.DeviceIdType.MESH,
    )


def run_stages(items):
    plan = []
    for order, (time, stages) in enumerate(items):
        for index, stage in enumerate(stages):
            plan.append((time + index, order, stage))
    for _, _, stage in sorted(plan, key=lambda step: step[:2]):
        stage()


class LineGather:
    def __init__(self, place, own, slot, sems):
        self.place, self.own, self.slot, self.sems = place, own, slot, sems

    def copies(self, hop, receiving):
        place = self.place
        col, cols = place.col, place.cols
        for way, step in ((0, 1), (1, -1)):
            target = col + step
            if receiving:
                slot = col - step * (hop + 1)
                valid = (slot >= 0) & (slot < cols)
            else:
                slot = col - step * hop
                valid = (slot >= 0) & (slot < cols) & (target >= 0) & (target < cols)
            src = self.own if hop == 0 and not receiving else self.slot(slot)
            yield valid, lambda src=src, slot=slot, way=way, target=target: remote(
                src,
                self.slot(slot),
                self.sems.at[0, way, hop],
                self.sems.at[1, way, hop],
                (place.row, target),
            )

    def start(self, hop):
        for valid, copy in self.copies(hop, False):
            pl.when(valid)(lambda copy=copy: copy().start())

    def wait_recv(self, hop):
        for valid, copy in self.copies(hop, True):
            pl.when(valid)(lambda copy=copy: copy().wait_recv())

    def wait_send(self, hop):
        for valid, copy in self.copies(hop, False):
            pl.when(valid)(lambda copy=copy: copy().wait_send())


def gather_item(place, own, whole, local_sem, line_sems, chip_sems, core_sems):
    hops = place.cols - 1
    row_slot = lambda col: whole.at[col, place.row // 2, place.core]
    line = LineGather(place, own, row_slot, line_sems)
    mine = lambda: pltpu.make_async_copy(own, row_slot(place.col), local_sem)
    half = place.cols // 2

    def chip_copies(phase, receiving):
        for part in range(2):
            order = place.orders[part]
            bit = order[phase]
            for index, row in enumerate(place.others(order[:phase])):
                if receiving:
                    row = place.flipped(row, bit)
                ref = whole.at[pl.ds(part * half, half), row // 2, row % 2]
                yield remote(
                    ref,
                    ref,
                    chip_sems.at[0, phase, part, index],
                    chip_sems.at[1, phase, part, index],
                    place.partner(bit),
                )

    def core_copy(receiving):
        ref = whole.at[:, :, 1 - place.core if receiving else place.core]
        return remote(ref, ref, core_sems.at[0], core_sems.at[1], place.partner(0))

    phases = len(place.bits)

    def first():
        mine().start()
        line.start(0)

    def hop_stage(hop):
        line.wait_recv(hop - 1)
        line.start(hop)

    def chip_stage(phase):
        if phase == 0:
            line.wait_recv(hops - 1)
            mine().wait()
        else:
            for copy in chip_copies(phase - 1, True):
                copy.wait_recv()
        for copy in chip_copies(phase, False):
            copy.start()

    def core_stage():
        for copy in chip_copies(phases - 1, True):
            copy.wait_recv()
        core_copy(False).start()

    def last():
        core_copy(True).wait_recv()
        core_copy(False).wait_send()
        for hop in range(hops):
            line.wait_send(hop)
        for phase in range(phases):
            for copy in chip_copies(phase, False):
                copy.wait_send()

    return (
        [first]
        + [functools.partial(hop_stage, hop) for hop in range(1, hops)]
        + [functools.partial(chip_stage, phase) for phase in range(phases)]
        + [core_stage, last]
    )


def gather_small_item(place, own, whole, local_sem, line_sems):
    hops = place.cols - 1
    line = LineGather(place, own, lambda col: whole.at[col], line_sems)
    mine = lambda: pltpu.make_async_copy(own, whole.at[place.col], local_sem)

    def first():
        mine().start()
        line.start(0)

    def hop_stage(hop):
        line.wait_recv(hop - 1)
        line.start(hop)

    def last():
        line.wait_recv(hops - 1)
        mine().wait()
        for hop in range(hops):
            line.wait_send(hop)

    return [first] + [functools.partial(hop_stage, hop) for hop in range(1, hops)] + [last]


def exchange_item(place, halves, whole, sems, delay):
    parity = place.col % 2
    copy = lambda: remote(
        halves.at[1 - parity],
        whole.at[parity],
        sems.at[0],
        sems.at[1],
        (place.row, place.col + 1 - 2 * parity),
    )
    arriving = lambda: remote(
        halves.at[1 - parity],
        whole.at[1 - parity],
        sems.at[0],
        sems.at[1],
        (place.row, place.col + 1 - 2 * parity),
    )
    mine = lambda: pltpu.make_async_copy(halves.at[parity], whole.at[parity], sems.at[2])

    def first():
        copy().start()
        mine().start()

    def last():
        arriving().wait_recv()
        copy().wait_send()
        mine().wait()

    return [first] + [lambda: None] * delay + [last]


def row_pieces(rs):
    return [(0, rs // 2), (rs // 2, rs // 2)] if rs % 32 == 0 and rs > 32 else [(0, rs)]


def gather_kernel(rows, cols, *refs):
    (full, lined), (small, tokens, marks) = (refs[:4], refs[4:8]), refs[8:11]
    (full_out, lined_out), (small_out, hidden, marks_out) = (refs[11:15], refs[15:19]), refs[19:22]
    local_sems, line_sems, chip_sems, core_sems, exchange_sems = refs[22:]
    place = Place(rows, cols)
    place.greet()
    items = [
        (0, exchange_item(place, marks, marks_out, exchange_sems.at[1], 16)),
        (0, gather_small_item(place, small, small_out, local_sems.at[0], line_sems.at[0])),
    ]
    number = 0
    for own, whole in zip(full, full_out):
        for begin, size in row_pieces(own.shape[0]):
            stages = gather_item(
                place,
                own.at[pl.ds(begin, size)],
                whole.at[:, :, :, pl.ds(begin, size)],
                local_sems.at[number + 1],
                line_sems.at[number + 1],
                chip_sems.at[number],
                core_sems.at[number],
            )
            items.append((number, stages))
            number += 1
    items.append((number, exchange_item(place, tokens, hidden, exchange_sems.at[0], 16)))
    for index, (own, whole) in enumerate(zip(lined, lined_out)):
        at = number + index
        items.append(
            (at, gather_small_item(place, own, whole, local_sems.at[at + 1], line_sems.at[at + 1]))
        )
    run_stages(items)


def gather_all(rows, cols, full, lined, small, tokens, marks):
    number = sum(len(row_pieces(x.shape[0])) for x in full)
    phases = rows.bit_length() - 2
    like = lambda x, lead=(): jax.ShapeDtypeStruct(lead + x.shape, x.dtype)
    outs = [like(x, (cols, rows // 2, 2)) for x in full] + [like(x, (cols,)) for x in lined]
    outs += [like(small, (cols,)), like(tokens), like(marks)]
    return pl.pallas_call(
        functools.partial(gather_kernel, rows, cols),
        out_shape=tuple(outs),
        in_specs=[ANY_SPEC] * 11,
        out_specs=(ANY_SPEC,) * 11,
        scratch_shapes=[
            DMA((number + len(lined) + 1,)),
            DMA((number + len(lined) + 1, 2, 2, cols - 1)),
            DMA((number, 2, phases, 2, 2 ** (phases - 1))),
            DMA((number, 2)),
            DMA((2, 3)),
        ],
        compiler_params=pltpu.CompilerParams(collective_id=0, has_side_effects=True),
    )(*full, *lined, small, tokens, marks)


class LineReduce:
    def __init__(self, place, slot, arrived, sems):
        self.place, self.slot, self.arrived, self.sems = place, slot, arrived, sems

    def copies(self, hop, receiving):
        place = self.place
        last = place.cols - 1
        for way, step in ((0, 1), (1, -1)):
            here = place.col if way == 0 else last - place.col
            from_start = here if not receiving else here - 1
            slot = last - hop + from_start
            valid = (from_start <= hop) & (from_start >= 0) & (from_start < last)
            slot = slot if way == 0 else last - slot
            yield valid, slot, way, lambda way=way, slot=slot, step=step: remote(
                self.slot(slot),
                self.arrived.at[way, hop],
                self.sems.at[0, way, hop],
                self.sems.at[1, way, hop],
                (place.row, place.col + step),
            )

    def start(self, hop):
        for valid, _, _, copy in self.copies(hop, False):
            pl.when(valid)(lambda copy=copy: copy().start())

    def wait_send(self, hop):
        for valid, _, _, copy in self.copies(hop, False):
            pl.when(valid)(lambda copy=copy: copy().wait_send())

    def take(self, hop):
        for valid, slot, way, copy in self.copies(hop, True):

            def add(slot=slot, way=way, copy=copy):
                pltpu.make_async_copy(
                    self.arrived.at[way, hop], self.arrived.at[way, hop], self.sems.at[1, way, hop]
                ).wait()
                ref = self.slot(slot)
                ref[...] = ref[...] + self.arrived.at[way, hop][...]

            pl.when(valid)(add)

    def finish(self, out):
        hop = self.place.cols - 2
        own = self.slot(self.place.col)
        out[...] = own[...].astype(F32)
        for valid, _, way, copy in self.copies(hop, True):

            def add(way=way):
                pltpu.make_async_copy(
                    self.arrived.at[way, hop], self.arrived.at[way, hop], self.sems.at[1, way, hop]
                ).wait()
                out[...] = out[...] + self.arrived.at[way, hop][...].astype(F32)

            pl.when(valid)(add)
        for hop in range(self.place.cols - 1):
            self.wait_send(hop)


def line_stages(line, out, before):
    hops = line.place.cols - 1

    def first():
        before()
        line.start(0)

    def hop_stage(hop):
        line.take(hop - 1)
        line.start(hop)

    return (
        [first]
        + [functools.partial(hop_stage, hop) for hop in range(1, hops)]
        + [lambda: line.finish(out)]
    )


def reduce_item(place, partial, out, sums, from_core, from_chips, from_line, sems):
    local_sem, core_sems, chip_sems, line_sems = sems
    half = place.cols // 2
    phases = len(place.bits)
    core_copy = lambda: remote(
        partial.at[:, :, 1 - place.core], from_core, core_sems.at[0], core_sems.at[1], place.partner(0)
    )
    load = lambda: pltpu.make_async_copy(partial.at[:, :, place.core], sums, local_sem)
    line = LineReduce(
        place, lambda col: sums.at[col, place.row // 2], from_line, line_sems
    )

    def chip_parts(phase):
        for part in range(2):
            order = place.orders[part][::-1]
            yield part, order[phase], order[phase + 1 :]

    def chip_copies(phase):
        for part, bit, rest in chip_parts(phase):
            for index, row in enumerate(place.others(rest)):
                row = place.flipped(row, bit)
                yield remote(
                    sums.at[pl.ds(part * half, half), row // 2],
                    from_chips[phase].at[part, index],
                    chip_sems.at[0, phase, part, index],
                    chip_sems.at[1, phase, part, index],
                    place.partner(bit),
                )

    def chip_take(phase):
        for part, _, rest in chip_parts(phase):
            for index, row in enumerate(place.others(rest)):
                arrived = from_chips[phase].at[part, index]
                pltpu.make_async_copy(arrived, arrived, chip_sems.at[1, phase, part, index]).wait()

                def add(col, carry, part=part, index=index, row=row):
                    ref = sums.at[part * half + col, row // 2]
                    ref[...] = ref[...] + from_chips[phase].at[part, index, col][...]
                    return carry

                lax.fori_loop(0, half, add, 0)

    def first():
        core_copy().start()
        load().start()

    def chip_stage(phase):
        if phase == 0:
            load().wait()
            core_copy().wait_recv()

            def add(slot, carry):
                col, pair = slot // (place.rows // 2), slot % (place.rows // 2)
                ref = sums.at[col, pair]
                ref[...] = ref[...] + from_core.at[col, pair][...]
                return carry

            lax.fori_loop(0, place.cols * (place.rows // 2), add, 0)
        else:
            chip_take(phase - 1)
        for copy in chip_copies(phase):
            copy.start()

    def last():
        core_copy().wait_send()
        for phase in range(phases):
            for copy in chip_copies(phase):
                copy.wait_send()

    return (
        [first]
        + [functools.partial(chip_stage, phase) for phase in range(phases)]
        + line_stages(line, out, lambda: chip_take(phases - 1))
        + [last]
    )


def reduce_line_item(place, partial, out, sums, from_line, local_sem, line_sems):
    load = lambda: pltpu.make_async_copy(partial, sums, local_sem)
    line = LineReduce(place, lambda col: sums.at[col], from_line, line_sems)
    return [lambda: load().start()] + line_stages(line, out, lambda: load().wait())


def reduce_small_item(place, partial, out, sums, arrived, from_line, sems, line_sems):
    bits = [0, *place.bits]
    line = LineReduce(place, lambda col: sums.at[col], from_line, line_sems)
    copy = lambda index: remote(
        sums, arrived.at[index], sems.at[0, index], sems.at[1, index], place.partner(bits[index])
    )

    def take(index):
        copy(index).wait()
        sums[...] = sums[...] + arrived[index]

    def stage(index):
        if index == 0:
            sums[...] = partial[...]
        else:
            take(index - 1)
        copy(index).start()

    return [functools.partial(stage, index) for index in range(len(bits))] + line_stages(
        line, out, lambda: take(len(bits) - 1)
    )


def reduce_kernel(rows, cols, full, lined, *refs):
    phases = rows.bit_length() - 2
    refs = list(refs)

    def take(number):
        taken = refs[:number]
        del refs[:number]
        return taken

    full_in, line_in, (small_in, tokens) = take(full), take(lined), take(2)
    full_out, line_out, (small_out, tokens_out) = take(full), take(lined), take(2)
    place = Place(rows, cols)
    place.greet()
    items = []
    small_sums, small_arrived, small_line, small_sems, small_line_sems = take(5)
    [token_sems] = take(1)
    parity = place.col % 2
    token_copy = lambda: remote(
        tokens, tokens_out, token_sems.at[0], token_sems.at[1], (place.row, place.col + 1 - 2 * parity)
    )
    time = 0
    for index in range(full):
        sums, from_core, from_line = take(3)
        from_chips = take(phases)
        local_sems, core_sems, chip_sems, line_sems = take(4)
        for piece, (begin, size) in enumerate(row_pieces(full_in[index].shape[-2])):
            rows_of = lambda ref, begin=begin, size=size: ref.at[
                (slice(None),) * (len(ref.shape) - 2) + (pl.ds(begin, size),)
            ]
            stages = reduce_item(
                place,
                rows_of(full_in[index]),
                rows_of(full_out[index]),
                rows_of(sums),
                rows_of(from_core),
                [rows_of(ref) for ref in from_chips],
                rows_of(from_line),
                (local_sems.at[piece], core_sems.at[piece], chip_sems.at[piece], line_sems.at[piece]),
            )
            items.append((time, stages))
            time += 1
    for index in range(lined):
        sums, from_line, local_sem, line_sems = take(4)
        items.append(
            (index, reduce_line_item(place, line_in[index], line_out[index], sums, from_line, local_sem.at[0], line_sems))
        )
    items.append(
        (1, reduce_small_item(place, small_in, small_out, small_sums, small_arrived, small_line, small_sems, small_line_sems))
    )
    items.append(
        (0, [lambda: token_copy().start()] + [lambda: None] * 12 + [lambda: token_copy().wait()])
    )
    run_stages(items)


def reduce_all(rows, cols, full, lined, small, tokens):
    phases = rows.bit_length() - 2
    hops = cols - 1
    shard = lambda x: x.shape[-2:]
    outs = [jax.ShapeDtypeStruct(shard(x), F32) for x in (*full, *lined, small)]
    outs.append(jax.ShapeDtypeStruct(tokens.shape, tokens.dtype))
    scratch = [
        pltpu.VMEM(small.shape, F32),
        pltpu.VMEM((phases + 1,) + small.shape, F32),
        pltpu.VMEM((2, hops) + shard(small), F32),
        DMA((2, phases + 1)),
        DMA((2, 2, hops)),
        DMA((2,)),
    ]
    for x in full:
        scratch += [
            pltpu.VMEM((cols, rows // 2) + shard(x), BF16),
            pltpu.VMEM((cols, rows // 2) + shard(x), BF16),
            pltpu.VMEM((2, hops) + shard(x), BF16),
        ]
        scratch += [
            pltpu.VMEM((2, 2 ** (phases - 1 - phase), cols // 2) + shard(x), BF16)
            for phase in range(phases)
        ]
        count = len(row_pieces(x.shape[-2]))
        scratch += [
            DMA((count,)),
            DMA((count, 2)),
            DMA((count, 2, phases, 2, 2 ** (phases - 1))),
            DMA((count, 2, 2, hops)),
        ]
    for x in lined:
        scratch += [
            pltpu.VMEM((cols,) + shard(x), BF16),
            pltpu.VMEM((2, hops) + shard(x), BF16),
            DMA((1,)),
            DMA((2, 2, hops)),
        ]
    many = len(full) + len(lined)
    return pl.pallas_call(
        functools.partial(reduce_kernel, rows, cols, len(full), len(lined)),
        out_shape=tuple(outs),
        in_specs=[ANY_SPEC] * many + [VMEM_SPEC, ANY_SPEC],
        out_specs=(VMEM_SPEC,) * (many + 1) + (ANY_SPEC,),
        scratch_shapes=scratch,
        compiler_params=pltpu.CompilerParams(
            collective_id=1, has_side_effects=True, vmem_limit_bytes=62 << 20
        ),
    )(*full, *lined, small, tokens)


def shards(
    rows, cols, tokens, seg_ids, pad_mask, rand_blocks, w_qkv, w_out, w_up, w_down, layer_vectors, bias_up, d_out
):
    layers = w_qkv.shape[0]
    parity = lax.axis_index("col") % 2
    half = seg_ids.shape[1]
    chosen = rand_blocks.reshape(2, 1, -1)
    chosen = jnp.pad(chosen, ((0, 0), (0, 0), (0, 128 - chosen.shape[2])))
    marks = jnp.concatenate(
        [seg_ids.reshape(2, -1, 128), pad_mask.reshape(2, -1, 128), chosen], axis=1
    )
    marks = jnp.pad(marks, ((0, 0), (0, -marks.shape[1] % 8), (0, 0)))
    part = layer_vectors.shape[2]
    small = jnp.concatenate([layer_vectors.reshape(-1, part), bias_up.reshape(-1, part)])
    small_rows = small.shape[0]
    small = jnp.pad(small, ((0, -small_rows % 16), (0, 0)))
    mats = (w_qkv, w_out, w_up, w_down)
    got = gather_all(
        rows, cols, [w[0] for w in mats], [w[1] for w in mats], small, tokens, marks
    )
    vectors = got[8][:, : layers * 8].transpose(1, 0, 2).reshape(layers, 8, -1).astype(F32)
    up_biases = got[8][:, layers * 8 : small_rows].reshape(cols, layers, -1).transpose(1, 0, 2)
    up_biases = up_biases.reshape(layers, -1).astype(F32)
    hidden = got[9].reshape(2 * half, -1)
    marks = got[10]
    lines = half // 128
    seg, pad = marks[:, :lines].reshape(-1), marks[:, lines : 2 * lines].reshape(-1)
    rand = marks[:, 2 * lines, : half // BLOCK * rand_blocks.shape[2]]
    pattern = key_pattern(seg, pad, rand.reshape(-1, rand_blocks.shape[2]))

    def assembled(slots):
        return slots.transpose(1, 2, 0, 3).reshape(rows * slots.shape[2], -1)

    first_mats = [assembled(g.reshape((cols, rows) + g.shape[3:])) for g in got[:4]]
    second_mats = [
        assembled(lax.all_gather(g, "row", axis=0).transpose(1, 0, 2, 3)) for g in got[4:8]
    ]
    weights = [
        (*layer_mats, vectors[layer], up_biases[layer])
        for layer, layer_mats in enumerate((first_mats, second_mats))
    ]
    kept = []
    for layer in range(layers):
        hidden, saved = layer_forward(hidden, weights[layer], pattern)
        kept.append(saved)
    output = from_sequence(hidden, parity, BF16)
    flow = to_sequence(d_out, parity).astype(F32)
    grads, vec_grads, up_grads = [None] * layers, [None] * layers, [None] * layers
    for layer in reversed(range(layers)):
        flow, grads[layer], vec_grads[layer], up_grads[layer] = layer_backward(
            flow, weights[layer], kept[layer], pattern
        )
    full = []
    for mat in grads[0]:
        mat = mat.astype(BF16).reshape(rows // 2, 2, mat.shape[0] // rows, cols, -1)
        full.append(mat.transpose(3, 0, 1, 2, 4))
    lined = []
    for mat in grads[1]:
        mat = lax.psum_scatter(mat.astype(BF16), "row", scatter_dimension=0, tiled=True)
        lined.append(mat.reshape(mat.shape[0], cols, -1).transpose(1, 0, 2))
    small = jnp.concatenate(
        [
            jnp.stack(vec_grads).reshape(layers * 8, cols, part).transpose(1, 0, 2),
            jnp.stack(up_grads).reshape(layers, cols, -1, part).transpose(1, 0, 2, 3).reshape(cols, -1, part),
        ],
        axis=1,
    )
    halves = flow.reshape(2, half, -1)
    summed = reduce_all(rows, cols, full, lined, small, pick(halves, 1 - parity).astype(BF16))
    own, other = pick(halves, parity), summed[9].astype(F32)
    first = parity == 0
    d_tokens = jnp.stack([jnp.where(first, own, other), jnp.where(first, other, own)])
    mats = [jnp.stack([summed[i], summed[4 + i]]) for i in range(4)]
    vec = summed[8][: layers * 8].reshape(layers, 8, part)
    ups = summed[8][layers * 8 :].reshape(layers, -1)
    return output, d_tokens, *mats, vec, ups


def solution(mesh):
    in_specs = (
        P(None, ("row", "col"), None),
        P(None, ("row", "col")),
        P(None, ("row", "col")),
        P(None, ("row", "col"), None),
        P(None, "row", "col"),
        P(None, "row", "col"),
        P(None, "row", "col"),
        P(None, "row", "col"),
        P(None, None, "col"),
        P(None, "col"),
        P(None, ("row", "col"), None),
    )
    out_specs = (
        P(None, ("row", "col"), None),
        P(None, ("row", "col"), None),
        P(None, "row", "col"),
        P(None, "row", "col"),
        P(None, "row", "col"),
        P(None, "row", "col"),
        P(None, None, "col"),
        P(None, "col"),
    )
    local = functools.partial(shards, mesh.shape["row"], mesh.shape["col"])
    return jax.shard_map(local, mesh=mesh, in_specs=in_specs, out_specs=out_specs, check_vma=False)
```

```python
import functools
import jax
import jax.numpy as jnp
from jax import lax
from jax.experimental import pallas as pl
from jax.experimental.pallas import tpu as pltpu
from jax.sharding import PartitionSpec as P

HEAD = 64
PAIR = 2 * HEAD
TILE = 128
VMEM_SPEC = pl.BlockSpec(memory_space=pltpu.VMEM)
UNROLL = 6
UNROLL_BACK = 6
WIDTHS = (3, 4, 5, 6, 8)
SCALE = HEAD ** (-0.5)
NT = (((1,), (1,)), ((), ()))
F32 = jnp.float32
BF16 = jnp.bfloat16


def stack_heads(rows):
    first = lax.broadcasted_iota(jnp.int32, rows.shape, 1) < HEAD
    zero = jnp.zeros_like(rows)
    return jnp.concatenate([jnp.where(first, rows, zero), jnp.where(first, zero, rows)], axis=0)


def unstack_heads(both):
    half = both.shape[1] // 2
    first = lax.broadcasted_iota(jnp.int32, (both.shape[0], half), 0) < HEAD
    return jnp.where(first, both[:, :half], both[:, half:])


def by_width(count, blocks, run):
    low = 0
    for width in WIDTHS:
        width = min(width, blocks)
        if width == low:
            continue
        pl.when((count > low) & (count <= width))(functools.partial(run, width))
        low = width


def attend_kernel(first_ref, count_ref, qkv_ref, bias_ref, mix_ref, lse_ref, vt_ref):
    length, width3 = qkv_ref.shape
    model = width3 // 3
    blocks = length // TILE
    pairs = model // PAIR
    vt_ref[...] = qkv_ref[:, 2 * model :].T

    def one_tile(tile, carry):
        rows = pl.ds(pl.multiple_of(tile * TILE, TILE), TILE)

        def run(width):
            begin = jnp.minimum(first_ref[tile], blocks - width)
            keys = pl.ds(pl.multiple_of(begin * TILE, TILE), width * TILE)

            def one_pair(pair):
                cols = pl.ds(pl.multiple_of(pair * PAIR, PAIR), PAIR)
                k_cols = pl.ds(pl.multiple_of(model + pair * PAIR, PAIR), PAIR)
                both_q = stack_heads(qkv_ref[rows, cols] * SCALE)
                bias = bias_ref[keys, rows]
                scores = lax.dot_general(
                    qkv_ref[keys, k_cols], both_q, NT, preferred_element_type=F32
                ) + jnp.concatenate([bias, bias], axis=1)
                peak = jnp.max(scores, axis=0, keepdims=True)
                exponent = jnp.exp(scores - peak)
                total = jnp.sum(exponent, axis=0, keepdims=True)
                mixed = jnp.dot(
                    vt_ref[cols, keys], exponent.astype(BF16), preferred_element_type=F32
                )
                mixed = unstack_heads(mixed / total)
                mix_ref[rows, cols] = mixed.T.astype(BF16)
                lse_ref[pair, pl.ds(tile, 1), :] = peak + jnp.log(total)

            def some_pairs(step, carry):
                for offset in range(UNROLL):
                    one_pair(step * UNROLL + offset)
                return carry

            lax.fori_loop(0, pairs // UNROLL, some_pairs, 0)

        by_width(count_ref[tile], blocks, run)
        return carry

    lax.fori_loop(0, blocks, one_tile, 0)


def attend_back_kernel(
    first_ref, count_ref, qkv_ref, grad_ref, bias_ref, lse_ref, out_ref, kt_ref, dk_ref, dv_ref
):
    length, width3 = qkv_ref.shape
    model = width3 // 3
    blocks = length // TILE
    pairs = model // PAIR
    kt_ref[...] = qkv_ref[:, model : 2 * model].T
    dk_ref[...] = jnp.zeros_like(dk_ref)
    dv_ref[...] = jnp.zeros_like(dv_ref)

    def one_tile(tile, carry):
        rows = pl.ds(pl.multiple_of(tile * TILE, TILE), TILE)

        def run(width):
            begin = jnp.minimum(first_ref[tile], blocks - width)
            keys = pl.ds(pl.multiple_of(begin * TILE, TILE), width * TILE)

            def one_pair(pair):
                cols, k_cols, v_cols = (
                    pl.ds(pl.multiple_of(part * model + pair * PAIR, PAIR), PAIR)
                    for part in range(3)
                )
                both_q = stack_heads(qkv_ref[rows, cols] * SCALE)
                both_g = stack_heads(grad_ref[rows, cols])
                lse = lse_ref[pair, pl.ds(tile, 1), :]
                bias = bias_ref[keys, rows]
                scores = lax.dot_general(
                    qkv_ref[keys, k_cols], both_q, NT, preferred_element_type=F32
                ) + jnp.concatenate([bias, bias], axis=1)
                prob = jnp.exp(scores - lse)
                grad_p = lax.dot_general(
                    qkv_ref[keys, v_cols], both_g, NT, preferred_element_type=F32
                )
                delta = jnp.sum(grad_p * prob, axis=0, keepdims=True)
                grad_s = (prob * (grad_p - delta)).astype(BF16)
                dv = jnp.dot(prob.astype(BF16), both_g, preferred_element_type=F32)
                dk = jnp.dot(grad_s, both_q, preferred_element_type=F32)
                grad_q = jnp.dot(kt_ref[cols, keys], grad_s, preferred_element_type=F32)
                return (cols, dv, dk, (unstack_heads(grad_q) * SCALE).T.astype(BF16))

            def some_pairs(step, carry):
                done = [one_pair(step * UNROLL_BACK + offset) for offset in range(UNROLL_BACK)]
                for cols, dv, dk, dq in done:
                    dv_ref[keys, cols] += dv
                    dk_ref[keys, cols] += dk
                    out_ref[rows, cols] = dq
                return carry

            lax.fori_loop(0, pairs // UNROLL_BACK, some_pairs, 0)

        by_width(count_ref[tile], blocks, run)
        return carry

    lax.fori_loop(0, blocks, one_tile, 0)
    out_ref[:, model : 2 * model] = dk_ref[...].astype(BF16)
    out_ref[:, 2 * model :] = dv_ref[...].astype(BF16)


SMEM_SPEC = pl.BlockSpec(memory_space=pltpu.SMEM)


def attend(first, count, qkv, bias):
    length, width3 = qkv.shape
    model = width3 // 3
    pairs, blocks = model // PAIR, length // TILE
    return pl.pallas_call(
        attend_kernel,
        out_shape=(
            jax.ShapeDtypeStruct((length, model), BF16),
            jax.ShapeDtypeStruct((pairs, blocks, 2 * TILE), F32),
        ),
        in_specs=[SMEM_SPEC, SMEM_SPEC, VMEM_SPEC, VMEM_SPEC],
        out_specs=(VMEM_SPEC, VMEM_SPEC),
        scratch_shapes=[pltpu.VMEM((model, length), BF16)],
        compiler_params=pltpu.CompilerParams(vmem_limit_bytes=40 << 20),
    )(first, count, qkv, bias)


def attend_back(first, count, qkv, grad_mix, bias, lse):
    length, width3 = qkv.shape
    model = width3 // 3
    return pl.pallas_call(
        attend_back_kernel,
        out_shape=jax.ShapeDtypeStruct((length, width3), BF16),
        in_specs=[SMEM_SPEC, SMEM_SPEC] + [VMEM_SPEC] * 4,
        out_specs=VMEM_SPEC,
        scratch_shapes=[
            pltpu.VMEM((model, length), BF16),
            pltpu.VMEM((length, model), F32),
            pltpu.VMEM((length, model), F32),
        ],
        compiler_params=pltpu.CompilerParams(vmem_limit_bytes=48 << 20),
    )(first, count, qkv, grad_mix, bias, lse)

NEG_FILL = -1e30
EPS = 1e-06
ROOT_HALF = 0.7071067811865476
INV_ROOT_TAU = 0.3989422804014327
BLOCK = 64


def norm_forward(residual, norm_gain, norm_shift):
    center = residual - jnp.mean(residual, axis=-1, keepdims=True)
    scale_inv = lax.rsqrt(jnp.mean(center * center, axis=-1, keepdims=True) + EPS)
    normed = center * scale_inv
    return (normed * norm_gain + norm_shift, normed, scale_inv)


def norm_backward(grad_y, normed, scale_inv, norm_gain):
    grad_n = grad_y * norm_gain
    return scale_inv * (
        grad_n
        - jnp.mean(grad_n, axis=-1, keepdims=True)
        - normed * jnp.mean(grad_n * normed, axis=-1, keepdims=True)
    )


def gelu_value(pre_act):
    return 0.5 * pre_act * (1.0 + lax.erf(pre_act * ROOT_HALF))


def gelu_slope(pre_act):
    return 0.5 * (1.0 + lax.erf(pre_act * ROOT_HALF)) + pre_act * INV_ROOT_TAU * jnp.exp(
        -0.5 * pre_act * pre_act
    )


def swapped(block):
    count = lax.axis_size("col")
    return lax.ppermute(block, "col", [(i, i ^ 1) for i in range(count)])


def pick(array, index):
    return lax.dynamic_index_in_dim(array, index, 0, keepdims=False)


def to_sequence(halves, parity):
    own = pick(halves, parity)
    other = swapped(pick(halves, 1 - parity))
    first = parity == 0
    return jnp.concatenate([jnp.where(first, own, other), jnp.where(first, other, own)])


def from_sequence(whole, parity, narrow):
    halves = whole.reshape((2, -1) + whole.shape[1:])
    own = pick(halves, parity)
    other = swapped(pick(halves, 1 - parity).astype(narrow)).astype(whole.dtype)
    first = parity == 0
    return jnp.stack([jnp.where(first, own, other), jnp.where(first, other, own)])


def key_pattern(seg, pad, rand):
    length = seg.shape[0]
    places = jnp.arange(length, dtype=jnp.int32)
    starts = jnp.sum((seg[None, :] < seg[:, None]).astype(jnp.int32), axis=1)
    ends = jnp.sum((seg[None, :] <= seg[:, None]).astype(jnp.int32), axis=1)
    whole = places - starts < 2 * BLOCK
    block = places // BLOCK
    chosen = jnp.repeat(rand, BLOCK, axis=0)
    near = jnp.abs(block[:, None] - block[None, :]) <= 1
    hit = jnp.zeros((length, length), bool)
    for slot in range(rand.shape[1]):
        hit = hit | (block[:, None] == chosen[None, :, slot])
    allowed = (
        (seg[:, None] == seg[None, :])
        & (pad[:, None] > 0)
        & (whole[:, None] | whole[None, :] | near | hit)
    )
    allowed = allowed | (places[:, None] == places[None, :])
    bias = jnp.where(allowed, 0.0, NEG_FILL).astype(F32)
    first = starts[::TILE] // TILE
    count = (ends[TILE - 1 :: TILE] + TILE - 1) // TILE - first
    return bias, first, count


def layer_forward(hidden, weights, pattern):
    mat_qkv, mat_out, mat_up, mat_down, vectors, up_bias = weights
    bias, first, count = pattern
    qkv_bias = jnp.concatenate([vectors[0], jnp.zeros_like(vectors[0]), vectors[1]])
    qkv = (jnp.dot(hidden, mat_qkv, preferred_element_type=F32) + qkv_bias).astype(BF16)
    mixture, lse = attend(first, count, qkv, bias)
    branch = jnp.dot(mixture, mat_out, preferred_element_type=F32) + vectors[2]
    first_norm, normed_one, inv_one = norm_forward(
        hidden.astype(F32) + branch, vectors[4], vectors[5]
    )
    first_out = first_norm.astype(BF16)
    pre_act = jnp.dot(first_out, mat_up, preferred_element_type=F32) + up_bias
    act_low = gelu_value(pre_act).astype(BF16)
    down_out = jnp.dot(act_low, mat_down, preferred_element_type=F32) + vectors[3]
    final_out, normed_two, inv_two = norm_forward(
        first_out.astype(F32) + down_out, vectors[6], vectors[7]
    )
    saved = (
        hidden, qkv, lse, mixture, normed_one, inv_one, first_out, pre_act, act_low, normed_two, inv_two,
    )
    return final_out.astype(BF16), saved


def layer_backward(grad_y, weights, saved, pattern):
    mat_qkv, mat_out, mat_up, mat_down, vectors, up_bias = weights
    (
        hidden, qkv, lse, mixture, normed_one, inv_one, first_out, pre_act, act_low, normed_two, inv_two,
    ) = saved
    bias, first, count = pattern
    width = hidden.shape[1]
    grad_gain_two = jnp.sum(grad_y * normed_two, axis=0)
    grad_shift_two = jnp.sum(grad_y, axis=0)
    grad_two = norm_backward(grad_y, normed_two, inv_two, vectors[6])
    grad_down_low = grad_two.astype(BF16)
    grad_bias_down = jnp.sum(grad_down_low.astype(F32), axis=0)
    grad_mat_down = jnp.einsum("tf,td->fd", act_low, grad_down_low, preferred_element_type=F32)
    grad_act = jnp.einsum("td,fd->tf", grad_down_low, mat_down, preferred_element_type=F32)
    grad_pre = (grad_act * gelu_slope(pre_act)).astype(BF16)
    grad_bias_hidden = jnp.sum(grad_pre.astype(F32), axis=0)
    grad_mat_up = jnp.einsum("td,tf->df", first_out, grad_pre, preferred_element_type=F32)
    grad_first = grad_two + jnp.einsum("tf,df->td", grad_pre, mat_up, preferred_element_type=F32)
    grad_gain_one = jnp.sum(grad_first * normed_one, axis=0)
    grad_shift_one = jnp.sum(grad_first, axis=0)
    grad_one = norm_backward(grad_first, normed_one, inv_one, vectors[4])
    grad_branch = grad_one.astype(BF16)
    grad_bias_out = jnp.sum(grad_branch.astype(F32), axis=0)
    grad_mat_out = jnp.einsum("td,te->de", mixture, grad_branch, preferred_element_type=F32)
    grad_mix = jnp.einsum("te,de->td", grad_branch, mat_out, preferred_element_type=F32)
    grad_qkv = attend_back(first, count, qkv, grad_mix.astype(BF16), bias, lse)
    grad_mat_qkv = jnp.einsum("td,te->de", hidden, grad_qkv, preferred_element_type=F32)
    grad_hidden = grad_one + jnp.einsum("te,de->td", grad_qkv, mat_qkv, preferred_element_type=F32)
    bias_qkv = jnp.sum(grad_qkv.astype(F32), axis=0)
    grad_rows = jnp.stack(
        [
            bias_qkv[:width], bias_qkv[2 * width :], grad_bias_out, grad_bias_down,
            grad_gain_one, grad_shift_one, grad_gain_two, grad_shift_two,
        ]
    )
    return grad_hidden, (grad_mat_qkv, grad_mat_out, grad_mat_up, grad_mat_down), grad_rows, grad_bias_hidden


ANY_SPEC = pl.BlockSpec(memory_space=pl.ANY)
DMA = pltpu.SemaphoreType.DMA


class Place:
    def __init__(self, rows, cols):
        self.rows, self.cols = rows, cols
        self.row, self.col = lax.axis_index("row"), lax.axis_index("col")
        self.core = self.row % 2
        self.bits = list(range(1, rows.bit_length() - 1))
        self.orders = (self.bits, self.bits[::-1])

    def flipped(self, row, bit):
        return row + (1 - 2 * ((row // 2**bit) % 2)) * 2**bit

    def partner(self, bit):
        return (self.flipped(self.row, bit), self.col)

    def others(self, bits):
        found = [self.row]
        for bit in bits:
            found += [self.flipped(row, bit) for row in found]
        return found

    def greet(self):
        barrier = pltpu.get_barrier_semaphore()

        def signal(row, col):
            pl.semaphore_signal(
                barrier, inc=1, device_id=(row, col), device_id_type=pl.DeviceIdType.MESH
            )

        for bit in [0, *self.bits]:
            signal(*self.partner(bit))
        pl.when(self.col > 0)(lambda: signal(self.row, self.col - 1))
        pl.when(self.col < self.cols - 1)(lambda: signal(self.row, self.col + 1))
        inside = jnp.where((self.col > 0) & (self.col < self.cols - 1), 1, 0)
        pl.semaphore_wait(barrier, len(self.bits) + 2 + inside)


def remote(src, dst, send, recv, target):
    return pltpu.make_async_remote_copy(
        src_ref=src,
        dst_ref=dst,
        send_sem=send,
        recv_sem=recv,
        device_id=target,
        device_id_type=pl.DeviceIdType.MESH,
    )


def run_stages(items):
    plan = []
    for order, (time, stages) in enumerate(items):
        for index, stage in enumerate(stages):
            plan.append((time + index, order, stage))
    for _, _, stage in sorted(plan, key=lambda step: step[:2]):
        stage()


class LineGather:
    def __init__(self, place, own, slot, sems):
        self.place, self.own, self.slot, self.sems = place, own, slot, sems

    def copies(self, hop, receiving):
        place = self.place
        col, cols = place.col, place.cols
        for way, step in ((0, 1), (1, -1)):
            target = col + step
            if receiving:
                slot = col - step * (hop + 1)
                valid = (slot >= 0) & (slot < cols)
            else:
                slot = col - step * hop
                valid = (slot >= 0) & (slot < cols) & (target >= 0) & (target < cols)
            src = self.own if hop == 0 and not receiving else self.slot(slot)
            yield valid, lambda src=src, slot=slot, way=way, target=target: remote(
                src,
                self.slot(slot),
                self.sems.at[0, way, hop],
                self.sems.at[1, way, hop],
                (place.row, target),
            )

    def start(self, hop):
        for valid, copy in self.copies(hop, False):
            pl.when(valid)(lambda copy=copy: copy().start())

    def wait_recv(self, hop):
        for valid, copy in self.copies(hop, True):
            pl.when(valid)(lambda copy=copy: copy().wait_recv())

    def wait_send(self, hop):
        for valid, copy in self.copies(hop, False):
            pl.when(valid)(lambda copy=copy: copy().wait_send())


def cut(begin, size):
    first = size // 32 * 16
    return ((begin, first), (begin + first, size - first))


def place_side_by_side(slots, rows, out):
    width = slots.shape[2]
    for col in range(slots.shape[0]):
        out[rows, col * width : (col + 1) * width] = slots[col, rows, :]


def take_apart(whole, rows, slots):
    width = slots.shape[2]
    for col in range(slots.shape[0]):
        slots[col, rows, :] = whole[rows, col * width : (col + 1) * width]


def gather_item(place, own, slots, wide, whole, piece, local_sems, line_sems, chip_sems, core_sems):
    hops = place.cols - 1
    rows = pl.ds(*piece)
    line = LineGather(place, own.at[rows], lambda col: slots.at[col, rows], line_sems)
    mine = lambda: pltpu.make_async_copy(own.at[rows], slots.at[place.col, rows], local_sems.at[0])
    home = lambda: pltpu.make_async_copy(
        wide.at[rows], whole.at[place.row // 2, place.core, rows], local_sems.at[1]
    )

    def chip_copies(phase, receiving):
        for part, span in enumerate(cut(*piece)):
            order = place.orders[part]
            bit = order[phase]
            for index, row in enumerate(place.others(order[:phase])):
                if receiving:
                    row = place.flipped(row, bit)
                ref = whole.at[row // 2, row % 2, pl.ds(*span)]
                yield remote(
                    wide.at[pl.ds(*span)] if index == 0 else ref,
                    ref,
                    chip_sems.at[0, phase, part, index],
                    chip_sems.at[1, phase, part, index],
                    place.partner(bit),
                )

    def core_copy(receiving):
        ref = whole.at[:, 1 - place.core if receiving else place.core, rows]
        return remote(ref, ref, core_sems.at[0], core_sems.at[1], place.partner(0))

    phases = len(place.bits)

    def first():
        mine().start()
        line.start(0)

    def hop_stage(hop):
        line.wait_recv(hop - 1)
        line.start(hop)

    def chip_stage(phase):
        if phase == 0:
            line.wait_recv(hops - 1)
            mine().wait()
            place_side_by_side(slots, rows, wide)
        else:
            for copy in chip_copies(phase - 1, True):
                copy.wait_recv()
        for copy in chip_copies(phase, False):
            copy.start()
        if phase == 0:
            home().start()

    def core_stage():
        for copy in chip_copies(phases - 1, True):
            copy.wait_recv()
        home().wait()
        core_copy(False).start()

    def last():
        core_copy(True).wait_recv()
        core_copy(False).wait_send()
        for hop in range(hops):
            line.wait_send(hop)
        for phase in range(phases):
            for copy in chip_copies(phase, False):
                copy.wait_send()

    return (
        [first]
        + [functools.partial(hop_stage, hop) for hop in range(1, hops)]
        + [functools.partial(chip_stage, phase) for phase in range(phases)]
        + [core_stage, last]
    )


def gather_line_item(place, own, slots, wide, local_sem, line_sems):
    hops = place.cols - 1
    line = LineGather(place, own, lambda col: slots.at[col], line_sems)
    mine = lambda: pltpu.make_async_copy(own, slots.at[place.col], local_sem)

    def first():
        mine().start()
        line.start(0)

    def hop_stage(hop):
        line.wait_recv(hop - 1)
        line.start(hop)

    def last():
        line.wait_recv(hops - 1)
        mine().wait()
        if wide is not None:
            place_side_by_side(slots, slice(None), wide)
        for hop in range(hops):
            line.wait_send(hop)

    return [first] + [functools.partial(hop_stage, hop) for hop in range(1, hops)] + [last]


def exchange_item(place, halves, whole, sems, delay):
    parity = place.col % 2
    copy = lambda: remote(
        halves.at[1 - parity],
        whole.at[parity],
        sems.at[0],
        sems.at[1],
        (place.row, place.col + 1 - 2 * parity),
    )
    arriving = lambda: remote(
        halves.at[1 - parity],
        whole.at[1 - parity],
        sems.at[0],
        sems.at[1],
        (place.row, place.col + 1 - 2 * parity),
    )
    mine = lambda: pltpu.make_async_copy(halves.at[parity], whole.at[parity], sems.at[2])

    def first():
        copy().start()
        mine().start()

    def last():
        arriving().wait_recv()
        copy().wait_send()
        mine().wait()

    return [first] + [lambda: None] * delay + [last]


def row_pieces(rs):
    return [(0, rs // 2), (rs // 2, rs // 2)] if rs % 32 == 0 and rs > 32 else [(0, rs)]


def gather_kernel(rows, cols, *refs):
    (full, lined), (small, tokens, marks) = (refs[:4], refs[4:8]), refs[8:11]
    (full_out, lined_out), (small_out, hidden, marks_out) = (refs[11:15], refs[15:19]), refs[19:22]
    slots, wide, lined_slots = refs[22:26], refs[26:30], refs[30:34]
    local_sems, line_sems, chip_sems, core_sems, exchange_sems = refs[34:]
    place = Place(rows, cols)
    place.greet()
    items = [
        (0, exchange_item(place, marks, marks_out, exchange_sems.at[1], 16)),
        (0, gather_line_item(place, small, small_out, None, local_sems.at[0, 0], line_sems.at[0])),
    ]
    number = 0
    for index in range(4):
        for piece in row_pieces(full[index].shape[0]):
            stages = gather_item(
                place,
                full[index],
                slots[index],
                wide[index],
                full_out[index],
                piece,
                local_sems.at[number + 1],
                line_sems.at[number + 1],
                chip_sems.at[number],
                core_sems.at[number],
            )
            items.append((number, stages))
            number += 1
    items.append((number, exchange_item(place, tokens, hidden, exchange_sems.at[0], 16)))
    for index in range(4):
        at = number + index
        stages = gather_line_item(
            place,
            lined[index],
            lined_slots[index],
            lined_out[index],
            local_sems.at[at + 1, 0],
            line_sems.at[at + 1],
        )
        items.append((at, stages))
    run_stages(items)


def gather_all(rows, cols, full, lined, small, tokens, marks):
    number = sum(len(row_pieces(x.shape[0])) for x in full)
    phases = rows.bit_length() - 2
    like = lambda x, lead=(): jax.ShapeDtypeStruct(lead + x.shape, x.dtype)
    wide = [(x.shape[0], cols * x.shape[1]) for x in full]
    outs = [jax.ShapeDtypeStruct((rows // 2, 2) + shape, BF16) for shape in wide]
    outs += [jax.ShapeDtypeStruct(shape, BF16) for shape in wide]
    outs += [like(small, (cols,)), like(tokens), like(marks)]
    return pl.pallas_call(
        functools.partial(gather_kernel, rows, cols),
        out_shape=tuple(outs),
        in_specs=[ANY_SPEC] * 11,
        out_specs=(ANY_SPEC,) * 4 + (VMEM_SPEC,) * 4 + (ANY_SPEC,) * 3,
        scratch_shapes=[pltpu.VMEM((cols,) + x.shape, BF16) for x in full]
        + [pltpu.VMEM(shape, BF16) for shape in wide]
        + [pltpu.VMEM((cols,) + x.shape, BF16) for x in lined]
        + [
            DMA((number + len(lined) + 1, 2)),
            DMA((number + len(lined) + 1, 2, 2, cols - 1)),
            DMA((number, 2, phases, 2, 2 ** (phases - 1))),
            DMA((number, 2)),
            DMA((2, 3)),
        ],
        compiler_params=pltpu.CompilerParams(
            collective_id=0, has_side_effects=True, vmem_limit_bytes=50 << 20
        ),
    )(*full, *lined, small, tokens, marks)


class LineReduce:
    def __init__(self, place, slot, arrived, sems):
        self.place, self.slot, self.arrived, self.sems = place, slot, arrived, sems

    def copies(self, hop, receiving):
        place = self.place
        last = place.cols - 1
        for way, step in ((0, 1), (1, -1)):
            here = place.col if way == 0 else last - place.col
            from_start = here if not receiving else here - 1
            slot = last - hop + from_start
            valid = (from_start <= hop) & (from_start >= 0) & (from_start < last)
            slot = slot if way == 0 else last - slot
            yield valid, slot, way, lambda way=way, slot=slot, step=step: remote(
                self.slot(slot),
                self.arrived.at[way, hop],
                self.sems.at[0, way, hop],
                self.sems.at[1, way, hop],
                (place.row, place.col + step),
            )

    def start(self, hop):
        for valid, _, _, copy in self.copies(hop, False):
            pl.when(valid)(lambda copy=copy: copy().start())

    def wait_send(self, hop):
        for valid, _, _, copy in self.copies(hop, False):
            pl.when(valid)(lambda copy=copy: copy().wait_send())

    def take(self, hop):
        for valid, slot, way, copy in self.copies(hop, True):

            def add(slot=slot, way=way, copy=copy):
                pltpu.make_async_copy(
                    self.arrived.at[way, hop], self.arrived.at[way, hop], self.sems.at[1, way, hop]
                ).wait()
                ref = self.slot(slot)
                ref[...] = ref[...] + self.arrived.at[way, hop][...]

            pl.when(valid)(add)

    def finish(self, out):
        hop = self.place.cols - 2
        own = self.slot(self.place.col)
        out[...] = own[...].astype(F32)
        for valid, _, way, copy in self.copies(hop, True):

            def add(way=way):
                pltpu.make_async_copy(
                    self.arrived.at[way, hop], self.arrived.at[way, hop], self.sems.at[1, way, hop]
                ).wait()
                out[...] = out[...] + self.arrived.at[way, hop][...].astype(F32)

            pl.when(valid)(add)
        for hop in range(self.place.cols - 1):
            self.wait_send(hop)


def line_stages(line, out, before):
    hops = line.place.cols - 1

    def first():
        before()
        line.start(0)

    def hop_stage(hop):
        line.take(hop - 1)
        line.start(hop)

    return (
        [first]
        + [functools.partial(hop_stage, hop) for hop in range(1, hops)]
        + [lambda: line.finish(out)]
    )


def reduce_item(place, partial, out, sums, from_core, from_chips, slots, from_line, piece, sems):
    local_sem, core_sems, chip_sems, line_sems = sems
    phases = len(place.bits)
    rows = pl.ds(*piece)
    core_copy = lambda: remote(
        partial.at[:, 1 - place.core, rows],
        from_core.at[:, rows],
        core_sems.at[0],
        core_sems.at[1],
        place.partner(0),
    )
    load = lambda: pltpu.make_async_copy(
        partial.at[:, place.core, rows], sums.at[:, rows], local_sem
    )
    line = LineReduce(
        place, lambda col: slots.at[col, rows], from_line.at[:, :, rows], line_sems
    )

    def chip_parts(phase):
        for part, span in enumerate(cut(*piece)):
            order = place.orders[part][::-1]
            yield part, pl.ds(*span), order[phase], order[phase + 1 :]

    def chip_copies(phase):
        for part, span, bit, rest in chip_parts(phase):
            for index, row in enumerate(place.others(rest)):
                row = place.flipped(row, bit)
                yield remote(
                    sums.at[row // 2, span],
                    from_chips[phase].at[index, span],
                    chip_sems.at[0, phase, part, index],
                    chip_sems.at[1, phase, part, index],
                    place.partner(bit),
                )

    def chip_take(phase):
        for part, span, _, rest in chip_parts(phase):
            for index, row in enumerate(place.others(rest)):
                arrived = from_chips[phase].at[index, span]
                pltpu.make_async_copy(arrived, arrived, chip_sems.at[1, phase, part, index]).wait()
                ref = sums.at[row // 2, span]
                ref[...] = ref[...] + arrived[...]

    def first():
        core_copy().start()
        load().start()

    def chip_stage(phase):
        if phase == 0:
            load().wait()
            core_copy().wait_recv()

            def add(pair, carry):
                ref = sums.at[pair, rows]
                ref[...] = ref[...] + from_core.at[pair, rows][...]
                return carry

            lax.fori_loop(0, place.rows // 2, add, 0)
        else:
            chip_take(phase - 1)
        for copy in chip_copies(phase):
            copy.start()

    def to_slots():
        chip_take(phases - 1)
        take_apart(sums.at[place.row // 2], rows, slots)

    def last():
        core_copy().wait_send()
        for phase in range(phases):
            for copy in chip_copies(phase):
                copy.wait_send()

    return (
        [first]
        + [functools.partial(chip_stage, phase) for phase in range(phases)]
        + line_stages(line, out.at[rows], to_slots)
        + [last]
    )


def reduce_line_item(place, partial, out, slots, from_line, line_sems):
    line = LineReduce(place, lambda col: slots.at[col], from_line, line_sems)
    return line_stages(line, out, lambda: take_apart(partial, slice(None), slots))


def reduce_small_item(place, partial, out, sums, arrived, from_line, sems, line_sems):
    bits = [0, *place.bits]
    line = LineReduce(place, lambda col: sums.at[col], from_line, line_sems)
    copy = lambda index: remote(
        sums, arrived.at[index], sems.at[0, index], sems.at[1, index], place.partner(bits[index])
    )

    def take(index):
        copy(index).wait()
        sums[...] = sums[...] + arrived[index]

    def stage(index):
        if index == 0:
            sums[...] = partial[...]
        else:
            take(index - 1)
        copy(index).start()

    return [functools.partial(stage, index) for index in range(len(bits))] + line_stages(
        line, out, lambda: take(len(bits) - 1)
    )


def reduce_kernel(rows, cols, full, lined, *refs):
    phases = rows.bit_length() - 2
    refs = list(refs)

    def take(number):
        taken = refs[:number]
        del refs[:number]
        return taken

    full_in, line_in, (small_in, tokens) = take(full), take(lined), take(2)
    full_out, line_out, (small_out, tokens_out) = take(full), take(lined), take(2)
    place = Place(rows, cols)
    place.greet()
    items = []
    small_sums, small_arrived, small_line, small_sems, small_line_sems = take(5)
    [token_sems] = take(1)
    parity = place.col % 2
    token_copy = lambda: remote(
        tokens, tokens_out, token_sems.at[0], token_sems.at[1], (place.row, place.col + 1 - 2 * parity)
    )
    time = 0
    for index in range(full):
        sums, from_core, slots, from_line = take(4)
        from_chips = take(phases)
        local_sems, core_sems, chip_sems, line_sems = take(4)
        for number, piece in enumerate(row_pieces(full_in[index].shape[2])):
            stages = reduce_item(
                place,
                full_in[index],
                full_out[index],
                sums,
                from_core,
                from_chips,
                slots,
                from_line,
                piece,
                (local_sems.at[number], core_sems.at[number], chip_sems.at[number], line_sems.at[number]),
            )
            items.append((time, stages))
            time += 1
    for index in range(lined):
        slots, from_line, line_sems = take(3)
        items.append(
            (index, reduce_line_item(place, line_in[index], line_out[index], slots, from_line, line_sems))
        )
    items.append(
        (1, reduce_small_item(place, small_in, small_out, small_sums, small_arrived, small_line, small_sems, small_line_sems))
    )
    items.append(
        (0, [lambda: token_copy().start()] + [lambda: None] * 12 + [lambda: token_copy().wait()])
    )
    run_stages(items)


def reduce_all(rows, cols, full, lined, small, tokens):
    phases = rows.bit_length() - 2
    hops = cols - 1
    shard = lambda x: (x.shape[-2], x.shape[-1] // cols)
    outs = [jax.ShapeDtypeStruct(shard(x), F32) for x in (*full, *lined)]
    outs.append(jax.ShapeDtypeStruct(small.shape[1:], F32))
    outs.append(jax.ShapeDtypeStruct(tokens.shape, tokens.dtype))
    scratch = [
        pltpu.VMEM(small.shape, F32),
        pltpu.VMEM((phases + 1,) + small.shape, F32),
        pltpu.VMEM((2, hops) + small.shape[1:], F32),
        DMA((2, phases + 1)),
        DMA((2, 2, hops)),
        DMA((2,)),
    ]
    for x in full:
        count = len(row_pieces(x.shape[2]))
        scratch += [
            pltpu.VMEM((rows // 2,) + x.shape[2:], BF16),
            pltpu.VMEM((rows // 2,) + x.shape[2:], BF16),
            pltpu.VMEM((cols,) + shard(x), BF16),
            pltpu.VMEM((2, hops) + shard(x), BF16),
        ]
        scratch += [
            pltpu.VMEM((2 ** (phases - 1 - phase),) + x.shape[2:], BF16) for phase in range(phases)
        ]
        scratch += [
            DMA((count,)),
            DMA((count, 2)),
            DMA((count, 2, phases, 2, 2 ** (phases - 1))),
            DMA((count, 2, 2, hops)),
        ]
    for x in lined:
        scratch += [
            pltpu.VMEM((cols,) + shard(x), BF16),
            pltpu.VMEM((2, hops) + shard(x), BF16),
            DMA((2, 2, hops)),
        ]
    return pl.pallas_call(
        functools.partial(reduce_kernel, rows, cols, len(full), len(lined)),
        out_shape=tuple(outs),
        in_specs=[ANY_SPEC] * len(full) + [VMEM_SPEC] * (len(lined) + 1) + [ANY_SPEC],
        out_specs=(VMEM_SPEC,) * (len(full) + len(lined) + 1) + (ANY_SPEC,),
        scratch_shapes=scratch,
        compiler_params=pltpu.CompilerParams(
            collective_id=1, has_side_effects=True, vmem_limit_bytes=60 << 20
        ),
    )(*full, *lined, small, tokens)


def shards(
    rows, cols, tokens, seg_ids, pad_mask, rand_blocks, w_qkv, w_out, w_up, w_down, layer_vectors, bias_up, d_out
):
    layers = w_qkv.shape[0]
    parity = lax.axis_index("col") % 2
    half = seg_ids.shape[1]
    chosen = rand_blocks.reshape(2, 1, -1)
    chosen = jnp.pad(chosen, ((0, 0), (0, 0), (0, 128 - chosen.shape[2])))
    marks = jnp.concatenate(
        [seg_ids.reshape(2, -1, 128), pad_mask.reshape(2, -1, 128), chosen], axis=1
    )
    marks = jnp.pad(marks, ((0, 0), (0, -marks.shape[1] % 8), (0, 0)))
    part = layer_vectors.shape[2]
    small = jnp.concatenate([layer_vectors.reshape(-1, part), bias_up.reshape(-1, part)])
    small_rows = small.shape[0]
    small = jnp.pad(small, ((0, -small_rows % 16), (0, 0)))
    mats = (w_qkv, w_out, w_up, w_down)
    got = gather_all(
        rows, cols, [w[0] for w in mats], [w[1] for w in mats], small, tokens, marks
    )
    vectors = got[8][:, : layers * 8].transpose(1, 0, 2).reshape(layers, 8, -1).astype(F32)
    up_biases = got[8][:, layers * 8 : small_rows].reshape(cols, layers, -1).transpose(1, 0, 2)
    up_biases = up_biases.reshape(layers, -1).astype(F32)
    hidden = got[9].reshape(2 * half, -1)
    marks = got[10]
    lines = half // 128
    seg, pad = marks[:, :lines].reshape(-1), marks[:, lines : 2 * lines].reshape(-1)
    rand = marks[:, 2 * lines, : half // BLOCK * rand_blocks.shape[2]]
    pattern = key_pattern(seg, pad, rand.reshape(-1, rand_blocks.shape[2]))

    first_mats = [g.reshape(-1, g.shape[3]) for g in got[:4]]
    second_mats = [lax.all_gather(g, "row", axis=0, tiled=True) for g in got[4:8]]
    weights = [
        (*layer_mats, vectors[layer], up_biases[layer])
        for layer, layer_mats in enumerate((first_mats, second_mats))
    ]
    kept = []
    for layer in range(layers):
        hidden, saved = layer_forward(hidden, weights[layer], pattern)
        kept.append(saved)
    output = from_sequence(hidden, parity, BF16)
    flow = to_sequence(d_out, parity).astype(F32)
    grads, vec_grads, up_grads = [None] * layers, [None] * layers, [None] * layers
    for layer in reversed(range(layers)):
        flow, grads[layer], vec_grads[layer], up_grads[layer] = layer_backward(
            flow, weights[layer], kept[layer], pattern
        )
    full = [
        mat.astype(BF16).reshape(rows // 2, 2, -1, mat.shape[1]) for mat in grads[0]
    ]
    lined = [
        lax.psum_scatter(mat.astype(BF16), "row", scatter_dimension=0, tiled=True)
        for mat in grads[1]
    ]
    small = jnp.concatenate(
        [
            jnp.stack(vec_grads).reshape(layers * 8, cols, part).transpose(1, 0, 2),
            jnp.stack(up_grads).reshape(layers, cols, -1, part).transpose(1, 0, 2, 3).reshape(cols, -1, part),
        ],
        axis=1,
    )
    halves = flow.reshape(2, half, -1)
    summed = reduce_all(rows, cols, full, lined, small, pick(halves, 1 - parity).astype(BF16))
    own, other = pick(halves, parity), summed[9].astype(F32)
    first = parity == 0
    d_tokens = jnp.stack([jnp.where(first, own, other), jnp.where(first, other, own)])
    mats = [jnp.stack([summed[i], summed[4 + i]]) for i in range(4)]
    vec = summed[8][: layers * 8].reshape(layers, 8, part)
    ups = summed[8][layers * 8 :].reshape(layers, -1)
    return output, d_tokens, *mats, vec, ups


def solution(mesh):
    in_specs = (
        P(None, ("row", "col"), None),
        P(None, ("row", "col")),
        P(None, ("row", "col")),
        P(None, ("row", "col"), None),
        P(None, "row", "col"),
        P(None, "row", "col"),
        P(None, "row", "col"),
        P(None, "row", "col"),
        P(None, None, "col"),
        P(None, "col"),
        P(None, ("row", "col"), None),
    )
    out_specs = (
        P(None, ("row", "col"), None),
        P(None, ("row", "col"), None),
        P(None, "row", "col"),
        P(None, "row", "col"),
        P(None, "row", "col"),
        P(None, "row", "col"),
        P(None, None, "col"),
        P(None, "col"),
    )
    local = functools.partial(shards, mesh.shape["row"], mesh.shape["col"])
    return jax.shard_map(local, mesh=mesh, in_specs=in_specs, out_specs=out_specs, check_vma=False)
```

```python
import functools
import jax
import jax.numpy as jnp
from jax import lax
from jax.experimental import pallas as pl
from jax.experimental.pallas import tpu as pltpu
from jax.sharding import PartitionSpec as P

HEAD = 64
PAIR = 2 * HEAD
TILE = 128
VMEM_SPEC = pl.BlockSpec(memory_space=pltpu.VMEM)
UNROLL = 6
UNROLL_BACK = 6
WIDTHS = (3, 4, 5, 6, 8)
SCALE = HEAD ** (-0.5)
NT = (((1,), (1,)), ((), ()))
F32 = jnp.float32
BF16 = jnp.bfloat16


def stack_heads(rows):
    first = lax.broadcasted_iota(jnp.int32, rows.shape, 1) < HEAD
    zero = jnp.zeros_like(rows)
    return jnp.concatenate([jnp.where(first, rows, zero), jnp.where(first, zero, rows)], axis=0)


def unstack_heads(both):
    half = both.shape[1] // 2
    first = lax.broadcasted_iota(jnp.int32, (both.shape[0], half), 0) < HEAD
    return jnp.where(first, both[:, :half], both[:, half:])


def by_width(count, blocks, run):
    low = 0
    for width in WIDTHS:
        width = min(width, blocks)
        if width == low:
            continue
        pl.when((count > low) & (count <= width))(functools.partial(run, width))
        low = width


def attend_kernel(first_ref, count_ref, qkv_ref, bias_ref, mix_ref, lse_ref, vt_ref):
    length, width3 = qkv_ref.shape
    model = width3 // 3
    blocks = length // TILE
    pairs = model // PAIR
    vt_ref[...] = qkv_ref[:, 2 * model :].T

    def one_tile(tile, carry):
        rows = pl.ds(pl.multiple_of(tile * TILE, TILE), TILE)

        def run(width):
            begin = jnp.minimum(first_ref[tile], blocks - width)
            keys = pl.ds(pl.multiple_of(begin * TILE, TILE), width * TILE)

            def one_pair(pair):
                cols = pl.ds(pl.multiple_of(pair * PAIR, PAIR), PAIR)
                k_cols = pl.ds(pl.multiple_of(model + pair * PAIR, PAIR), PAIR)
                both_q = stack_heads(qkv_ref[rows, cols] * SCALE)
                bias = bias_ref[keys, rows]
                scores = lax.dot_general(
                    qkv_ref[keys, k_cols], both_q, NT, preferred_element_type=F32
                ) + jnp.concatenate([bias, bias], axis=1)
                peak = jnp.max(scores, axis=0, keepdims=True)
                exponent = jnp.exp(scores - peak)
                total = jnp.sum(exponent, axis=0, keepdims=True)
                mixed = jnp.dot(
                    vt_ref[cols, keys], exponent.astype(BF16), preferred_element_type=F32
                )
                mixed = unstack_heads(mixed / total)
                mix_ref[rows, cols] = mixed.T.astype(BF16)
                lse_ref[pair, pl.ds(tile, 1), :] = peak + jnp.log(total)

            def some_pairs(step, carry):
                for offset in range(UNROLL):
                    one_pair(step * UNROLL + offset)
                return carry

            lax.fori_loop(0, pairs // UNROLL, some_pairs, 0)

        by_width(count_ref[tile], blocks, run)
        return carry

    lax.fori_loop(0, blocks, one_tile, 0)


def attend_back_kernel(
    first_ref, count_ref, qkv_ref, grad_ref, bias_ref, lse_ref, out_ref, kt_ref, dk_ref, dv_ref
):
    length, width3 = qkv_ref.shape
    model = width3 // 3
    blocks = length // TILE
    pairs = model // PAIR
    kt_ref[...] = qkv_ref[:, model : 2 * model].T
    dk_ref[...] = jnp.zeros_like(dk_ref)
    dv_ref[...] = jnp.zeros_like(dv_ref)

    def one_tile(tile, carry):
        rows = pl.ds(pl.multiple_of(tile * TILE, TILE), TILE)

        def run(width):
            begin = jnp.minimum(first_ref[tile], blocks - width)
            keys = pl.ds(pl.multiple_of(begin * TILE, TILE), width * TILE)

            def one_pair(pair):
                cols, k_cols, v_cols = (
                    pl.ds(pl.multiple_of(part * model + pair * PAIR, PAIR), PAIR)
                    for part in range(3)
                )
                both_q = stack_heads(qkv_ref[rows, cols] * SCALE)
                both_g = stack_heads(grad_ref[rows, cols])
                lse = lse_ref[pair, pl.ds(tile, 1), :]
                bias = bias_ref[keys, rows]
                scores = lax.dot_general(
                    qkv_ref[keys, k_cols], both_q, NT, preferred_element_type=F32
                ) + jnp.concatenate([bias, bias], axis=1)
                prob = jnp.exp(scores - lse)
                grad_p = lax.dot_general(
                    qkv_ref[keys, v_cols], both_g, NT, preferred_element_type=F32
                )
                delta = jnp.sum(grad_p * prob, axis=0, keepdims=True)
                grad_s = (prob * (grad_p - delta)).astype(BF16)
                dv = jnp.dot(prob.astype(BF16), both_g, preferred_element_type=F32)
                dk = jnp.dot(grad_s, both_q, preferred_element_type=F32)
                grad_q = jnp.dot(kt_ref[cols, keys], grad_s, preferred_element_type=F32)
                return (cols, dv, dk, (unstack_heads(grad_q) * SCALE).T.astype(BF16))

            def some_pairs(step, carry):
                done = [one_pair(step * UNROLL_BACK + offset) for offset in range(UNROLL_BACK)]
                for cols, dv, dk, dq in done:
                    dv_ref[keys, cols] += dv
                    dk_ref[keys, cols] += dk
                    out_ref[rows, cols] = dq
                return carry

            lax.fori_loop(0, pairs // UNROLL_BACK, some_pairs, 0)

        by_width(count_ref[tile], blocks, run)
        return carry

    lax.fori_loop(0, blocks, one_tile, 0)
    out_ref[:, model : 2 * model] = dk_ref[...].astype(BF16)
    out_ref[:, 2 * model :] = dv_ref[...].astype(BF16)


SMEM_SPEC = pl.BlockSpec(memory_space=pltpu.SMEM)


def attend(first, count, qkv, bias):
    length, width3 = qkv.shape
    model = width3 // 3
    pairs, blocks = model // PAIR, length // TILE
    return pl.pallas_call(
        attend_kernel,
        out_shape=(
            jax.ShapeDtypeStruct((length, model), BF16),
            jax.ShapeDtypeStruct((pairs, blocks, 2 * TILE), F32),
        ),
        in_specs=[SMEM_SPEC, SMEM_SPEC, VMEM_SPEC, VMEM_SPEC],
        out_specs=(VMEM_SPEC, VMEM_SPEC),
        scratch_shapes=[pltpu.VMEM((model, length), BF16)],
        compiler_params=pltpu.CompilerParams(vmem_limit_bytes=40 << 20),
    )(first, count, qkv, bias)


def attend_back(first, count, qkv, grad_mix, bias, lse):
    length, width3 = qkv.shape
    model = width3 // 3
    return pl.pallas_call(
        attend_back_kernel,
        out_shape=jax.ShapeDtypeStruct((length, width3), BF16),
        in_specs=[SMEM_SPEC, SMEM_SPEC] + [VMEM_SPEC] * 4,
        out_specs=VMEM_SPEC,
        scratch_shapes=[
            pltpu.VMEM((model, length), BF16),
            pltpu.VMEM((length, model), F32),
            pltpu.VMEM((length, model), F32),
        ],
        compiler_params=pltpu.CompilerParams(vmem_limit_bytes=48 << 20),
    )(first, count, qkv, grad_mix, bias, lse)

NEG_FILL = -1e30
EPS = 1e-06
ROOT_HALF = 0.7071067811865476
INV_ROOT_TAU = 0.3989422804014327
BLOCK = 64


def norm_forward(residual, norm_gain, norm_shift):
    center = residual - jnp.mean(residual, axis=-1, keepdims=True)
    scale_inv = lax.rsqrt(jnp.mean(center * center, axis=-1, keepdims=True) + EPS)
    normed = center * scale_inv
    return (normed * norm_gain + norm_shift, normed, scale_inv)


def norm_backward(grad_y, normed, scale_inv, norm_gain):
    grad_n = grad_y * norm_gain
    return scale_inv * (
        grad_n
        - jnp.mean(grad_n, axis=-1, keepdims=True)
        - normed * jnp.mean(grad_n * normed, axis=-1, keepdims=True)
    )


def gelu_both(pre_act):
    below = 0.5 * (1.0 + lax.erf(pre_act * ROOT_HALF))
    density = INV_ROOT_TAU * jnp.exp(-0.5 * pre_act * pre_act)
    return pre_act * below, below + pre_act * density


def swapped(block):
    count = lax.axis_size("col")
    return lax.ppermute(block, "col", [(i, i ^ 1) for i in range(count)])


def pick(array, index):
    return lax.dynamic_index_in_dim(array, index, 0, keepdims=False)


def to_sequence(halves, parity):
    own = pick(halves, parity)
    other = swapped(pick(halves, 1 - parity))
    first = parity == 0
    return jnp.concatenate([jnp.where(first, own, other), jnp.where(first, other, own)])


def from_sequence(whole, parity, narrow):
    halves = whole.reshape((2, -1) + whole.shape[1:])
    own = pick(halves, parity)
    other = swapped(pick(halves, 1 - parity).astype(narrow)).astype(whole.dtype)
    mine = jnp.arange(2)[:, None, None] == parity
    return jnp.where(mine, own[None], other[None])


def key_pattern(seg, pad, rand):
    length = seg.shape[0]
    places = jnp.arange(length, dtype=jnp.int32)
    starts = jnp.sum((seg[None, :] < seg[:, None]).astype(jnp.int32), axis=1)
    ends = jnp.sum((seg[None, :] <= seg[:, None]).astype(jnp.int32), axis=1)
    whole = places - starts < 2 * BLOCK
    block = places // BLOCK
    chosen = jnp.repeat(rand, BLOCK, axis=0)
    near = jnp.abs(block[:, None] - block[None, :]) <= 1
    hit = jnp.zeros((length, length), bool)
    for slot in range(rand.shape[1]):
        hit = hit | (block[:, None] == chosen[None, :, slot])
    allowed = (
        (seg[:, None] == seg[None, :])
        & (pad[:, None] > 0)
        & (whole[:, None] | whole[None, :] | near | hit)
    )
    allowed = allowed | (places[:, None] == places[None, :])
    bias = jnp.where(allowed, 0.0, NEG_FILL).astype(F32)
    first = starts[::TILE] // TILE
    count = (ends[TILE - 1 :: TILE] + TILE - 1) // TILE - first
    return bias, first, count


def layer_forward(hidden, weights, pattern):
    mat_qkv, mat_out, mat_up, mat_down, vectors, up_bias = weights
    bias, first, count = pattern
    qkv_bias = jnp.concatenate([vectors[0], jnp.zeros_like(vectors[0]), vectors[1]])
    qkv = (jnp.dot(hidden, mat_qkv, preferred_element_type=F32) + qkv_bias).astype(BF16)
    mixture, lse = attend(first, count, qkv, bias)
    branch = jnp.dot(mixture, mat_out, preferred_element_type=F32) + vectors[2]
    first_norm, normed_one, inv_one = norm_forward(
        hidden.astype(F32) + branch, vectors[4], vectors[5]
    )
    first_out = first_norm.astype(BF16)
    pre_act = jnp.dot(first_out, mat_up, preferred_element_type=F32) + up_bias
    act, slope = gelu_both(pre_act)
    act_low, slope = act.astype(BF16), slope.astype(BF16)
    down_out = jnp.dot(act_low, mat_down, preferred_element_type=F32) + vectors[3]
    final_out, normed_two, inv_two = norm_forward(
        first_out.astype(F32) + down_out, vectors[6], vectors[7]
    )
    saved = (
        hidden, qkv, lse, mixture, normed_one, inv_one, first_out, slope, act_low, normed_two, inv_two,
    )
    return final_out.astype(BF16), saved


def layer_backward(grad_y, weights, saved, pattern, settle, after):
    mat_qkv, mat_out, mat_up, mat_down, vectors, up_bias = weights
    (
        hidden, qkv, lse, mixture, normed_one, inv_one, first_out, slope, act_low, normed_two, inv_two,
    ) = saved
    bias, first, count = pattern
    width = hidden.shape[1]
    grad_gain_two = jnp.sum(grad_y * normed_two, axis=0)
    grad_shift_two = jnp.sum(grad_y, axis=0)
    grad_two = norm_backward(grad_y, normed_two, inv_two, vectors[6])
    grad_down_low = grad_two.astype(BF16)
    grad_bias_down = jnp.sum(grad_down_low.astype(F32), axis=0)
    grad_mat_down, grad_down_low = settle(
        jnp.einsum("tf,td->fd", act_low, grad_down_low, preferred_element_type=F32), grad_down_low
    )
    grad_act = jnp.einsum("td,fd->tf", grad_down_low, mat_down, preferred_element_type=F32)
    grad_pre = (grad_act * slope.astype(F32)).astype(BF16)
    grad_bias_hidden = jnp.sum(grad_pre.astype(F32), axis=0)
    grad_mat_up, grad_pre = settle(
        jnp.einsum("td,tf->df", first_out, grad_pre, preferred_element_type=F32), grad_pre
    )
    grad_first = grad_two + jnp.einsum("tf,df->td", grad_pre, mat_up, preferred_element_type=F32)
    grad_gain_one = jnp.sum(grad_first * normed_one, axis=0)
    grad_shift_one = jnp.sum(grad_first, axis=0)
    grad_one = norm_backward(grad_first, normed_one, inv_one, vectors[4])
    grad_branch = grad_one.astype(BF16)
    grad_bias_out = jnp.sum(grad_branch.astype(F32), axis=0)
    grad_mat_out, grad_branch = settle(
        jnp.einsum("td,te->de", mixture, grad_branch, preferred_element_type=F32), grad_branch
    )
    grad_mix = jnp.einsum("te,de->td", grad_branch, mat_out, preferred_element_type=F32)
    grad_qkv = after(attend_back(first, count, qkv, grad_mix.astype(BF16), bias, lse))
    grad_mat_qkv, grad_qkv = settle(
        jnp.einsum("td,te->de", hidden, grad_qkv, preferred_element_type=F32), grad_qkv
    )
    grad_hidden = grad_one + jnp.einsum("te,de->td", grad_qkv, mat_qkv, preferred_element_type=F32)
    bias_qkv = jnp.sum(grad_qkv.astype(F32), axis=0)
    grad_rows = jnp.stack(
        [
            bias_qkv[:width], bias_qkv[2 * width :], grad_bias_out, grad_bias_down,
            grad_gain_one, grad_shift_one, grad_gain_two, grad_shift_two,
        ]
    )
    return grad_hidden, (grad_mat_qkv, grad_mat_out, grad_mat_up, grad_mat_down), grad_rows, grad_bias_hidden


ANY_SPEC = pl.BlockSpec(memory_space=pl.ANY)
DMA = pltpu.SemaphoreType.DMA


class Place:
    def __init__(self, rows, cols):
        self.rows, self.cols = rows, cols
        self.row, self.col = lax.axis_index("row"), lax.axis_index("col")
        self.core = self.row % 2
        self.bits = list(range(1, rows.bit_length() - 1))
        self.orders = (self.bits, self.bits[::-1])

    def flipped(self, row, bit):
        return row + (1 - 2 * ((row // 2**bit) % 2)) * 2**bit

    def partner(self, bit):
        return (self.flipped(self.row, bit), self.col)

    def others(self, bits):
        found = [self.row]
        for bit in bits:
            found += [self.flipped(row, bit) for row in found]
        return found

    def greet(self):
        barrier = pltpu.get_barrier_semaphore()

        def signal(row, col):
            pl.semaphore_signal(
                barrier, inc=1, device_id=(row, col), device_id_type=pl.DeviceIdType.MESH
            )

        for bit in [0, *self.bits]:
            signal(*self.partner(bit))
        pl.when(self.col > 0)(lambda: signal(self.row, self.col - 1))
        pl.when(self.col < self.cols - 1)(lambda: signal(self.row, self.col + 1))
        inside = jnp.where((self.col > 0) & (self.col < self.cols - 1), 1, 0)
        pl.semaphore_wait(barrier, len(self.bits) + 2 + inside)


def remote(src, dst, send, recv, target):
    return pltpu.make_async_remote_copy(
        src_ref=src,
        dst_ref=dst,
        send_sem=send,
        recv_sem=recv,
        device_id=target,
        device_id_type=pl.DeviceIdType.MESH,
    )


def run_stages(items):
    plan = []
    for order, (time, stages) in enumerate(items):
        for index, stage in enumerate(stages):
            plan.append((time + index * GAP, order, stage))
    for _, _, stage in sorted(plan, key=lambda step: step[:2]):
        stage()


class LineGather:
    def __init__(self, place, own, slot, sems):
        self.place, self.own, self.slot, self.sems = place, own, slot, sems

    def copies(self, hop, receiving):
        place = self.place
        col, cols = place.col, place.cols
        for way, step in ((0, 1), (1, -1)):
            target = col + step
            if receiving:
                slot = col - step * (hop + 1)
                valid = (slot >= 0) & (slot < cols)
            else:
                slot = col - step * hop
                valid = (slot >= 0) & (slot < cols) & (target >= 0) & (target < cols)
            src = self.own if hop == 0 and not receiving else self.slot(slot)
            yield valid, lambda src=src, slot=slot, way=way, target=target: remote(
                src,
                self.slot(slot),
                self.sems.at[0, way, hop],
                self.sems.at[1, way, hop],
                (place.row, target),
            )

    def start(self, hop):
        for valid, copy in self.copies(hop, False):
            pl.when(valid)(lambda copy=copy: copy().start())

    def wait_recv(self, hop):
        for valid, copy in self.copies(hop, True):
            pl.when(valid)(lambda copy=copy: copy().wait_recv())

    def wait_send(self, hop):
        for valid, copy in self.copies(hop, False):
            pl.when(valid)(lambda copy=copy: copy().wait_send())


def cut(begin, size):
    first = size // 32 * 16
    return ((begin, first), (begin + first, size - first))


def place_side_by_side(slots, rows, out):
    width = slots.shape[2]
    for col in range(slots.shape[0]):
        out[rows, col * width : (col + 1) * width] = slots[col, rows, :]


def take_apart(whole, rows, slots):
    width = slots.shape[2]
    for col in range(slots.shape[0]):
        slots[col, rows, :] = whole[rows, col * width : (col + 1) * width]


def gather_item(place, own, slots, wide, whole, piece, local_sems, line_sems, chip_sems, core_sems):
    hops = place.cols - 1
    rows = pl.ds(*piece)
    line = LineGather(place, own.at[rows], lambda col: slots.at[col, rows], line_sems)
    mine = lambda: pltpu.make_async_copy(own.at[rows], slots.at[place.col, rows], local_sems.at[0])
    home = lambda: pltpu.make_async_copy(
        wide.at[rows], whole.at[place.row // 2, place.core, rows], local_sems.at[1]
    )

    def chip_copies(phase, receiving):
        for part, span in enumerate(cut(*piece)):
            order = place.orders[part]
            bit = order[phase]
            for index, row in enumerate(place.others(order[:phase])):
                if receiving:
                    row = place.flipped(row, bit)
                ref = whole.at[row // 2, row % 2, pl.ds(*span)]
                yield remote(
                    wide.at[pl.ds(*span)] if index == 0 else ref,
                    ref,
                    chip_sems.at[0, phase, part, index],
                    chip_sems.at[1, phase, part, index],
                    place.partner(bit),
                )

    def core_copy(receiving):
        ref = whole.at[:, 1 - place.core if receiving else place.core, rows]
        return remote(ref, ref, core_sems.at[0], core_sems.at[1], place.partner(0))

    phases = len(place.bits)

    def first():
        mine().start()
        line.start(0)

    def hop_stage(hop):
        line.wait_recv(hop - 1)
        line.start(hop)

    def chip_stage(phase):
        if phase == 0:
            line.wait_recv(hops - 1)
            mine().wait()
            place_side_by_side(slots, rows, wide)
        else:
            for copy in chip_copies(phase - 1, True):
                copy.wait_recv()
        for copy in chip_copies(phase, False):
            copy.start()
        if phase == 0:
            home().start()

    def core_stage():
        for copy in chip_copies(phases - 1, True):
            copy.wait_recv()
        home().wait()
        core_copy(False).start()

    def last():
        core_copy(True).wait_recv()
        core_copy(False).wait_send()
        for hop in range(hops):
            line.wait_send(hop)
        for phase in range(phases):
            for copy in chip_copies(phase, False):
                copy.wait_send()

    return (
        [first]
        + [functools.partial(hop_stage, hop) for hop in range(1, hops)]
        + [functools.partial(chip_stage, phase) for phase in range(phases)]
        + [core_stage, last]
    )


def gather_line_item(place, own, slots, wide, local_sem, line_sems):
    hops = place.cols - 1
    line = LineGather(place, own, lambda col: slots.at[col], line_sems)
    mine = lambda: pltpu.make_async_copy(own, slots.at[place.col], local_sem)

    def first():
        mine().start()
        line.start(0)

    def hop_stage(hop):
        line.wait_recv(hop - 1)
        line.start(hop)

    def last():
        line.wait_recv(hops - 1)
        mine().wait()
        if wide is not None:
            place_side_by_side(slots, slice(None), wide)
        for hop in range(hops):
            line.wait_send(hop)

    return [first] + [functools.partial(hop_stage, hop) for hop in range(1, hops)] + [last]


def exchange_item(place, halves, whole, sems, delay):
    parity = place.col % 2
    copy = lambda: remote(
        halves.at[1 - parity],
        whole.at[parity],
        sems.at[0],
        sems.at[1],
        (place.row, place.col + 1 - 2 * parity),
    )
    arriving = lambda: remote(
        halves.at[1 - parity],
        whole.at[1 - parity],
        sems.at[0],
        sems.at[1],
        (place.row, place.col + 1 - 2 * parity),
    )
    mine = lambda: pltpu.make_async_copy(halves.at[parity], whole.at[parity], sems.at[2])

    def first():
        copy().start()
        mine().start()

    def last():
        arriving().wait_recv()
        copy().wait_send()
        mine().wait()

    return [first] + [lambda: None] * delay + [last]


PIECE = 96
GAP = 2


def row_pieces(rs):
    return [(begin, min(PIECE, rs)) for begin in range(0, rs, PIECE)]


def gather_kernel(rows, cols, full_count, lined_count, *refs):
    refs = list(refs)

    def take(number):
        taken = refs[:number]
        del refs[:number]
        return taken

    full, lined, (small, tokens, marks) = take(full_count), take(lined_count), take(3)
    full_out, lined_out = take(full_count), take(lined_count)
    small_out, hidden, marks_out = take(3)
    slots, wide, lined_slots = take(full_count), take(full_count), take(lined_count)
    local_sems, line_sems, chip_sems, core_sems, exchange_sems = refs
    place = Place(rows, cols)
    place.greet()
    items = [
        (0, exchange_item(place, marks, marks_out, exchange_sems.at[1], 16)),
        (0, gather_line_item(place, small, small_out, None, local_sems.at[0, 0], line_sems.at[0])),
    ]
    number = 0
    for index in range(full_count):
        for piece in row_pieces(full[index].shape[0]):
            stages = gather_item(
                place,
                full[index],
                slots[index],
                wide[index],
                full_out[index],
                piece,
                local_sems.at[number + 1],
                line_sems.at[number + 1],
                chip_sems.at[number],
                core_sems.at[number],
            )
            items.append((number, stages))
            number += 1
    items.append((number, exchange_item(place, tokens, hidden, exchange_sems.at[0], 16)))
    for index in range(lined_count):
        at = number + index
        stages = gather_line_item(
            place,
            lined[index],
            lined_slots[index],
            lined_out[index],
            local_sems.at[at + 1, 0],
            line_sems.at[at + 1],
        )
        items.append((at, stages))
    run_stages(items)


def gather_all(rows, cols, full, lined, small, tokens, marks):
    number = sum(len(row_pieces(x.shape[0])) for x in full)
    phases = rows.bit_length() - 2
    like = lambda x, lead=(): jax.ShapeDtypeStruct(lead + x.shape, x.dtype)
    wide = [(x.shape[0], cols * x.shape[1]) for x in full]
    outs = [jax.ShapeDtypeStruct((rows // 2, 2) + shape, BF16) for shape in wide]
    outs += [jax.ShapeDtypeStruct((x.shape[0], cols * x.shape[1]), BF16) for x in lined]
    outs += [like(small, (cols,)), like(tokens), like(marks)]
    return pl.pallas_call(
        functools.partial(gather_kernel, rows, cols, len(full), len(lined)),
        out_shape=tuple(outs),
        in_specs=[ANY_SPEC] * (len(full) + len(lined) + 3),
        out_specs=(ANY_SPEC,) * len(full) + (VMEM_SPEC,) * len(lined) + (ANY_SPEC,) * 3,
        scratch_shapes=[pltpu.VMEM((cols,) + x.shape, BF16) for x in full]
        + [pltpu.VMEM(shape, BF16) for shape in wide]
        + [pltpu.VMEM((cols,) + x.shape, BF16) for x in lined]
        + [
            DMA((number + len(lined) + 1, 2)),
            DMA((number + len(lined) + 1, 2, 2, cols - 1)),
            DMA((number, 2, phases, 2, 2 ** (phases - 1))),
            DMA((number, 2)),
            DMA((2, 3)),
        ],
        compiler_params=pltpu.CompilerParams(
            collective_id=0, has_side_effects=True, vmem_limit_bytes=50 << 20
        ),
    )(*full, *lined, small, tokens, marks)


class LineReduce:
    def __init__(self, place, slot, arrived, sems):
        self.place, self.slot, self.arrived, self.sems = place, slot, arrived, sems

    def copies(self, hop, receiving):
        place = self.place
        last = place.cols - 1
        for way, step in ((0, 1), (1, -1)):
            here = place.col if way == 0 else last - place.col
            from_start = here if not receiving else here - 1
            slot = last - hop + from_start
            valid = (from_start <= hop) & (from_start >= 0) & (from_start < last)
            slot = slot if way == 0 else last - slot
            yield valid, slot, way, lambda way=way, slot=slot, step=step: remote(
                self.slot(slot),
                self.arrived.at[way, hop],
                self.sems.at[0, way, hop],
                self.sems.at[1, way, hop],
                (place.row, place.col + step),
            )

    def start(self, hop):
        for valid, _, _, copy in self.copies(hop, False):
            pl.when(valid)(lambda copy=copy: copy().start())

    def wait_send(self, hop):
        for valid, _, _, copy in self.copies(hop, False):
            pl.when(valid)(lambda copy=copy: copy().wait_send())

    def take(self, hop):
        for valid, slot, way, copy in self.copies(hop, True):

            def add(slot=slot, way=way, copy=copy):
                pltpu.make_async_copy(
                    self.arrived.at[way, hop], self.arrived.at[way, hop], self.sems.at[1, way, hop]
                ).wait()
                ref = self.slot(slot)
                ref[...] = ref[...] + self.arrived.at[way, hop][...]

            pl.when(valid)(add)

    def finish(self, out):
        hop = self.place.cols - 2
        own = self.slot(self.place.col)
        out[...] = own[...].astype(F32)
        for valid, _, way, copy in self.copies(hop, True):

            def add(way=way):
                pltpu.make_async_copy(
                    self.arrived.at[way, hop], self.arrived.at[way, hop], self.sems.at[1, way, hop]
                ).wait()
                out[...] = out[...] + self.arrived.at[way, hop][...].astype(F32)

            pl.when(valid)(add)
        for hop in range(self.place.cols - 1):
            self.wait_send(hop)


def line_stages(line, out, before):
    hops = line.place.cols - 1

    def first():
        before()
        line.start(0)

    def hop_stage(hop):
        line.take(hop - 1)
        line.start(hop)

    return (
        [first]
        + [functools.partial(hop_stage, hop) for hop in range(1, hops)]
        + [lambda: line.finish(out)]
    )


def reduce_item(place, partial, out, sums, from_core, from_chips, slots, from_line, piece, sems):
    local_sem, core_sems, chip_sems, line_sems = sems
    phases = len(place.bits)
    rows = pl.ds(*piece)
    core_copy = lambda: remote(
        partial.at[:, 1 - place.core, rows],
        from_core.at[:, rows],
        core_sems.at[0],
        core_sems.at[1],
        place.partner(0),
    )
    load = lambda: pltpu.make_async_copy(
        partial.at[:, place.core, rows], sums.at[:, rows], local_sem
    )
    line = LineReduce(
        place, lambda col: slots.at[col, rows], from_line.at[:, :, rows], line_sems
    )

    def chip_parts(phase):
        for part, span in enumerate(cut(*piece)):
            order = place.orders[part][::-1]
            yield part, pl.ds(*span), order[phase], order[phase + 1 :]

    def chip_copies(phase):
        for part, span, bit, rest in chip_parts(phase):
            for index, row in enumerate(place.others(rest)):
                row = place.flipped(row, bit)
                yield remote(
                    sums.at[row // 2, span],
                    from_chips[phase].at[index, span],
                    chip_sems.at[0, phase, part, index],
                    chip_sems.at[1, phase, part, index],
                    place.partner(bit),
                )

    def chip_take(phase):
        for part, span, _, rest in chip_parts(phase):
            for index, row in enumerate(place.others(rest)):
                arrived = from_chips[phase].at[index, span]
                pltpu.make_async_copy(arrived, arrived, chip_sems.at[1, phase, part, index]).wait()
                ref = sums.at[row // 2, span]
                ref[...] = ref[...] + arrived[...]

    def first():
        core_copy().start()
        load().start()

    def chip_stage(phase):
        if phase == 0:
            load().wait()
            core_copy().wait_recv()

            def add(pair, carry):
                ref = sums.at[pair, rows]
                ref[...] = ref[...] + from_core.at[pair, rows][...]
                return carry

            lax.fori_loop(0, place.rows // 2, add, 0)
        else:
            chip_take(phase - 1)
        for copy in chip_copies(phase):
            copy.start()

    def to_slots():
        chip_take(phases - 1)
        take_apart(sums.at[place.row // 2], rows, slots)

    def last():
        core_copy().wait_send()
        for phase in range(phases):
            for copy in chip_copies(phase):
                copy.wait_send()

    return (
        [first]
        + [functools.partial(chip_stage, phase) for phase in range(phases)]
        + line_stages(line, out.at[rows], to_slots)
        + [last]
    )


def reduce_line_item(place, partial, out, slots, from_line, line_sems):
    line = LineReduce(place, lambda col: slots.at[col], from_line, line_sems)
    return line_stages(line, out, lambda: take_apart(partial, slice(None), slots))


def reduce_small_item(place, partial, out, sums, arrived, from_line, sems, line_sems):
    bits = [0, *place.bits]
    line = LineReduce(place, lambda col: sums.at[col], from_line, line_sems)
    copy = lambda index: remote(
        sums, arrived.at[index], sems.at[0, index], sems.at[1, index], place.partner(bits[index])
    )

    def take(index):
        copy(index).wait()
        sums[...] = sums[...] + arrived[index]

    def stage(index):
        if index == 0:
            sums[...] = partial[...]
        else:
            take(index - 1)
        copy(index).start()

    return [functools.partial(stage, index) for index in range(len(bits))] + line_stages(
        line, out, lambda: take(len(bits) - 1)
    )


def reduce_kernel(rows, cols, full, lined, *refs):
    phases = rows.bit_length() - 2
    refs = list(refs)

    def take(number):
        taken = refs[:number]
        del refs[:number]
        return taken

    full_in, line_in, (small_in, tokens) = take(full), take(lined), take(2)
    mats_out, (small_out, tokens_out) = take(full), take(2)
    full_out, line_out = [ref.at[0] for ref in mats_out], [ref.at[1] for ref in mats_out]
    place = Place(rows, cols)
    place.greet()
    items = []
    small_sums, small_arrived, small_line, small_sems, small_line_sems = take(5)
    [token_sems] = take(1)
    parity = place.col % 2
    token_copy = lambda: remote(
        tokens, tokens_out, token_sems.at[0], token_sems.at[1], (place.row, place.col + 1 - 2 * parity)
    )
    time = 0
    for index in range(full):
        sums, from_core, slots, from_line = take(4)
        from_chips = take(phases)
        local_sems, core_sems, chip_sems, line_sems = take(4)
        for number, piece in enumerate(row_pieces(full_in[index].shape[2])):
            stages = reduce_item(
                place,
                full_in[index],
                full_out[index],
                sums,
                from_core,
                from_chips,
                slots,
                from_line,
                piece,
                (local_sems.at[number], core_sems.at[number], chip_sems.at[number], line_sems.at[number]),
            )
            items.append((time, stages))
            time += 1
    for index in range(lined):
        slots, from_line, line_sems = take(3)
        items.append(
            (index, reduce_line_item(place, line_in[index], line_out[index], slots, from_line, line_sems))
        )
    items.append(
        (1, reduce_small_item(place, small_in, small_out, small_sums, small_arrived, small_line, small_sems, small_line_sems))
    )
    items.append(
        (0, [lambda: token_copy().start()] + [lambda: None] * 12 + [lambda: token_copy().wait()])
    )
    run_stages(items)


def reduce_all(rows, cols, full, lined, small, tokens):
    phases = rows.bit_length() - 2
    hops = cols - 1
    shard = lambda x: (x.shape[-2], x.shape[-1] // cols)
    outs = [jax.ShapeDtypeStruct((2,) + shard(x), F32) for x in full]
    outs.append(jax.ShapeDtypeStruct(small.shape[1:], F32))
    outs.append(jax.ShapeDtypeStruct(tokens.shape, tokens.dtype))
    scratch = [
        pltpu.VMEM(small.shape, F32),
        pltpu.VMEM((phases + 1,) + small.shape, F32),
        pltpu.VMEM((2, hops) + small.shape[1:], F32),
        DMA((2, phases + 1)),
        DMA((2, 2, hops)),
        DMA((2,)),
    ]
    for x in full:
        count = len(row_pieces(x.shape[2]))
        scratch += [
            pltpu.VMEM((rows // 2,) + x.shape[2:], BF16),
            pltpu.VMEM((rows // 2,) + x.shape[2:], BF16),
            pltpu.VMEM((cols,) + shard(x), BF16),
            pltpu.VMEM((2, hops) + shard(x), BF16),
        ]
        scratch += [
            pltpu.VMEM((2 ** (phases - 1 - phase),) + x.shape[2:], BF16) for phase in range(phases)
        ]
        scratch += [
            DMA((count,)),
            DMA((count, 2)),
            DMA((count, 2, phases, 2, 2 ** (phases - 1))),
            DMA((count, 2, 2, hops)),
        ]
    for x in lined:
        scratch += [
            pltpu.VMEM((cols,) + shard(x), BF16),
            pltpu.VMEM((2, hops) + shard(x), BF16),
            DMA((2, 2, hops)),
        ]
    return pl.pallas_call(
        functools.partial(reduce_kernel, rows, cols, len(full), len(lined)),
        out_shape=tuple(outs),
        in_specs=[ANY_SPEC] * len(full) + [VMEM_SPEC] * (len(lined) + 1) + [ANY_SPEC],
        out_specs=(VMEM_SPEC,) * (len(full) + 1) + (ANY_SPEC,),
        scratch_shapes=scratch,
        compiler_params=pltpu.CompilerParams(
            collective_id=1, has_side_effects=True, vmem_limit_bytes=60 << 20
        ),
    )(*full, *lined, small, tokens)


def shards(
    rows, cols, tokens, seg_ids, pad_mask, rand_blocks, w_qkv, w_out, w_up, w_down, layer_vectors, bias_up, d_out
):
    layers = w_qkv.shape[0]
    parity = lax.axis_index("col") % 2
    half = seg_ids.shape[1]
    chosen = rand_blocks.reshape(2, 1, -1)
    chosen = jnp.pad(chosen, ((0, 0), (0, 0), (0, 128 - chosen.shape[2])))
    marks = jnp.concatenate(
        [seg_ids.reshape(2, -1, 128), pad_mask.reshape(2, -1, 128), chosen], axis=1
    )
    marks = jnp.pad(marks, ((0, 0), (0, -marks.shape[1] % 8), (0, 0)))
    part = layer_vectors.shape[2]
    small = jnp.concatenate([layer_vectors.reshape(-1, part), bias_up.reshape(-1, part)])
    small_rows = small.shape[0]
    small = jnp.pad(small, ((0, -small_rows % 16), (0, 0)))
    got = gather_all(
        rows,
        cols,
        [w_qkv[0], w_out[0], w_up[0], w_down[0], w_out[1]],
        [w_qkv[1], w_up[1], w_down[1]],
        small,
        tokens,
        marks,
    )
    vectors = got[8][:, : layers * 8].transpose(1, 0, 2).reshape(layers, 8, -1).astype(F32)
    up_biases = got[8][:, layers * 8 : small_rows].reshape(cols, layers, -1).transpose(1, 0, 2)
    up_biases = up_biases.reshape(layers, -1).astype(F32)
    hidden = got[9].reshape(2 * half, -1)
    marks = got[10]
    lines = half // 128
    seg, pad = marks[:, :lines].reshape(-1), marks[:, lines : 2 * lines].reshape(-1)
    rand = marks[:, 2 * lines, : half // BLOCK * rand_blocks.shape[2]]
    pattern = key_pattern(seg, pad, rand.reshape(-1, rand_blocks.shape[2]))

    whole = [g.reshape(-1, g.shape[3]) for g in got[:5]]
    qkv, up, down = (lax.all_gather(g, "row", axis=0, tiled=True) for g in got[5:8])
    first_mats, second_mats = whole[:4], (qkv, whole[4], up, down)
    weights = [
        (*layer_mats, vectors[layer], up_biases[layer])
        for layer, layer_mats in enumerate((first_mats, second_mats))
    ]
    kept = []
    for layer in range(layers):
        hidden, saved = layer_forward(hidden, weights[layer], pattern)
        kept.append(saved)
    output = from_sequence(hidden, parity, BF16)
    flow = to_sequence(d_out, parity).astype(F32)

    def settle_none(mat, following):
        return mat.astype(BF16), following

    def settle_rows(mat, following):
        mat, following = lax.optimization_barrier((mat.astype(BF16), following))
        return lax.psum_scatter(mat, "row", scatter_dimension=0, tiled=True), following

    grads, vec_grads, up_grads = [None] * layers, [None] * layers, [None] * layers
    flow, grads[1], vec_grads[1], up_grads[1] = layer_backward(
        flow, weights[1], kept[1], pattern, settle_rows, lambda x: x
    )
    qkv, out, up, down = grads[1]
    flow, down = lax.optimization_barrier((flow, down))
    held = []

    def after(x):
        x, other = lax.optimization_barrier((x, up))
        held.append(other)
        return x

    flow, grads[0], vec_grads[0], up_grads[0] = layer_backward(
        flow, weights[0], kept[0], pattern, settle_none, after
    )
    grads[1] = (qkv, out, held[0], down)
    full = [mat.reshape(rows // 2, 2, -1, mat.shape[1]) for mat in grads[0]]
    lined = grads[1]
    small = jnp.concatenate(
        [
            jnp.stack(vec_grads).reshape(layers * 8, cols, part).transpose(1, 0, 2),
            jnp.stack(up_grads).reshape(layers, cols, -1, part).transpose(1, 0, 2, 3).reshape(cols, -1, part),
        ],
        axis=1,
    )
    halves = flow.reshape(2, half, -1)
    summed = reduce_all(rows, cols, full, lined, small, pick(halves, 1 - parity).astype(BF16))
    mine = jnp.arange(2)[:, None, None] == parity
    d_tokens = jnp.where(mine, pick(halves, parity)[None], summed[5].astype(F32)[None])
    mats = summed[:4]
    vec = summed[4][: layers * 8].reshape(layers, 8, part)
    ups = summed[4][layers * 8 :].reshape(layers, -1)
    return output, d_tokens, *mats, vec, ups


def solution(mesh):
    in_specs = (
        P(None, ("row", "col"), None),
        P(None, ("row", "col")),
        P(None, ("row", "col")),
        P(None, ("row", "col"), None),
        P(None, "row", "col"),
        P(None, "row", "col"),
        P(None, "row", "col"),
        P(None, "row", "col"),
        P(None, None, "col"),
        P(None, "col"),
        P(None, ("row", "col"), None),
    )
    out_specs = (
        P(None, ("row", "col"), None),
        P(None, ("row", "col"), None),
        P(None, "row", "col"),
        P(None, "row", "col"),
        P(None, "row", "col"),
        P(None, "row", "col"),
        P(None, None, "col"),
        P(None, "col"),
    )
    local = functools.partial(shards, mesh.shape["row"], mesh.shape["col"])
    return jax.shard_map(local, mesh=mesh, in_specs=in_specs, out_specs=out_specs, check_vma=False)
```

```python
import functools
import jax
import jax.numpy as jnp
from jax import lax
from jax.experimental import pallas as pl
from jax.experimental.pallas import tpu as pltpu
from jax.sharding import PartitionSpec as P

HEAD = 64
PAIR = 2 * HEAD
TILE = 128
VMEM_SPEC = pl.BlockSpec(memory_space=pltpu.VMEM)
UNROLL = 6
UNROLL_BACK = 6
WIDTHS = (3, 4, 5, 6, 8)
SCALE = HEAD ** (-0.5)
NT = (((1,), (1,)), ((), ()))
F32 = jnp.float32
BF16 = jnp.bfloat16


def stack_heads(rows):
    first = lax.broadcasted_iota(jnp.int32, rows.shape, 1) < HEAD
    zero = jnp.zeros_like(rows)
    return jnp.concatenate([jnp.where(first, rows, zero), jnp.where(first, zero, rows)], axis=0)


def unstack_heads(both):
    half = both.shape[1] // 2
    first = lax.broadcasted_iota(jnp.int32, (both.shape[0], half), 0) < HEAD
    return jnp.where(first, both[:, :half], both[:, half:])


def by_width(count, blocks, run):
    low = 0
    for width in WIDTHS:
        width = min(width, blocks)
        if width == low:
            continue
        pl.when((count > low) & (count <= width))(functools.partial(run, width))
        low = width


def attend_kernel(first_ref, count_ref, qkv_ref, bias_ref, mix_ref, lse_ref, vt_ref):
    length, width3 = qkv_ref.shape
    model = width3 // 3
    blocks = length // TILE
    pairs = model // PAIR
    vt_ref[...] = qkv_ref[:, 2 * model :].T

    def one_tile(tile, carry):
        rows = pl.ds(pl.multiple_of(tile * TILE, TILE), TILE)

        def run(width):
            begin = jnp.minimum(first_ref[tile], blocks - width)
            keys = pl.ds(pl.multiple_of(begin * TILE, TILE), width * TILE)

            def one_pair(pair):
                cols = pl.ds(pl.multiple_of(pair * PAIR, PAIR), PAIR)
                k_cols = pl.ds(pl.multiple_of(model + pair * PAIR, PAIR), PAIR)
                both_q = stack_heads(qkv_ref[rows, cols] * SCALE)
                bias = bias_ref[keys, rows]
                scores = lax.dot_general(
                    qkv_ref[keys, k_cols], both_q, NT, preferred_element_type=F32
                ) + jnp.concatenate([bias, bias], axis=1)
                peak = jnp.max(scores, axis=0, keepdims=True)
                exponent = jnp.exp(scores - peak)
                total = jnp.sum(exponent, axis=0, keepdims=True)
                mixed = jnp.dot(
                    vt_ref[cols, keys], exponent.astype(BF16), preferred_element_type=F32
                )
                mixed = unstack_heads(mixed / total)
                mix_ref[rows, cols] = mixed.T.astype(BF16)
                lse_ref[pair, pl.ds(tile, 1), :] = peak + jnp.log(total)

            def some_pairs(step, carry):
                for offset in range(UNROLL):
                    one_pair(step * UNROLL + offset)
                return carry

            lax.fori_loop(0, pairs // UNROLL, some_pairs, 0)

        by_width(count_ref[tile], blocks, run)
        return carry

    lax.fori_loop(0, blocks, one_tile, 0)


def attend_back_kernel(
    first_ref, count_ref, qkv_ref, grad_ref, bias_ref, lse_ref, out_ref, kt_ref, dk_ref, dv_ref
):
    length, width3 = qkv_ref.shape
    model = width3 // 3
    blocks = length // TILE
    pairs = model // PAIR
    kt_ref[...] = qkv_ref[:, model : 2 * model].T
    dk_ref[...] = jnp.zeros_like(dk_ref)
    dv_ref[...] = jnp.zeros_like(dv_ref)

    def one_tile(tile, carry):
        rows = pl.ds(pl.multiple_of(tile * TILE, TILE), TILE)

        def run(width):
            begin = jnp.minimum(first_ref[tile], blocks - width)
            keys = pl.ds(pl.multiple_of(begin * TILE, TILE), width * TILE)

            def one_pair(pair):
                cols, k_cols, v_cols = (
                    pl.ds(pl.multiple_of(part * model + pair * PAIR, PAIR), PAIR)
                    for part in range(3)
                )
                both_q = stack_heads(qkv_ref[rows, cols] * SCALE)
                both_g = stack_heads(grad_ref[rows, cols])
                lse = lse_ref[pair, pl.ds(tile, 1), :]
                bias = bias_ref[keys, rows]
                scores = lax.dot_general(
                    qkv_ref[keys, k_cols], both_q, NT, preferred_element_type=F32
                ) + jnp.concatenate([bias, bias], axis=1)
                prob = jnp.exp(scores - lse)
                grad_p = lax.dot_general(
                    qkv_ref[keys, v_cols], both_g, NT, preferred_element_type=F32
                )
                delta = jnp.sum(grad_p * prob, axis=0, keepdims=True)
                grad_s = (prob * (grad_p - delta)).astype(BF16)
                dv = jnp.dot(prob.astype(BF16), both_g, preferred_element_type=F32)
                dk = jnp.dot(grad_s, both_q, preferred_element_type=F32)
                grad_q = jnp.dot(kt_ref[cols, keys], grad_s, preferred_element_type=F32)
                return (cols, dv, dk, (unstack_heads(grad_q) * SCALE).T.astype(BF16))

            def some_pairs(step, carry):
                done = [one_pair(step * UNROLL_BACK + offset) for offset in range(UNROLL_BACK)]
                for cols, dv, dk, dq in done:
                    dv_ref[keys, cols] += dv
                    dk_ref[keys, cols] += dk
                    out_ref[rows, cols] = dq
                return carry

            lax.fori_loop(0, pairs // UNROLL_BACK, some_pairs, 0)

        by_width(count_ref[tile], blocks, run)
        return carry

    lax.fori_loop(0, blocks, one_tile, 0)
    out_ref[:, model : 2 * model] = dk_ref[...].astype(BF16)
    out_ref[:, 2 * model :] = dv_ref[...].astype(BF16)


SMEM_SPEC = pl.BlockSpec(memory_space=pltpu.SMEM)


def attend(first, count, qkv, bias):
    length, width3 = qkv.shape
    model = width3 // 3
    pairs, blocks = model // PAIR, length // TILE
    return pl.pallas_call(
        attend_kernel,
        out_shape=(
            jax.ShapeDtypeStruct((length, model), BF16),
            jax.ShapeDtypeStruct((pairs, blocks, 2 * TILE), F32),
        ),
        in_specs=[SMEM_SPEC, SMEM_SPEC, VMEM_SPEC, VMEM_SPEC],
        out_specs=(VMEM_SPEC, VMEM_SPEC),
        scratch_shapes=[pltpu.VMEM((model, length), BF16)],
        compiler_params=pltpu.CompilerParams(vmem_limit_bytes=40 << 20),
    )(first, count, qkv, bias)


def attend_back(first, count, qkv, grad_mix, bias, lse):
    length, width3 = qkv.shape
    model = width3 // 3
    return pl.pallas_call(
        attend_back_kernel,
        out_shape=jax.ShapeDtypeStruct((length, width3), BF16),
        in_specs=[SMEM_SPEC, SMEM_SPEC] + [VMEM_SPEC] * 4,
        out_specs=VMEM_SPEC,
        scratch_shapes=[
            pltpu.VMEM((model, length), BF16),
            pltpu.VMEM((length, model), F32),
            pltpu.VMEM((length, model), F32),
        ],
        compiler_params=pltpu.CompilerParams(vmem_limit_bytes=48 << 20),
    )(first, count, qkv, grad_mix, bias, lse)

NEG_FILL = -1e30
EPS = 1e-06
ROOT_HALF = 0.7071067811865476
INV_ROOT_TAU = 0.3989422804014327
BLOCK = 64


def norm_forward(residual, norm_gain, norm_shift):
    center = residual - jnp.mean(residual, axis=-1, keepdims=True)
    scale_inv = lax.rsqrt(jnp.mean(center * center, axis=-1, keepdims=True) + EPS)
    normed = center * scale_inv
    return (normed * norm_gain + norm_shift, normed, scale_inv)


def norm_backward(grad_y, normed, scale_inv, norm_gain):
    grad_n = grad_y * norm_gain
    return scale_inv * (
        grad_n
        - jnp.mean(grad_n, axis=-1, keepdims=True)
        - normed * jnp.mean(grad_n * normed, axis=-1, keepdims=True)
    )


def gelu_both(pre_act):
    below = 0.5 * (1.0 + lax.erf(pre_act * ROOT_HALF))
    density = INV_ROOT_TAU * jnp.exp(-0.5 * pre_act * pre_act)
    return pre_act * below, below + pre_act * density


def swapped(block):
    count = lax.axis_size("col")
    return lax.ppermute(block, "col", [(i, i ^ 1) for i in range(count)])


def pick(array, index):
    return lax.dynamic_index_in_dim(array, index, 0, keepdims=False)


def to_sequence(halves, parity):
    own = pick(halves, parity)
    other = swapped(pick(halves, 1 - parity))
    first = parity == 0
    return jnp.concatenate([jnp.where(first, own, other), jnp.where(first, other, own)])


def from_sequence(whole, parity, narrow):
    halves = whole.reshape((2, -1) + whole.shape[1:])
    own = pick(halves, parity)
    other = swapped(pick(halves, 1 - parity).astype(narrow)).astype(whole.dtype)
    mine = jnp.arange(2)[:, None, None] == parity
    return jnp.where(mine, own[None], other[None])


def key_pattern(seg, pad, rand):
    length = seg.shape[0]
    places = jnp.arange(length, dtype=jnp.int32)
    starts = jnp.sum((seg[None, :] < seg[:, None]).astype(jnp.int32), axis=1)
    ends = jnp.sum((seg[None, :] <= seg[:, None]).astype(jnp.int32), axis=1)
    whole = places - starts < 2 * BLOCK
    block = places // BLOCK
    chosen = jnp.repeat(rand, BLOCK, axis=0)
    near = jnp.abs(block[:, None] - block[None, :]) <= 1
    hit = jnp.zeros((length, length), bool)
    for slot in range(rand.shape[1]):
        hit = hit | (block[:, None] == chosen[None, :, slot])
    allowed = (
        (seg[:, None] == seg[None, :])
        & (pad[:, None] > 0)
        & (whole[:, None] | whole[None, :] | near | hit)
    )
    allowed = allowed | (places[:, None] == places[None, :])
    bias = jnp.where(allowed, 0.0, NEG_FILL).astype(F32)
    first = starts[::TILE] // TILE
    count = (ends[TILE - 1 :: TILE] + TILE - 1) // TILE - first
    return bias, first, count


def layer_forward(hidden, weights, pattern):
    mat_qkv, mat_out, mat_up, mat_down, vectors, up_bias = weights
    bias, first, count = pattern
    qkv_bias = jnp.concatenate([vectors[0], jnp.zeros_like(vectors[0]), vectors[1]])
    qkv = (jnp.dot(hidden, mat_qkv, preferred_element_type=F32) + qkv_bias).astype(BF16)
    mixture, lse = attend(first, count, qkv, bias)
    branch = jnp.dot(mixture, mat_out, preferred_element_type=F32) + vectors[2]
    first_norm, normed_one, inv_one = norm_forward(
        hidden.astype(F32) + branch, vectors[4], vectors[5]
    )
    first_out = first_norm.astype(BF16)
    pre_act = jnp.dot(first_out, mat_up, preferred_element_type=F32) + up_bias
    act, slope = gelu_both(pre_act)
    act_low, slope = act.astype(BF16), slope.astype(BF16)
    down_out = jnp.dot(act_low, mat_down, preferred_element_type=F32) + vectors[3]
    final_out, normed_two, inv_two = norm_forward(
        first_out.astype(F32) + down_out, vectors[6], vectors[7]
    )
    saved = (
        hidden, qkv, lse, mixture, normed_one, inv_one, first_out, slope, act_low, normed_two, inv_two,
    )
    return final_out.astype(BF16), saved


def layer_backward(grad_y, weights, saved, pattern, settle, after):
    mat_qkv, mat_out, mat_up, mat_down, vectors, up_bias = weights
    (
        hidden, qkv, lse, mixture, normed_one, inv_one, first_out, slope, act_low, normed_two, inv_two,
    ) = saved
    bias, first, count = pattern
    width = hidden.shape[1]
    grad_gain_two = jnp.sum(grad_y * normed_two, axis=0)
    grad_shift_two = jnp.sum(grad_y, axis=0)
    grad_two = norm_backward(grad_y, normed_two, inv_two, vectors[6])
    grad_down_low = grad_two.astype(BF16)
    grad_bias_down = jnp.sum(grad_down_low.astype(F32), axis=0)
    grad_mat_down, grad_down_low = settle("down", act_low, grad_down_low)
    grad_act = jnp.einsum("td,fd->tf", grad_down_low, mat_down, preferred_element_type=F32)
    grad_pre = (grad_act * slope.astype(F32)).astype(BF16)
    grad_bias_hidden = jnp.sum(grad_pre.astype(F32), axis=0)
    grad_mat_up, grad_pre = settle("up", first_out, grad_pre)
    grad_first = grad_two + jnp.einsum("tf,df->td", grad_pre, mat_up, preferred_element_type=F32)
    grad_gain_one = jnp.sum(grad_first * normed_one, axis=0)
    grad_shift_one = jnp.sum(grad_first, axis=0)
    grad_one = norm_backward(grad_first, normed_one, inv_one, vectors[4])
    grad_branch = grad_one.astype(BF16)
    grad_bias_out = jnp.sum(grad_branch.astype(F32), axis=0)
    grad_mat_out, grad_branch = settle("out", mixture, grad_branch)
    grad_mix = jnp.einsum("te,de->td", grad_branch, mat_out, preferred_element_type=F32)
    grad_qkv = after(attend_back(first, count, qkv, grad_mix.astype(BF16), bias, lse))
    grad_mat_qkv, grad_qkv = settle("qkv", hidden, grad_qkv)
    grad_hidden = grad_one + jnp.einsum("te,de->td", grad_qkv, mat_qkv, preferred_element_type=F32)
    bias_qkv = jnp.sum(grad_qkv.astype(F32), axis=0)
    grad_rows = jnp.stack(
        [
            bias_qkv[:width], bias_qkv[2 * width :], grad_bias_out, grad_bias_down,
            grad_gain_one, grad_shift_one, grad_gain_two, grad_shift_two,
        ]
    )
    return grad_hidden, (grad_mat_qkv, grad_mat_out, grad_mat_up, grad_mat_down), grad_rows, grad_bias_hidden


ANY_SPEC = pl.BlockSpec(memory_space=pl.ANY)
DMA = pltpu.SemaphoreType.DMA


class Place:
    def __init__(self, rows, cols):
        self.rows, self.cols = rows, cols
        self.row, self.col = lax.axis_index("row"), lax.axis_index("col")
        self.core = self.row % 2
        self.bits = list(range(1, rows.bit_length() - 1))
        self.orders = (self.bits, self.bits[::-1])

    def flipped(self, row, bit):
        return row + (1 - 2 * ((row // 2**bit) % 2)) * 2**bit

    def partner(self, bit):
        return (self.flipped(self.row, bit), self.col)

    def others(self, bits):
        found = [self.row]
        for bit in bits:
            found += [self.flipped(row, bit) for row in found]
        return found

    def greet(self):
        barrier = pltpu.get_barrier_semaphore()

        def signal(row, col):
            pl.semaphore_signal(
                barrier, inc=1, device_id=(row, col), device_id_type=pl.DeviceIdType.MESH
            )

        for bit in [0, *self.bits]:
            signal(*self.partner(bit))
        pl.when(self.col > 0)(lambda: signal(self.row, self.col - 1))
        pl.when(self.col < self.cols - 1)(lambda: signal(self.row, self.col + 1))
        inside = jnp.where((self.col > 0) & (self.col < self.cols - 1), 1, 0)
        pl.semaphore_wait(barrier, len(self.bits) + 2 + inside)


def remote(src, dst, send, recv, target):
    return pltpu.make_async_remote_copy(
        src_ref=src,
        dst_ref=dst,
        send_sem=send,
        recv_sem=recv,
        device_id=target,
        device_id_type=pl.DeviceIdType.MESH,
    )


def run_stages(items):
    plan = []
    for order, (time, stages) in enumerate(items):
        for index, stage in enumerate(stages):
            plan.append((time + index * GAP, order, stage))
    for _, _, stage in sorted(plan, key=lambda step: step[:2]):
        stage()


class LineGather:
    def __init__(self, place, own, slot, sems):
        self.place, self.own, self.slot, self.sems = place, own, slot, sems

    def copies(self, hop, receiving):
        place = self.place
        col, cols = place.col, place.cols
        for way, step in ((0, 1), (1, -1)):
            target = col + step
            if receiving:
                slot = col - step * (hop + 1)
                valid = (slot >= 0) & (slot < cols)
            else:
                slot = col - step * hop
                valid = (slot >= 0) & (slot < cols) & (target >= 0) & (target < cols)
            src = self.own if hop == 0 and not receiving else self.slot(slot)
            yield valid, lambda src=src, slot=slot, way=way, target=target: remote(
                src,
                self.slot(slot),
                self.sems.at[0, way, hop],
                self.sems.at[1, way, hop],
                (place.row, target),
            )

    def start(self, hop):
        for valid, copy in self.copies(hop, False):
            pl.when(valid)(lambda copy=copy: copy().start())

    def wait_recv(self, hop):
        for valid, copy in self.copies(hop, True):
            pl.when(valid)(lambda copy=copy: copy().wait_recv())

    def wait_send(self, hop):
        for valid, copy in self.copies(hop, False):
            pl.when(valid)(lambda copy=copy: copy().wait_send())


def cut(begin, size):
    first = size // 32 * 16
    return ((begin, first), (begin + first, size - first))


def place_side_by_side(slots, rows, out):
    width = slots.shape[2]
    for col in range(slots.shape[0]):
        out[rows, col * width : (col + 1) * width] = slots[col, rows, :]


def take_apart(whole, rows, slots):
    width = slots.shape[2]
    for col in range(slots.shape[0]):
        slots[col, rows, :] = whole[rows, col * width : (col + 1) * width]


def gather_item(place, own, slots, wide, whole, piece, local_sems, line_sems, chip_sems, core_sems):
    hops = place.cols - 1
    rows = pl.ds(*piece)
    line = LineGather(place, own.at[rows], lambda col: slots.at[col, rows], line_sems)
    mine = lambda: pltpu.make_async_copy(own.at[rows], slots.at[place.col, rows], local_sems.at[0])
    home = lambda: pltpu.make_async_copy(
        wide.at[rows], whole.at[place.row // 2, place.core, rows], local_sems.at[1]
    )

    def chip_copies(phase, receiving):
        for part, span in enumerate(cut(*piece)):
            order = place.orders[part]
            bit = order[phase]
            for index, row in enumerate(place.others(order[:phase])):
                if receiving:
                    row = place.flipped(row, bit)
                ref = whole.at[row // 2, row % 2, pl.ds(*span)]
                yield remote(
                    wide.at[pl.ds(*span)] if index == 0 else ref,
                    ref,
                    chip_sems.at[0, phase, part, index],
                    chip_sems.at[1, phase, part, index],
                    place.partner(bit),
                )

    def core_copy(receiving):
        ref = whole.at[:, 1 - place.core if receiving else place.core, rows]
        return remote(ref, ref, core_sems.at[0], core_sems.at[1], place.partner(0))

    phases = len(place.bits)

    def first():
        mine().start()
        line.start(0)

    def hop_stage(hop):
        line.wait_recv(hop - 1)
        line.start(hop)

    def chip_stage(phase):
        if phase == 0:
            line.wait_recv(hops - 1)
            mine().wait()
            place_side_by_side(slots, rows, wide)
        else:
            for copy in chip_copies(phase - 1, True):
                copy.wait_recv()
        for copy in chip_copies(phase, False):
            copy.start()
        if phase == 0:
            home().start()

    def core_stage():
        for copy in chip_copies(phases - 1, True):
            copy.wait_recv()
        home().wait()
        core_copy(False).start()

    def last():
        core_copy(True).wait_recv()
        core_copy(False).wait_send()
        for hop in range(hops):
            line.wait_send(hop)
        for phase in range(phases):
            for copy in chip_copies(phase, False):
                copy.wait_send()

    return (
        [first]
        + [functools.partial(hop_stage, hop) for hop in range(1, hops)]
        + [functools.partial(chip_stage, phase) for phase in range(phases)]
        + [core_stage, last]
    )


def gather_line_item(place, own, slots, wide, local_sem, line_sems):
    hops = place.cols - 1
    line = LineGather(place, own, lambda col: slots.at[col], line_sems)
    mine = lambda: pltpu.make_async_copy(own, slots.at[place.col], local_sem)

    def first():
        mine().start()
        line.start(0)

    def hop_stage(hop):
        line.wait_recv(hop - 1)
        line.start(hop)

    def last():
        line.wait_recv(hops - 1)
        mine().wait()
        if wide is not None:
            place_side_by_side(slots, slice(None), wide)
        for hop in range(hops):
            line.wait_send(hop)

    return [first] + [functools.partial(hop_stage, hop) for hop in range(1, hops)] + [last]


def exchange_item(place, halves, whole, sems, delay):
    parity = place.col % 2
    copy = lambda: remote(
        halves.at[1 - parity],
        whole.at[parity],
        sems.at[0],
        sems.at[1],
        (place.row, place.col + 1 - 2 * parity),
    )
    arriving = lambda: remote(
        halves.at[1 - parity],
        whole.at[1 - parity],
        sems.at[0],
        sems.at[1],
        (place.row, place.col + 1 - 2 * parity),
    )
    mine = lambda: pltpu.make_async_copy(halves.at[parity], whole.at[parity], sems.at[2])

    def first():
        copy().start()
        mine().start()

    def last():
        arriving().wait_recv()
        copy().wait_send()
        mine().wait()

    return [first] + [lambda: None] * delay + [last]


PIECE = 96
GAP = 2


def row_pieces(rs):
    return [(begin, min(PIECE, rs)) for begin in range(0, rs, PIECE)]


FULL = ((0, 0), (1, 0), (2, 0), (3, 0), (1, 1))
ALONG = ((0, 1), (2, 1), (3, 1))


def gather_kernel(rows, cols, *refs):
    refs = list(refs)

    def take(number):
        taken = refs[:number]
        del refs[:number]
        return taken

    full_count, lined_count = len(FULL), len(ALONG)
    mats, (small, tokens, marks) = take(4), take(3)
    full = [mats[index].at[layer] for index, layer in FULL]
    lined = [mats[index].at[layer] for index, layer in ALONG]
    full_out, lined_out = take(full_count), take(lined_count)
    small_out, hidden, marks_out = take(3)
    slots, wide, lined_slots = take(full_count), take(full_count), take(lined_count)
    local_sems, line_sems, chip_sems, core_sems, exchange_sems = refs
    place = Place(rows, cols)
    place.greet()
    items = [
        (0, exchange_item(place, marks, marks_out, exchange_sems.at[1], 16)),
        (0, gather_line_item(place, small, small_out, None, local_sems.at[0, 0], line_sems.at[0])),
    ]
    number = 0
    for index in range(full_count):
        for piece in row_pieces(full[index].shape[0]):
            stages = gather_item(
                place,
                full[index],
                slots[index],
                wide[index],
                full_out[index],
                piece,
                local_sems.at[number + 1],
                line_sems.at[number + 1],
                chip_sems.at[number],
                core_sems.at[number],
            )
            items.append((number, stages))
            number += 1
    items.append((number, exchange_item(place, tokens, hidden, exchange_sems.at[0], 16)))
    for index in range(lined_count):
        at = number + index
        stages = gather_line_item(
            place,
            lined[index],
            lined_slots[index],
            lined_out[index],
            local_sems.at[at + 1, 0],
            line_sems.at[at + 1],
        )
        items.append((at, stages))
    run_stages(items)


def gather_all(rows, cols, mats, small, tokens, marks):
    full = [jax.ShapeDtypeStruct(mats[index].shape[1:], BF16) for index, _ in FULL]
    lined = [jax.ShapeDtypeStruct(mats[index].shape[1:], BF16) for index, _ in ALONG]
    number = sum(len(row_pieces(x.shape[0])) for x in full)
    phases = rows.bit_length() - 2
    like = lambda x, lead=(): jax.ShapeDtypeStruct(lead + x.shape, x.dtype)
    wide = [(x.shape[0], cols * x.shape[1]) for x in full]
    outs = [jax.ShapeDtypeStruct((rows // 2, 2) + shape, BF16) for shape in wide]
    outs += [jax.ShapeDtypeStruct((x.shape[0], cols * x.shape[1]), BF16) for x in lined]
    outs += [like(small, (cols,)), like(tokens), like(marks)]
    return pl.pallas_call(
        functools.partial(gather_kernel, rows, cols),
        out_shape=tuple(outs),
        in_specs=[ANY_SPEC] * 7,
        out_specs=(ANY_SPEC,) * len(full) + (VMEM_SPEC,) * len(lined) + (ANY_SPEC,) * 3,
        scratch_shapes=[pltpu.VMEM((cols,) + x.shape, BF16) for x in full]
        + [pltpu.VMEM(shape, BF16) for shape in wide]
        + [pltpu.VMEM((cols,) + x.shape, BF16) for x in lined]
        + [
            DMA((number + len(lined) + 1, 2)),
            DMA((number + len(lined) + 1, 2, 2, cols - 1)),
            DMA((number, 2, phases, 2, 2 ** (phases - 1))),
            DMA((number, 2)),
            DMA((2, 3)),
        ],
        compiler_params=pltpu.CompilerParams(
            collective_id=0, has_side_effects=True, vmem_limit_bytes=50 << 20
        ),
    )(*mats, small, tokens, marks)


class LineReduce:
    def __init__(self, place, slot, arrived, sems):
        self.place, self.slot, self.arrived, self.sems = place, slot, arrived, sems

    def copies(self, hop, receiving):
        place = self.place
        last = place.cols - 1
        for way, step in ((0, 1), (1, -1)):
            here = place.col if way == 0 else last - place.col
            from_start = here if not receiving else here - 1
            slot = last - hop + from_start
            valid = (from_start <= hop) & (from_start >= 0) & (from_start < last)
            slot = slot if way == 0 else last - slot
            yield valid, slot, way, lambda way=way, slot=slot, step=step: remote(
                self.slot(slot),
                self.arrived.at[way, hop],
                self.sems.at[0, way, hop],
                self.sems.at[1, way, hop],
                (place.row, place.col + step),
            )

    def start(self, hop):
        for valid, _, _, copy in self.copies(hop, False):
            pl.when(valid)(lambda copy=copy: copy().start())

    def wait_send(self, hop):
        for valid, _, _, copy in self.copies(hop, False):
            pl.when(valid)(lambda copy=copy: copy().wait_send())

    def take(self, hop):
        for valid, slot, way, copy in self.copies(hop, True):

            def add(slot=slot, way=way, copy=copy):
                pltpu.make_async_copy(
                    self.arrived.at[way, hop], self.arrived.at[way, hop], self.sems.at[1, way, hop]
                ).wait()
                ref = self.slot(slot)
                ref[...] = ref[...] + self.arrived.at[way, hop][...]

            pl.when(valid)(add)

    def finish(self, out):
        hop = self.place.cols - 2
        own = self.slot(self.place.col)
        out[...] = own[...].astype(F32)
        for valid, _, way, copy in self.copies(hop, True):

            def add(way=way):
                pltpu.make_async_copy(
                    self.arrived.at[way, hop], self.arrived.at[way, hop], self.sems.at[1, way, hop]
                ).wait()
                out[...] = out[...] + self.arrived.at[way, hop][...].astype(F32)

            pl.when(valid)(add)
        for hop in range(self.place.cols - 1):
            self.wait_send(hop)


def line_stages(line, out, before):
    hops = line.place.cols - 1

    def first():
        before()
        line.start(0)

    def hop_stage(hop):
        line.take(hop - 1)
        line.start(hop)

    return (
        [first]
        + [functools.partial(hop_stage, hop) for hop in range(1, hops)]
        + [lambda: line.finish(out)]
    )


def chunk_columns(x, y):
    width = y.shape[1] // max(1, x.shape[1] * y.shape[1] // (768 * 768))
    width = -(-width // 128) * 128
    return [slice(at, at + width) for at in range(0, y.shape[1], width)]


def product_step(place, x, y, sums, away, chunk):
    cols = chunk_columns(x, y)[chunk]
    result = lax.dot_general(
        x[...], y[:, cols], (((0,), (0,)), ((), ())), preferred_element_type=F32
    ).astype(BF16)
    size = sums.shape[1]
    for pair in range(place.rows // 2):
        even = result[2 * pair * size : (2 * pair + 1) * size]
        odd = result[(2 * pair + 1) * size : (2 * pair + 2) * size]
        sums[pair, :, cols] = jnp.where(place.core == 0, even, odd)
        away[pair, :, cols] = jnp.where(place.core == 0, odd, even)


def reduce_item(place, partial, away, out, sums, from_core, from_chips, slots, from_line, piece, sems):
    local_sem, core_sems, chip_sems, line_sems = sems
    phases = len(place.bits)
    rows = pl.ds(*piece)
    core_copy = lambda: remote(
        away.at[:, rows] if partial is None else partial.at[:, 1 - place.core, rows],
        from_core.at[:, rows],
        core_sems.at[0],
        core_sems.at[1],
        place.partner(0),
    )
    load = lambda: pltpu.make_async_copy(
        partial.at[:, place.core, rows], sums.at[:, rows], local_sem
    )
    line = LineReduce(
        place, lambda col: slots.at[col, rows], from_line.at[:, :, rows], line_sems
    )

    def chip_parts(phase):
        for part, span in enumerate(cut(*piece)):
            order = place.orders[part][::-1]
            yield part, pl.ds(*span), order[phase], order[phase + 1 :]

    def chip_copies(phase):
        for part, span, bit, rest in chip_parts(phase):
            for index, row in enumerate(place.others(rest)):
                row = place.flipped(row, bit)
                yield remote(
                    sums.at[row // 2, span],
                    from_chips[phase].at[index, span],
                    chip_sems.at[0, phase, part, index],
                    chip_sems.at[1, phase, part, index],
                    place.partner(bit),
                )

    def chip_take(phase):
        for part, span, _, rest in chip_parts(phase):
            for index, row in enumerate(place.others(rest)):
                arrived = from_chips[phase].at[index, span]
                pltpu.make_async_copy(arrived, arrived, chip_sems.at[1, phase, part, index]).wait()
                ref = sums.at[row // 2, span]
                ref[...] = ref[...] + arrived[...]

    def first():
        core_copy().start()
        if partial is not None:
            load().start()

    def chip_stage(phase):
        if phase == 0:
            if partial is not None:
                load().wait()
            core_copy().wait_recv()

            def add(pair, carry):
                ref = sums.at[pair, rows]
                ref[...] = ref[...] + from_core.at[pair, rows][...]
                return carry

            lax.fori_loop(0, place.rows // 2, add, 0)
        else:
            chip_take(phase - 1)
        for copy in chip_copies(phase):
            copy.start()

    def to_slots():
        chip_take(phases - 1)
        take_apart(sums.at[place.row // 2], rows, slots)

    def last():
        core_copy().wait_send()
        for phase in range(phases):
            for copy in chip_copies(phase):
                copy.wait_send()

    return (
        [first]
        + [functools.partial(chip_stage, phase) for phase in range(phases)]
        + line_stages(line, out.at[rows], to_slots)
        + [last]
    )


def reduce_line_item(place, partial, out, slots, from_line, line_sems):
    line = LineReduce(place, lambda col: slots.at[col], from_line, line_sems)
    return line_stages(line, out, lambda: take_apart(partial, slice(None), slots))


def reduce_small_item(place, partial, out, sums, arrived, from_line, sems, line_sems):
    bits = [0, *place.bits]
    line = LineReduce(place, lambda col: sums.at[col], from_line, line_sems)
    copy = lambda index: remote(
        sums, arrived.at[index], sems.at[0, index], sems.at[1, index], place.partner(bits[index])
    )

    def take(index):
        copy(index).wait()
        sums[...] = sums[...] + arrived[index]

    def stage(index):
        if index == 0:
            sums[...] = partial[...]
        else:
            take(index - 1)
        copy(index).start()

    return [functools.partial(stage, index) for index in range(len(bits))] + line_stages(
        line, out, lambda: take(len(bits) - 1)
    )


READY = ((1, 1), (0, 0))
PRODUCTS = ((2, 0), (1, 0), (3, 0))
LINED = ((0, 1), (2, 1), (3, 1))
SHARER, SHARED = 4, 1


def reduce_kernel(rows, cols, *refs):
    phases = rows.bit_length() - 2
    refs = list(refs)

    def take(number):
        taken = refs[:number]
        del refs[:number]
        return taken

    ready, factors, line_in = take(len(READY)), take(2 * len(PRODUCTS)), take(len(LINED))
    (small_in, tokens), mats_out, (small_out, tokens_out) = take(2), take(4), take(2)
    shard_of = lambda name: mats_out[name[0]].at[name[1]]
    held, [factor_sems] = take(2 * len(PRODUCTS) - 1), take(1)
    held.insert(SHARER, held[SHARED])
    place = Place(rows, cols)
    items = []
    small_sums, small_arrived, small_line, small_sems, small_line_sems = take(5)
    [token_sems] = take(1)
    parity = place.col % 2
    token_copy = lambda: remote(
        tokens, tokens_out, token_sems.at[0], token_sems.at[1], (place.row, place.col + 1 - 2 * parity)
    )
    starts, steps = {(0, 0): 0, (1, 1): 1, (2, 0): 2, (1, 0): 3, (3, 0): 4}, []
    times = {(2, 0): (0, 0, 1, 1), (1, 0): (2,), (3, 0): (2, 2, 3, 3)}
    loads = [
        pltpu.make_async_copy(factors[i], held[i], factor_sems.at[i]) for i in range(len(factors))
    ]
    for index, load in enumerate(loads):
        if index != SHARER:
            load.start()
    place.greet()
    for index, name in enumerate(READY + PRODUCTS):
        sums, from_core, slots, from_line = take(4)
        from_chips = take(phases)
        local_sems, core_sems, chip_sems, line_sems = take(4)
        partial, away = (ready[index], None) if name in READY else (None, *take(1))
        if partial is None:
            at = 2 * (index - len(READY))
            x, y = held[at], held[at + 1]
            steps.append((times[name][0], [lambda at=at: (loads[at].wait(), loads[at + 1].wait())]))
            for chunk in range(len(chunk_columns(x, y))):
                step = functools.partial(product_step, place, x, y, sums, away, chunk)
                steps.append((times[name][chunk], [step]))
            if at + 1 == SHARED:
                steps.append((times[name][-1], [loads[SHARER].start]))
        for number, piece in enumerate(row_pieces(sums.shape[1])):
            stages = reduce_item(
                place,
                partial,
                away,
                shard_of(name),
                sums,
                from_core,
                from_chips,
                slots,
                from_line,
                piece,
                (local_sems.at[number], core_sems.at[number], chip_sems.at[number], line_sems.at[number]),
            )
            items.append((starts[name] + number, stages))
    for index, name in enumerate(LINED):
        slots, from_line, line_sems = take(3)
        items.append(
            (index, reduce_line_item(place, line_in[index], shard_of(name), slots, from_line, line_sems))
        )
    items.append(
        (1, reduce_small_item(place, small_in, small_out, small_sums, small_arrived, small_line, small_sems, small_line_sems))
    )
    items.append(
        (0, [lambda: token_copy().start()] + [lambda: None] * 12 + [lambda: token_copy().wait()])
    )
    run_stages(items + steps)


def reduce_all(rows, cols, ready, products, lined, small, tokens):
    phases = rows.bit_length() - 2
    hops = cols - 1
    full = [x.shape[2:] for x in ready] + [(x.shape[1] // rows, y.shape[1]) for x, y in products]
    shard = lambda shape: (shape[0], shape[1] // cols)
    shapes = dict(zip(READY + PRODUCTS, full)) | {n: x.shape for n, x in zip(LINED, lined)}
    outs = [jax.ShapeDtypeStruct((2,) + shard(shapes[index, 0]), F32) for index in range(4)]
    outs.append(jax.ShapeDtypeStruct(small.shape[1:], F32))
    outs.append(jax.ShapeDtypeStruct(tokens.shape, tokens.dtype))
    factors = [factor for pair in products for factor in pair]
    scratch = [pltpu.VMEM(x.shape, BF16) for i, x in enumerate(factors) if i != SHARER]
    scratch.append(DMA((len(factors),)))
    scratch += [
        pltpu.VMEM(small.shape, F32),
        pltpu.VMEM((phases + 1,) + small.shape, F32),
        pltpu.VMEM((2, hops) + small.shape[1:], F32),
        DMA((2, phases + 1)),
        DMA((2, 2, hops)),
        DMA((2,)),
    ]
    for index, shape in enumerate(full):
        count = len(row_pieces(shape[0]))
        scratch += [
            pltpu.VMEM((rows // 2,) + shape, BF16),
            pltpu.VMEM((rows // 2,) + shape, BF16),
            pltpu.VMEM((cols,) + shard(shape), BF16),
            pltpu.VMEM((2, hops) + shard(shape), BF16),
        ]
        scratch += [
            pltpu.VMEM((2 ** (phases - 1 - phase),) + shape, BF16) for phase in range(phases)
        ]
        scratch += [
            DMA((count,)),
            DMA((count, 2)),
            DMA((count, 2, phases, 2, 2 ** (phases - 1))),
            DMA((count, 2, 2, hops)),
        ]
        if index >= len(ready):
            scratch.append(pltpu.VMEM((rows // 2,) + shape, BF16))
    for x in lined:
        scratch += [
            pltpu.VMEM((cols,) + shard(x.shape), BF16),
            pltpu.VMEM((2, hops) + shard(x.shape), BF16),
            DMA((2, 2, hops)),
        ]
    return pl.pallas_call(
        functools.partial(reduce_kernel, rows, cols),
        out_shape=tuple(outs),
        in_specs=[ANY_SPEC] * (len(ready) + len(factors))
        + [VMEM_SPEC] * (len(lined) + 1)
        + [ANY_SPEC],
        out_specs=(VMEM_SPEC,) * 5 + (ANY_SPEC,),
        scratch_shapes=scratch,
        compiler_params=pltpu.CompilerParams(
            collective_id=1, has_side_effects=True, vmem_limit_bytes=62 << 20
        ),
    )(*ready, *factors, *lined, small, tokens)


def shards(
    rows, cols, tokens, seg_ids, pad_mask, rand_blocks, w_qkv, w_out, w_up, w_down, layer_vectors, bias_up, d_out
):
    layers = w_qkv.shape[0]
    parity = lax.axis_index("col") % 2
    half = seg_ids.shape[1]
    chosen = rand_blocks.reshape(2, 1, -1)
    chosen = jnp.pad(chosen, ((0, 0), (0, 0), (0, 128 - chosen.shape[2])))
    marks = jnp.concatenate(
        [seg_ids.reshape(2, -1, 128), pad_mask.reshape(2, -1, 128), chosen], axis=1
    )
    marks = jnp.pad(marks, ((0, 0), (0, -marks.shape[1] % 8), (0, 0)))
    part = layer_vectors.shape[2]
    small = jnp.concatenate([layer_vectors.reshape(-1, part), bias_up.reshape(-1, part)])
    small_rows = small.shape[0]
    small = jnp.pad(small, ((0, -small_rows % 16), (0, 0)))
    got = gather_all(rows, cols, (w_qkv, w_out, w_up, w_down), small, tokens, marks)
    vectors = got[8][:, : layers * 8].transpose(1, 0, 2).reshape(layers, 8, -1).astype(F32)
    up_biases = got[8][:, layers * 8 : small_rows].reshape(cols, layers, -1).transpose(1, 0, 2)
    up_biases = up_biases.reshape(layers, -1).astype(F32)
    hidden = got[9].reshape(2 * half, -1)
    marks = got[10]
    lines = half // 128
    seg, pad = marks[:, :lines].reshape(-1), marks[:, lines : 2 * lines].reshape(-1)
    rand = marks[:, 2 * lines, : half // BLOCK * rand_blocks.shape[2]]
    pattern = key_pattern(seg, pad, rand.reshape(-1, rand_blocks.shape[2]))

    whole = [g.reshape(-1, g.shape[3]) for g in got[:5]]
    qkv, up, down = (lax.all_gather(g, "row", axis=0, tiled=True) for g in got[5:8])
    first_mats, second_mats = whole[:4], (qkv, whole[4], up, down)
    weights = [
        (*layer_mats, vectors[layer], up_biases[layer])
        for layer, layer_mats in enumerate((first_mats, second_mats))
    ]
    kept = []
    for layer in range(layers):
        hidden, saved = layer_forward(hidden, weights[layer], pattern)
        kept.append(saved)
    output = from_sequence(hidden, parity, BF16)
    flow = to_sequence(d_out, parity).astype(F32)

    def product(x, y):
        return jnp.einsum("td,te->de", x, y, preferred_element_type=F32).astype(BF16)

    def settle_first(kind, x, y):
        return (product(x, y) if kind == "qkv" else (x, y)), y

    def settle_second(kind, x, y):
        mat, y = lax.optimization_barrier((product(x, y), y))
        if kind != "out":
            mat = lax.psum_scatter(mat, "row", scatter_dimension=0, tiled=True)
        return mat, y

    grads, vec_grads, up_grads = [None] * layers, [None] * layers, [None] * layers
    flow, grads[1], vec_grads[1], up_grads[1] = layer_backward(
        flow, weights[1], kept[1], pattern, settle_second, lambda x: x
    )
    qkv, out, up, down = grads[1]
    flow, down = lax.optimization_barrier((flow, down))
    held = []

    def after(x):
        x, other = lax.optimization_barrier((x, up))
        held.append(other)
        return x

    flow, grads[0], vec_grads[0], up_grads[0] = layer_backward(
        flow, weights[0], kept[0], pattern, settle_first, after
    )
    split_rows = lambda mat: mat.reshape(rows // 2, 2, -1, mat.shape[1])
    ready = [split_rows(out), split_rows(grads[0][0])]
    lined = [qkv, held[0], down]
    small = jnp.concatenate(
        [
            jnp.stack(vec_grads).reshape(layers * 8, cols, part).transpose(1, 0, 2),
            jnp.stack(up_grads).reshape(layers, cols, -1, part).transpose(1, 0, 2, 3).reshape(cols, -1, part),
        ],
        axis=1,
    )
    halves = flow.reshape(2, half, -1)
    products = [grads[0][i] for i in (2, 1, 3)]
    leaving = pick(halves, 1 - parity).astype(BF16)
    summed = reduce_all(rows, cols, ready, products, lined, small, leaving)
    mine = jnp.arange(2)[:, None, None] == parity
    d_tokens = jnp.where(mine, pick(halves, parity)[None], summed[5].astype(F32)[None])
    mats = summed[:4]
    vec = summed[4][: layers * 8].reshape(layers, 8, part)
    ups = summed[4][layers * 8 :].reshape(layers, -1)
    return output, d_tokens, *mats, vec, ups


def solution(mesh):
    in_specs = (
        P(None, ("row", "col"), None),
        P(None, ("row", "col")),
        P(None, ("row", "col")),
        P(None, ("row", "col"), None),
        P(None, "row", "col"),
        P(None, "row", "col"),
        P(None, "row", "col"),
        P(None, "row", "col"),
        P(None, None, "col"),
        P(None, "col"),
        P(None, ("row", "col"), None),
    )
    out_specs = (
        P(None, ("row", "col"), None),
        P(None, ("row", "col"), None),
        P(None, "row", "col"),
        P(None, "row", "col"),
        P(None, "row", "col"),
        P(None, "row", "col"),
        P(None, None, "col"),
        P(None, "col"),
    )
    local = functools.partial(shards, mesh.shape["row"], mesh.shape["col"])
    return jax.shard_map(local, mesh=mesh, in_specs=in_specs, out_specs=out_specs, check_vma=False)
```

```python
import functools
import jax
import jax.numpy as jnp
from jax import lax
from jax.experimental import pallas as pl
from jax.experimental.pallas import tpu as pltpu
from jax.sharding import PartitionSpec as P

HEAD = 64
PAIR = 2 * HEAD
TILE = 128
VMEM_SPEC = pl.BlockSpec(memory_space=pltpu.VMEM)
UNROLL = 6
UNROLL_BACK = 6
WIDTHS = (2, 3, 4, 5, 6, 8)
SCALE = HEAD ** (-0.5)
NT = (((1,), (1,)), ((), ()))
F32 = jnp.float32
BF16 = jnp.bfloat16


def stack_heads(rows):
    first = lax.broadcasted_iota(jnp.int32, rows.shape, 1) < HEAD
    zero = jnp.zeros_like(rows)
    return jnp.concatenate([jnp.where(first, rows, zero), jnp.where(first, zero, rows)], axis=0)


def unstack_heads(both):
    half = both.shape[1] // 2
    first = lax.broadcasted_iota(jnp.int32, (both.shape[0], half), 0) < HEAD
    return jnp.where(first, both[:, :half], both[:, half:])


def by_width(count, blocks, run):
    low = 0
    for width in WIDTHS:
        width = min(width, blocks)
        if width == low:
            continue
        pl.when((count > low) & (count <= width))(functools.partial(run, width))
        low = width


def attend_kernel(first_ref, count_ref, qkv_ref, bias_ref, mix_ref, lse_ref, vt_ref):
    length, width3 = qkv_ref.shape
    model = width3 // 3
    blocks = length // TILE
    pairs = model // PAIR
    vt_ref[...] = qkv_ref[:, 2 * model :].T

    def one_tile(tile, carry):
        rows = pl.ds(pl.multiple_of(tile * TILE, TILE), TILE)

        def run(width):
            begin = jnp.minimum(first_ref[tile], blocks - width)
            keys = pl.ds(pl.multiple_of(begin * TILE, TILE), width * TILE)

            def one_pair(pair):
                cols = pl.ds(pl.multiple_of(pair * PAIR, PAIR), PAIR)
                k_cols = pl.ds(pl.multiple_of(model + pair * PAIR, PAIR), PAIR)
                both_q = stack_heads(qkv_ref[rows, cols] * SCALE)
                bias = bias_ref[keys, rows]
                scores = lax.dot_general(
                    qkv_ref[keys, k_cols], both_q, NT, preferred_element_type=F32
                ) + jnp.concatenate([bias, bias], axis=1)
                peak = jnp.max(scores, axis=0, keepdims=True)
                exponent = jnp.exp(scores - peak)
                total = jnp.sum(exponent, axis=0, keepdims=True)
                mixed = jnp.dot(
                    vt_ref[cols, keys], exponent.astype(BF16), preferred_element_type=F32
                )
                mixed = unstack_heads(mixed / total)
                mix_ref[rows, cols] = mixed.T.astype(BF16)
                lse_ref[pair, pl.ds(tile, 1), :] = peak + jnp.log(total)

            def some_pairs(step, carry):
                for offset in range(UNROLL):
                    one_pair(step * UNROLL + offset)
                return carry

            lax.fori_loop(0, pairs // UNROLL, some_pairs, 0)

        by_width(count_ref[tile], blocks, run)
        return carry

    lax.fori_loop(0, blocks, one_tile, 0)


def attend_back_kernel(
    first_ref, count_ref, qkv_ref, grad_ref, bias_ref, lse_ref, out_ref, kt_ref, dk_ref, dv_ref
):
    length, width3 = qkv_ref.shape
    model = width3 // 3
    blocks = length // TILE
    pairs = model // PAIR
    kt_ref[...] = qkv_ref[:, model : 2 * model].T
    dk_ref[...] = jnp.zeros_like(dk_ref)
    dv_ref[...] = jnp.zeros_like(dv_ref)

    def one_tile(tile, carry):
        rows = pl.ds(pl.multiple_of(tile * TILE, TILE), TILE)

        def run(width):
            begin = jnp.minimum(first_ref[tile], blocks - width)
            keys = pl.ds(pl.multiple_of(begin * TILE, TILE), width * TILE)

            def one_pair(pair):
                cols, k_cols, v_cols = (
                    pl.ds(pl.multiple_of(part * model + pair * PAIR, PAIR), PAIR)
                    for part in range(3)
                )
                both_q = stack_heads(qkv_ref[rows, cols] * SCALE)
                both_g = stack_heads(grad_ref[rows, cols])
                lse = lse_ref[pair, pl.ds(tile, 1), :]
                bias = bias_ref[keys, rows]
                scores = lax.dot_general(
                    qkv_ref[keys, k_cols], both_q, NT, preferred_element_type=F32
                ) + jnp.concatenate([bias, bias], axis=1)
                prob = jnp.exp(scores - lse)
                grad_p = lax.dot_general(
                    qkv_ref[keys, v_cols], both_g, NT, preferred_element_type=F32
                )
                delta = jnp.sum(grad_p * prob, axis=0, keepdims=True)
                grad_s = (prob * (grad_p - delta)).astype(BF16)
                dv = jnp.dot(prob.astype(BF16), both_g, preferred_element_type=F32)
                dk = jnp.dot(grad_s, both_q, preferred_element_type=F32)
                grad_q = jnp.dot(kt_ref[cols, keys], grad_s, preferred_element_type=F32)
                return (cols, dv, dk, (unstack_heads(grad_q) * SCALE).T.astype(BF16))

            def some_pairs(step, carry):
                done = [one_pair(step * UNROLL_BACK + offset) for offset in range(UNROLL_BACK)]
                for cols, dv, dk, dq in done:
                    dv_ref[keys, cols] += dv
                    dk_ref[keys, cols] += dk
                    out_ref[rows, cols] = dq
                return carry

            lax.fori_loop(0, pairs // UNROLL_BACK, some_pairs, 0)

        by_width(count_ref[tile], blocks, run)
        return carry

    lax.fori_loop(0, blocks, one_tile, 0)
    out_ref[:, model : 2 * model] = dk_ref[...].astype(BF16)
    out_ref[:, 2 * model :] = dv_ref[...].astype(BF16)


SMEM_SPEC = pl.BlockSpec(memory_space=pltpu.SMEM)


def attend(first, count, qkv, bias):
    length, width3 = qkv.shape
    model = width3 // 3
    pairs, blocks = model // PAIR, length // TILE
    return pl.pallas_call(
        attend_kernel,
        out_shape=(
            jax.ShapeDtypeStruct((length, model), BF16),
            jax.ShapeDtypeStruct((pairs, blocks, 2 * TILE), F32),
        ),
        in_specs=[SMEM_SPEC, SMEM_SPEC, VMEM_SPEC, VMEM_SPEC],
        out_specs=(VMEM_SPEC, VMEM_SPEC),
        scratch_shapes=[pltpu.VMEM((model, length), BF16)],
        compiler_params=pltpu.CompilerParams(vmem_limit_bytes=20 << 20),
    )(first, count, qkv, bias)


def attend_back(first, count, qkv, grad_mix, bias, lse):
    length, width3 = qkv.shape
    model = width3 // 3
    return pl.pallas_call(
        attend_back_kernel,
        out_shape=jax.ShapeDtypeStruct((length, width3), BF16),
        in_specs=[SMEM_SPEC, SMEM_SPEC] + [VMEM_SPEC] * 4,
        out_specs=VMEM_SPEC,
        scratch_shapes=[
            pltpu.VMEM((model, length), BF16),
            pltpu.VMEM((length, model), F32),
            pltpu.VMEM((length, model), F32),
        ],
        compiler_params=pltpu.CompilerParams(vmem_limit_bytes=30 << 20),
    )(first, count, qkv, grad_mix, bias, lse)

NEG_FILL = -1e30
EPS = 1e-06
ROOT_HALF = 0.7071067811865476
INV_ROOT_TAU = 0.3989422804014327
BLOCK = 64


def norm_forward(residual, norm_gain, norm_shift):
    center = residual - jnp.mean(residual, axis=-1, keepdims=True)
    scale_inv = lax.rsqrt(jnp.mean(center * center, axis=-1, keepdims=True) + EPS)
    normed = center * scale_inv
    return (normed * norm_gain + norm_shift, normed, scale_inv)


def norm_backward(grad_y, normed, scale_inv, norm_gain):
    grad_n = grad_y * norm_gain
    return scale_inv * (
        grad_n
        - jnp.mean(grad_n, axis=-1, keepdims=True)
        - normed * jnp.mean(grad_n * normed, axis=-1, keepdims=True)
    )


def gelu_both(pre_act):
    below = 0.5 * (1.0 + lax.erf(pre_act * ROOT_HALF))
    density = INV_ROOT_TAU * jnp.exp(-0.5 * pre_act * pre_act)
    return pre_act * below, below + pre_act * density


def swapped(block):
    count = lax.axis_size("col")
    return lax.ppermute(block, "col", [(i, i ^ 1) for i in range(count)])


def pick(array, index):
    return lax.dynamic_index_in_dim(array, index, 0, keepdims=False)


def chosen_by(parity, own, other):
    mine = jnp.arange(2).reshape((2,) + (1,) * other.ndim) == parity
    return jnp.where(mine, own, other[None])


def to_sequence(halves, parity):
    both = chosen_by(parity, halves, swapped(pick(halves, 1 - parity)))
    return both.reshape((-1,) + both.shape[2:])


def from_sequence(whole, parity):
    halves = whole.reshape((2, -1) + whole.shape[1:])
    return chosen_by(parity, halves, swapped(pick(halves, 1 - parity)))


def key_pattern(seg, pad, rand):
    length = seg.shape[0]
    places = jnp.arange(length, dtype=jnp.int32)
    starts = jnp.sum((seg[None, :] < seg[:, None]).astype(jnp.int32), axis=1)
    ends = jnp.sum((seg[None, :] <= seg[:, None]).astype(jnp.int32), axis=1)
    whole = places - starts < 2 * BLOCK
    block = places // BLOCK
    chosen = jnp.repeat(rand, BLOCK, axis=0)
    near = jnp.abs(block[:, None] - block[None, :]) <= 1
    hit = jnp.zeros((length, length), bool)
    for slot in range(rand.shape[1]):
        hit = hit | (block[:, None] == chosen[None, :, slot])
    allowed = (
        (seg[:, None] == seg[None, :])
        & (pad[:, None] > 0)
        & (whole[:, None] | whole[None, :] | near | hit)
    )
    allowed = allowed | (places[:, None] == places[None, :])
    bias = jnp.where(allowed, 0.0, NEG_FILL).astype(F32)
    first = starts[::TILE] // TILE
    count = (ends[TILE - 1 :: TILE] + TILE - 1) // TILE - first
    return bias, first, count


def layer_forward(hidden, weights, pattern):
    mat_qkv, mat_out, mat_up, mat_down, vectors, up_bias = weights
    bias, first, count = pattern
    qkv_bias = jnp.concatenate([vectors[0], jnp.zeros_like(vectors[0]), vectors[1]])
    qkv = (jnp.dot(hidden, mat_qkv, preferred_element_type=F32) + qkv_bias).astype(BF16)
    mixture, lse = attend(first, count, qkv, bias)
    branch = jnp.dot(mixture, mat_out, preferred_element_type=F32) + vectors[2]
    first_norm, normed_one, inv_one = norm_forward(
        hidden.astype(F32) + branch, vectors[4], vectors[5]
    )
    first_out = first_norm.astype(BF16)
    pre_act = jnp.dot(first_out, mat_up, preferred_element_type=F32) + up_bias
    act, slope = gelu_both(pre_act)
    act_low, slope = act.astype(BF16), slope.astype(BF16)
    down_out = jnp.dot(act_low, mat_down, preferred_element_type=F32) + vectors[3]
    final_out, normed_two, inv_two = norm_forward(
        first_out.astype(F32) + down_out, vectors[6], vectors[7]
    )
    saved = (
        hidden, qkv, lse, mixture, normed_one, inv_one, first_out, slope, act_low, normed_two, inv_two,
    )
    return final_out.astype(BF16), saved


def layer_backward(grad_y, weights, saved, pattern, settle, after):
    mat_qkv, mat_out, mat_up, mat_down, vectors, up_bias = weights
    (
        hidden, qkv, lse, mixture, normed_one, inv_one, first_out, slope, act_low, normed_two, inv_two,
    ) = saved
    bias, first, count = pattern
    width = hidden.shape[1]
    grad_gain_two = jnp.sum(grad_y * normed_two, axis=0)
    grad_shift_two = jnp.sum(grad_y, axis=0)
    grad_two = norm_backward(grad_y, normed_two, inv_two, vectors[6])
    grad_down_low = grad_two.astype(BF16)
    grad_bias_down = jnp.sum(grad_down_low.astype(F32), axis=0)
    grad_mat_down, grad_down_low = settle("down", act_low, grad_down_low)
    grad_act = jnp.einsum("td,fd->tf", grad_down_low, mat_down, preferred_element_type=F32)
    grad_pre = (grad_act * slope.astype(F32)).astype(BF16)
    grad_bias_hidden = jnp.sum(grad_pre.astype(F32), axis=0)
    grad_mat_up, grad_pre = settle("up", first_out, grad_pre)
    grad_first = grad_two + jnp.einsum("tf,df->td", grad_pre, mat_up, preferred_element_type=F32)
    grad_gain_one = jnp.sum(grad_first * normed_one, axis=0)
    grad_shift_one = jnp.sum(grad_first, axis=0)
    grad_one = norm_backward(grad_first, normed_one, inv_one, vectors[4])
    grad_branch = grad_one.astype(BF16)
    grad_bias_out = jnp.sum(grad_branch.astype(F32), axis=0)
    grad_mat_out, grad_branch = settle("out", mixture, grad_branch)
    grad_mix = jnp.einsum("te,de->td", grad_branch, mat_out, preferred_element_type=F32)
    grad_qkv = after(attend_back(first, count, qkv, grad_mix.astype(BF16), bias, lse))
    grad_mat_qkv, grad_qkv = settle("qkv", hidden, grad_qkv)
    grad_hidden = grad_one + jnp.einsum("te,de->td", grad_qkv, mat_qkv, preferred_element_type=F32)
    bias_qkv = jnp.sum(grad_qkv.astype(F32), axis=0)
    grad_rows = jnp.stack(
        [
            bias_qkv[:width], bias_qkv[2 * width :], grad_bias_out, grad_bias_down,
            grad_gain_one, grad_shift_one, grad_gain_two, grad_shift_two,
        ]
    )
    return grad_hidden, (grad_mat_qkv, grad_mat_out, grad_mat_up, grad_mat_down), grad_rows, grad_bias_hidden


ANY_SPEC = pl.BlockSpec(memory_space=pl.ANY)
DMA = pltpu.SemaphoreType.DMA


class Place:
    def __init__(self, rows, cols):
        self.rows, self.cols = rows, cols
        self.row, self.col = lax.axis_index("row"), lax.axis_index("col")
        self.core = self.row % 2
        self.bits = list(range(1, rows.bit_length() - 1))
        self.orders = (self.bits, self.bits[::-1])

    def flipped(self, row, bit):
        return row + (1 - 2 * ((row // 2**bit) % 2)) * 2**bit

    def partner(self, bit):
        return (self.flipped(self.row, bit), self.col)

    def others(self, bits):
        found = [self.row]
        for bit in bits:
            found += [self.flipped(row, bit) for row in found]
        return found

    def greet(self):
        barrier = pltpu.get_barrier_semaphore()

        def signal(row, col):
            pl.semaphore_signal(
                barrier, inc=1, device_id=(row, col), device_id_type=pl.DeviceIdType.MESH
            )

        for bit in [0, *self.bits]:
            signal(*self.partner(bit))
        pl.when(self.col > 0)(lambda: signal(self.row, self.col - 1))
        pl.when(self.col < self.cols - 1)(lambda: signal(self.row, self.col + 1))
        inside = jnp.where((self.col > 0) & (self.col < self.cols - 1), 1, 0)
        pl.semaphore_wait(barrier, len(self.bits) + 2 + inside)


def remote(src, dst, send, recv, target):
    return pltpu.make_async_remote_copy(
        src_ref=src,
        dst_ref=dst,
        send_sem=send,
        recv_sem=recv,
        device_id=target,
        device_id_type=pl.DeviceIdType.MESH,
    )


def run_stages(items):
    plan = []
    for order, (time, stages) in enumerate(items):
        for index, stage in enumerate(stages):
            plan.append((time + index * GAP, order, stage))
    for _, _, stage in sorted(plan, key=lambda step: step[:2]):
        stage()


class LineGather:
    def __init__(self, place, own, slot, sems):
        self.place, self.own, self.slot, self.sems = place, own, slot, sems

    def copies(self, hop, receiving):
        place = self.place
        col, cols = place.col, place.cols
        for way, step in ((0, 1), (1, -1)):
            target = col + step
            if receiving:
                slot = col - step * (hop + 1)
                valid = (slot >= 0) & (slot < cols)
            else:
                slot = col - step * hop
                valid = (slot >= 0) & (slot < cols) & (target >= 0) & (target < cols)
            src = self.own if hop == 0 and not receiving else self.slot(slot)
            yield valid, lambda src=src, slot=slot, way=way, target=target: remote(
                src,
                self.slot(slot),
                self.sems.at[0, way, hop],
                self.sems.at[1, way, hop],
                (place.row, target),
            )

    def start(self, hop):
        for valid, copy in self.copies(hop, False):
            pl.when(valid)(lambda copy=copy: copy().start())

    def wait_recv(self, hop):
        for valid, copy in self.copies(hop, True):
            pl.when(valid)(lambda copy=copy: copy().wait_recv())

    def wait_send(self, hop):
        for valid, copy in self.copies(hop, False):
            pl.when(valid)(lambda copy=copy: copy().wait_send())


def cut(begin, size):
    first = size // 32 * 16
    return ((begin, first), (begin + first, size - first))


def place_side_by_side(slots, rows, out):
    width = slots.shape[2]
    for col in range(slots.shape[0]):
        out[rows, col * width : (col + 1) * width] = slots[col, rows, :]


def take_apart(whole, rows, slots):
    width = slots.shape[2]
    for col in range(slots.shape[0]):
        slots[col, rows, :] = whole[rows, col * width : (col + 1) * width]


def gather_item(place, own, slots, wide, whole, piece, local_sems, line_sems, chip_sems, core_sems):
    hops = place.cols - 1
    rows = pl.ds(*piece)
    line = LineGather(place, own.at[rows], lambda col: slots.at[col, rows], line_sems)
    mine = lambda: pltpu.make_async_copy(own.at[rows], slots.at[place.col, rows], local_sems.at[0])
    home = lambda: pltpu.make_async_copy(
        wide.at[rows], whole.at[place.row // 2, place.core, rows], local_sems.at[1]
    )

    def chip_copies(phase, receiving):
        for part, span in enumerate(cut(*piece)):
            order = place.orders[part]
            bit = order[phase]
            for index, row in enumerate(place.others(order[:phase])):
                if receiving:
                    row = place.flipped(row, bit)
                ref = whole.at[row // 2, row % 2, pl.ds(*span)]
                yield remote(
                    wide.at[pl.ds(*span)] if index == 0 else ref,
                    ref,
                    chip_sems.at[0, phase, part, index],
                    chip_sems.at[1, phase, part, index],
                    place.partner(bit),
                )

    def core_copy(receiving):
        ref = whole.at[:, 1 - place.core if receiving else place.core, rows]
        return remote(ref, ref, core_sems.at[0], core_sems.at[1], place.partner(0))

    phases = len(place.bits)

    def first():
        mine().start()
        line.start(0)

    def hop_stage(hop):
        line.wait_recv(hop - 1)
        line.start(hop)

    def chip_stage(phase):
        if phase == 0:
            line.wait_recv(hops - 1)
            mine().wait()
            place_side_by_side(slots, rows, wide)
        else:
            for copy in chip_copies(phase - 1, True):
                copy.wait_recv()
        for copy in chip_copies(phase, False):
            copy.start()
        if phase == 0:
            home().start()

    def core_stage():
        for copy in chip_copies(phases - 1, True):
            copy.wait_recv()
        home().wait()
        core_copy(False).start()

    def last():
        core_copy(True).wait_recv()
        core_copy(False).wait_send()
        for hop in range(hops):
            line.wait_send(hop)
        for phase in range(phases):
            for copy in chip_copies(phase, False):
                copy.wait_send()

    return (
        [first]
        + [functools.partial(hop_stage, hop) for hop in range(1, hops)]
        + [functools.partial(chip_stage, phase) for phase in range(phases)]
        + [core_stage, last]
    )


def gather_line_item(place, own, slots, wide, local_sem, line_sems):
    hops = place.cols - 1
    line = LineGather(place, own, lambda col: slots.at[col], line_sems)
    mine = lambda: pltpu.make_async_copy(own, slots.at[place.col], local_sem)

    def first():
        mine().start()
        line.start(0)

    def hop_stage(hop):
        line.wait_recv(hop - 1)
        line.start(hop)

    def last():
        line.wait_recv(hops - 1)
        mine().wait()
        if wide is not None:
            place_side_by_side(slots, slice(None), wide)
        for hop in range(hops):
            line.wait_send(hop)

    return [first] + [functools.partial(hop_stage, hop) for hop in range(1, hops)] + [last]


def exchange_item(place, halves, whole, sems, delay):
    parity = place.col % 2
    copy = lambda: remote(
        halves.at[1 - parity],
        whole.at[parity],
        sems.at[0],
        sems.at[1],
        (place.row, place.col + 1 - 2 * parity),
    )
    arriving = lambda: remote(
        halves.at[1 - parity],
        whole.at[1 - parity],
        sems.at[0],
        sems.at[1],
        (place.row, place.col + 1 - 2 * parity),
    )
    mine = lambda: pltpu.make_async_copy(halves.at[parity], whole.at[parity], sems.at[2])

    def first():
        copy().start()
        mine().start()

    def last():
        arriving().wait_recv()
        copy().wait_send()
        mine().wait()

    return [first] + [lambda: None] * delay + [last]


PIECE = 96
GAP = 2


def row_pieces(rs):
    return [(begin, min(PIECE, rs)) for begin in range(0, rs, PIECE)]


FULL = ((0, 0), (1, 0), (2, 0), (3, 0), (1, 1))
ALONG = ((0, 1), (2, 1), (3, 1))


def gather_kernel(rows, cols, *refs):
    refs = list(refs)

    def take(number):
        taken = refs[:number]
        del refs[:number]
        return taken

    full_count, lined_count = len(FULL), len(ALONG)
    mats, (small, tokens, marks) = take(4), take(3)
    full = [mats[index].at[layer] for index, layer in FULL]
    lined = [mats[index].at[layer] for index, layer in ALONG]
    full_out, lined_out = take(full_count), take(lined_count)
    small_out, hidden, marks_out = take(3)
    slots, wide, lined_slots = take(full_count), take(full_count), take(lined_count)
    local_sems, line_sems, chip_sems, core_sems, exchange_sems = refs
    place = Place(rows, cols)
    place.greet()
    items = [
        (0, exchange_item(place, marks, marks_out, exchange_sems.at[1], 16)),
        (0, gather_line_item(place, small, small_out, None, local_sems.at[0, 0], line_sems.at[0])),
    ]
    number = 0
    for index in range(full_count):
        for piece in row_pieces(full[index].shape[0]):
            stages = gather_item(
                place,
                full[index],
                slots[index],
                wide[index],
                full_out[index],
                piece,
                local_sems.at[number + 1],
                line_sems.at[number + 1],
                chip_sems.at[number],
                core_sems.at[number],
            )
            items.append((number, stages))
            number += 1
    items.append((number, exchange_item(place, tokens, hidden, exchange_sems.at[0], 16)))
    for index in range(lined_count):
        at = number + index
        stages = gather_line_item(
            place,
            lined[index],
            lined_slots[index],
            lined_out[index],
            local_sems.at[at + 1, 0],
            line_sems.at[at + 1],
        )
        items.append((at, stages))
    run_stages(items)


def gather_all(rows, cols, mats, small, tokens, marks):
    full = [jax.ShapeDtypeStruct(mats[index].shape[1:], BF16) for index, _ in FULL]
    lined = [jax.ShapeDtypeStruct(mats[index].shape[1:], BF16) for index, _ in ALONG]
    number = sum(len(row_pieces(x.shape[0])) for x in full)
    phases = rows.bit_length() - 2
    like = lambda x, lead=(): jax.ShapeDtypeStruct(lead + x.shape, x.dtype)
    wide = [(x.shape[0], cols * x.shape[1]) for x in full]
    outs = [jax.ShapeDtypeStruct((rows // 2, 2) + shape, BF16) for shape in wide]
    outs += [jax.ShapeDtypeStruct((x.shape[0], cols * x.shape[1]), BF16) for x in lined]
    outs += [like(small, (cols,)), like(tokens), like(marks)]
    return pl.pallas_call(
        functools.partial(gather_kernel, rows, cols),
        out_shape=tuple(outs),
        in_specs=[ANY_SPEC] * 7,
        out_specs=(ANY_SPEC,) * len(full) + (VMEM_SPEC,) * len(lined) + (ANY_SPEC,) * 3,
        scratch_shapes=[pltpu.VMEM((cols,) + x.shape, BF16) for x in full]
        + [pltpu.VMEM(shape, BF16) for shape in wide]
        + [pltpu.VMEM((cols,) + x.shape, BF16) for x in lined]
        + [
            DMA((number + len(lined) + 1, 2)),
            DMA((number + len(lined) + 1, 2, 2, cols - 1)),
            DMA((number, 2, phases, 2, 2 ** (phases - 1))),
            DMA((number, 2)),
            DMA((2, 3)),
        ],
        compiler_params=pltpu.CompilerParams(
            collective_id=0, has_side_effects=True, vmem_limit_bytes=50 << 20
        ),
    )(*mats, small, tokens, marks)


class LineReduce:
    def __init__(self, place, slot, arrived, sems):
        self.place, self.slot, self.arrived, self.sems = place, slot, arrived, sems

    def copies(self, hop, receiving):
        place = self.place
        last = place.cols - 1
        for way, step in ((0, 1), (1, -1)):
            here = place.col if way == 0 else last - place.col
            from_start = here if not receiving else here - 1
            slot = last - hop + from_start
            valid = (from_start <= hop) & (from_start >= 0) & (from_start < last)
            slot = slot if way == 0 else last - slot
            yield valid, slot, way, lambda way=way, slot=slot, step=step: remote(
                self.slot(slot),
                self.arrived.at[way, hop],
                self.sems.at[0, way, hop],
                self.sems.at[1, way, hop],
                (place.row, place.col + step),
            )

    def start(self, hop):
        for valid, _, _, copy in self.copies(hop, False):
            pl.when(valid)(lambda copy=copy: copy().start())

    def wait_send(self, hop):
        for valid, _, _, copy in self.copies(hop, False):
            pl.when(valid)(lambda copy=copy: copy().wait_send())

    def take(self, hop):
        for valid, slot, way, copy in self.copies(hop, True):

            def add(slot=slot, way=way, copy=copy):
                pltpu.make_async_copy(
                    self.arrived.at[way, hop], self.arrived.at[way, hop], self.sems.at[1, way, hop]
                ).wait()
                ref = self.slot(slot)
                ref[...] = ref[...] + self.arrived.at[way, hop][...]

            pl.when(valid)(add)

    def finish(self, out):
        hop = self.place.cols - 2
        own = self.slot(self.place.col)
        out[...] = own[...].astype(F32)
        for valid, _, way, copy in self.copies(hop, True):

            def add(way=way):
                pltpu.make_async_copy(
                    self.arrived.at[way, hop], self.arrived.at[way, hop], self.sems.at[1, way, hop]
                ).wait()
                out[...] = out[...] + self.arrived.at[way, hop][...].astype(F32)

            pl.when(valid)(add)
        for hop in range(self.place.cols - 1):
            self.wait_send(hop)


def line_stages(line, out, before):
    hops = line.place.cols - 1

    def first():
        before()
        line.start(0)

    def hop_stage(hop):
        line.take(hop - 1)
        line.start(hop)

    return (
        [first]
        + [functools.partial(hop_stage, hop) for hop in range(1, hops)]
        + [lambda: line.finish(out)]
    )


def chunk_columns(x, y):
    width = y.shape[1] // max(1, x.shape[1] * y.shape[1] // (768 * 768))
    width = -(-width // 128) * 128
    return [slice(at, at + width) for at in range(0, y.shape[1], width)]


def product_step(place, x, y, sums, away, chunk):
    cols = chunk_columns(x, y)[chunk]
    result = lax.dot_general(
        x[...], y[:, cols], (((0,), (0,)), ((), ())), preferred_element_type=F32
    ).astype(BF16)
    size = sums.shape[1]
    for pair in range(place.rows // 2):
        even = result[2 * pair * size : (2 * pair + 1) * size]
        odd = result[(2 * pair + 1) * size : (2 * pair + 2) * size]
        sums[pair, :, cols] = jnp.where(place.core == 0, even, odd)
        away[pair, :, cols] = jnp.where(place.core == 0, odd, even)


def reduce_item(place, partial, away, out, sums, from_core, from_chips, slots, from_line, piece, sems):
    local_sem, core_sems, chip_sems, line_sems = sems
    phases = len(place.bits)
    rows = pl.ds(*piece)
    core_copy = lambda: remote(
        away.at[:, rows] if partial is None else partial.at[:, 1 - place.core, rows],
        from_core.at[:, rows],
        core_sems.at[0],
        core_sems.at[1],
        place.partner(0),
    )
    load = lambda: pltpu.make_async_copy(
        partial.at[:, place.core, rows], sums.at[:, rows], local_sem
    )
    line = LineReduce(
        place, lambda col: slots.at[col, rows], from_line.at[:, :, rows], line_sems
    )

    def chip_parts(phase):
        for part, span in enumerate(cut(*piece)):
            order = place.orders[part][::-1]
            yield part, pl.ds(*span), order[phase], order[phase + 1 :]

    def chip_copies(phase):
        for part, span, bit, rest in chip_parts(phase):
            for index, row in enumerate(place.others(rest)):
                row = place.flipped(row, bit)
                yield remote(
                    sums.at[row // 2, span],
                    from_chips[phase].at[index, span],
                    chip_sems.at[0, phase, part, index],
                    chip_sems.at[1, phase, part, index],
                    place.partner(bit),
                )

    def chip_take(phase):
        for part, span, _, rest in chip_parts(phase):
            for index, row in enumerate(place.others(rest)):
                arrived = from_chips[phase].at[index, span]
                pltpu.make_async_copy(arrived, arrived, chip_sems.at[1, phase, part, index]).wait()
                ref = sums.at[row // 2, span]
                ref[...] = ref[...] + arrived[...]

    def first():
        core_copy().start()
        if partial is not None:
            load().start()

    def chip_stage(phase):
        if phase == 0:
            if partial is not None:
                load().wait()
            core_copy().wait_recv()

            def add(pair, carry):
                ref = sums.at[pair, rows]
                ref[...] = ref[...] + from_core.at[pair, rows][...]
                return carry

            lax.fori_loop(0, place.rows // 2, add, 0)
        else:
            chip_take(phase - 1)
        for copy in chip_copies(phase):
            copy.start()

    def to_slots():
        chip_take(phases - 1)
        take_apart(sums.at[place.row // 2], rows, slots)

    def last():
        core_copy().wait_send()
        for phase in range(phases):
            for copy in chip_copies(phase):
                copy.wait_send()

    return (
        [first]
        + [functools.partial(chip_stage, phase) for phase in range(phases)]
        + line_stages(line, out.at[rows], to_slots)
        + [last]
    )


def reduce_line_item(place, partial, out, slots, from_line, line_sems):
    line = LineReduce(place, lambda col: slots.at[col], from_line, line_sems)
    return line_stages(line, out, lambda: take_apart(partial, slice(None), slots))


def reduce_small_item(place, partial, out, sums, arrived, from_line, sems, line_sems):
    bits = [0, *place.bits]
    line = LineReduce(place, lambda col: sums.at[col], from_line, line_sems)
    copy = lambda index: remote(
        sums, arrived.at[index], sems.at[0, index], sems.at[1, index], place.partner(bits[index])
    )

    def take(index):
        copy(index).wait()
        sums[...] = sums[...] + arrived[index]

    def stage(index):
        if index == 0:
            sums[...] = partial[...]
        else:
            take(index - 1)
        copy(index).start()

    return [functools.partial(stage, index) for index in range(len(bits))] + line_stages(
        line, out, lambda: take(len(bits) - 1)
    )


READY = ((1, 1), (0, 0))
PRODUCTS = ((2, 0), (1, 0), (3, 0))
LINED = ((0, 1), (2, 1), (3, 1))
SHARER, SHARED = 4, 1


def reduce_kernel(rows, cols, *refs):
    phases = rows.bit_length() - 2
    refs = list(refs)

    def take(number):
        taken = refs[:number]
        del refs[:number]
        return taken

    ready, factors, line_in = take(len(READY)), take(2 * len(PRODUCTS)), take(len(LINED))
    (small_in, tokens), mats_out, (small_out, tokens_out) = take(2), take(4), take(2)
    shard_of = lambda name: mats_out[name[0]].at[name[1]]
    held, [factor_sems] = take(2 * len(PRODUCTS) - 1), take(1)
    held.insert(SHARER, held[SHARED])
    place = Place(rows, cols)
    items = []
    small_sums, small_arrived, small_line, small_sems, small_line_sems = take(5)
    [token_sems] = take(1)
    parity = place.col % 2
    token_copy = lambda: remote(
        tokens, tokens_out, token_sems.at[0], token_sems.at[1], (place.row, place.col + 1 - 2 * parity)
    )
    starts, steps = {(0, 0): 0, (1, 1): 1, (2, 0): 2, (1, 0): 3, (3, 0): 4}, []
    times = {(2, 0): (0, 0, 1, 1), (1, 0): (2,), (3, 0): (2, 2, 3, 3)}
    loads = [
        pltpu.make_async_copy(factors[i], held[i], factor_sems.at[i]) for i in range(len(factors))
    ]
    for index, load in enumerate(loads):
        if index != SHARER:
            load.start()
    place.greet()
    for index, name in enumerate(READY + PRODUCTS):
        sums, from_core, slots, from_line = take(4)
        from_chips = take(phases)
        local_sems, core_sems, chip_sems, line_sems = take(4)
        partial, away = (ready[index], None) if name in READY else (None, *take(1))
        if partial is None:
            at = 2 * (index - len(READY))
            x, y = held[at], held[at + 1]
            steps.append((times[name][0], [lambda at=at: (loads[at].wait(), loads[at + 1].wait())]))
            for chunk in range(len(chunk_columns(x, y))):
                step = functools.partial(product_step, place, x, y, sums, away, chunk)
                steps.append((times[name][chunk], [step]))
            if at + 1 == SHARED:
                steps.append((times[name][-1], [loads[SHARER].start]))
        for number, piece in enumerate(row_pieces(sums.shape[1])):
            stages = reduce_item(
                place,
                partial,
                away,
                shard_of(name),
                sums,
                from_core,
                from_chips,
                slots,
                from_line,
                piece,
                (local_sems.at[number], core_sems.at[number], chip_sems.at[number], line_sems.at[number]),
            )
            items.append((starts[name] + number, stages))
    for index, name in enumerate(LINED):
        slots, from_line, line_sems = take(3)
        items.append(
            (index, reduce_line_item(place, line_in[index], shard_of(name), slots, from_line, line_sems))
        )
    items.append(
        (1, reduce_small_item(place, small_in, small_out, small_sums, small_arrived, small_line, small_sems, small_line_sems))
    )
    items.append(
        (0, [lambda: token_copy().start()] + [lambda: None] * 12 + [lambda: token_copy().wait()])
    )
    run_stages(items + steps)


def reduce_all(rows, cols, ready, products, lined, small, tokens):
    phases = rows.bit_length() - 2
    hops = cols - 1
    full = [x.shape[2:] for x in ready] + [(x.shape[1] // rows, y.shape[1]) for x, y in products]
    shard = lambda shape: (shape[0], shape[1] // cols)
    shapes = dict(zip(READY + PRODUCTS, full)) | {n: x.shape for n, x in zip(LINED, lined)}
    outs = [jax.ShapeDtypeStruct((2,) + shard(shapes[index, 0]), F32) for index in range(4)]
    outs.append(jax.ShapeDtypeStruct(small.shape[1:], F32))
    outs.append(jax.ShapeDtypeStruct(tokens.shape, tokens.dtype))
    factors = [factor for pair in products for factor in pair]
    scratch = [pltpu.VMEM(x.shape, BF16) for i, x in enumerate(factors) if i != SHARER]
    scratch.append(DMA((len(factors),)))
    scratch += [
        pltpu.VMEM(small.shape, F32),
        pltpu.VMEM((phases + 1,) + small.shape, F32),
        pltpu.VMEM((2, hops) + small.shape[1:], F32),
        DMA((2, phases + 1)),
        DMA((2, 2, hops)),
        DMA((2,)),
    ]
    for index, shape in enumerate(full):
        count = len(row_pieces(shape[0]))
        scratch += [
            pltpu.VMEM((rows // 2,) + shape, BF16),
            pltpu.VMEM((rows // 2,) + shape, BF16),
            pltpu.VMEM((cols,) + shard(shape), BF16),
            pltpu.VMEM((2, hops) + shard(shape), BF16),
        ]
        scratch += [
            pltpu.VMEM((2 ** (phases - 1 - phase),) + shape, BF16) for phase in range(phases)
        ]
        scratch += [
            DMA((count,)),
            DMA((count, 2)),
            DMA((count, 2, phases, 2, 2 ** (phases - 1))),
            DMA((count, 2, 2, hops)),
        ]
        if index >= len(ready):
            scratch.append(pltpu.VMEM((rows // 2,) + shape, BF16))
    for x in lined:
        scratch += [
            pltpu.VMEM((cols,) + shard(x.shape), BF16),
            pltpu.VMEM((2, hops) + shard(x.shape), BF16),
            DMA((2, 2, hops)),
        ]
    return pl.pallas_call(
        functools.partial(reduce_kernel, rows, cols),
        out_shape=tuple(outs),
        in_specs=[ANY_SPEC] * (len(ready) + len(factors))
        + [VMEM_SPEC] * (len(lined) + 1)
        + [ANY_SPEC],
        out_specs=(VMEM_SPEC,) * 5 + (ANY_SPEC,),
        scratch_shapes=scratch,
        compiler_params=pltpu.CompilerParams(
            collective_id=1, has_side_effects=True, vmem_limit_bytes=62 << 20
        ),
    )(*ready, *factors, *lined, small, tokens)


def shards(
    rows, cols, tokens, seg_ids, pad_mask, rand_blocks, w_qkv, w_out, w_up, w_down, layer_vectors, bias_up, d_out
):
    layers = w_qkv.shape[0]
    parity = lax.axis_index("col") % 2
    half = seg_ids.shape[1]
    chosen = rand_blocks.reshape(2, 1, -1)
    chosen = jnp.pad(chosen, ((0, 0), (0, 0), (0, 128 - chosen.shape[2])))
    marks = jnp.concatenate(
        [seg_ids.reshape(2, -1, 128), pad_mask.reshape(2, -1, 128), chosen], axis=1
    )
    marks = jnp.pad(marks, ((0, 0), (0, -marks.shape[1] % 8), (0, 0)))
    part = layer_vectors.shape[2]
    small = jnp.concatenate([layer_vectors.reshape(-1, part), bias_up.reshape(-1, part)])
    small_rows = small.shape[0]
    small = jnp.pad(small, ((0, -small_rows % 16), (0, 0)))
    got = gather_all(rows, cols, (w_qkv, w_out, w_up, w_down), small, tokens, marks)
    vectors = got[8][:, : layers * 8].transpose(1, 0, 2).reshape(layers, 8, -1).astype(F32)
    up_biases = got[8][:, layers * 8 : small_rows].reshape(cols, layers, -1).transpose(1, 0, 2)
    up_biases = up_biases.reshape(layers, -1).astype(F32)
    hidden = got[9].reshape(2 * half, -1)
    marks = got[10]
    lines = half // 128
    seg, pad = marks[:, :lines].reshape(-1), marks[:, lines : 2 * lines].reshape(-1)
    rand = marks[:, 2 * lines, : half // BLOCK * rand_blocks.shape[2]]
    pattern = key_pattern(seg, pad, rand.reshape(-1, rand_blocks.shape[2]))

    whole = [g.reshape(-1, g.shape[3]) for g in got[:5]]
    qkv, up, down = (lax.all_gather(g, "row", axis=0, tiled=True) for g in got[5:8])
    first_mats, second_mats = whole[:4], (qkv, whole[4], up, down)
    weights = [
        (*layer_mats, vectors[layer], up_biases[layer])
        for layer, layer_mats in enumerate((first_mats, second_mats))
    ]
    kept = []
    for layer in range(layers):
        hidden, saved = layer_forward(hidden, weights[layer], pattern)
        kept.append(saved)
    output = from_sequence(hidden, parity)
    flow = to_sequence(d_out, parity).astype(F32)

    def product(x, y):
        return jnp.einsum("td,te->de", x, y, preferred_element_type=F32).astype(BF16)

    def settle_first(kind, x, y):
        return (product(x, y) if kind == "qkv" else (x, y)), y

    def settle_second(kind, x, y):
        mat, y = lax.optimization_barrier((product(x, y), y))
        if kind != "out":
            mat = lax.psum_scatter(mat, "row", scatter_dimension=0, tiled=True)
        return mat, y

    grads, vec_grads, up_grads = [None] * layers, [None] * layers, [None] * layers
    flow, grads[1], vec_grads[1], up_grads[1] = layer_backward(
        flow, weights[1], kept[1], pattern, settle_second, lambda x: x
    )
    qkv, out, up, down = grads[1]
    flow, down = lax.optimization_barrier((flow, down))
    held = []

    def after(x):
        x, other = lax.optimization_barrier((x, up))
        held.append(other)
        return x

    flow, grads[0], vec_grads[0], up_grads[0] = layer_backward(
        flow, weights[0], kept[0], pattern, settle_first, after
    )
    split_rows = lambda mat: mat.reshape(rows // 2, 2, -1, mat.shape[1])
    ready = [split_rows(out), split_rows(grads[0][0])]
    lined = [qkv, held[0], down]
    small = jnp.concatenate(
        [
            jnp.stack(vec_grads).reshape(layers * 8, cols, part).transpose(1, 0, 2),
            jnp.stack(up_grads).reshape(layers, cols, -1, part).transpose(1, 0, 2, 3).reshape(cols, -1, part),
        ],
        axis=1,
    )
    halves = flow.reshape(2, half, -1)
    products = [grads[0][i] for i in (2, 1, 3)]
    leaving = pick(halves, 1 - parity).astype(BF16)
    summed = reduce_all(rows, cols, ready, products, lined, small, leaving)
    d_tokens = chosen_by(parity, halves, summed[5].astype(F32))
    mats = summed[:4]
    vec = summed[4][: layers * 8].reshape(layers, 8, part)
    ups = summed[4][layers * 8 :].reshape(layers, -1)
    return output, d_tokens, *mats, vec, ups


def solution(mesh):
    in_specs = (
        P(None, ("row", "col"), None),
        P(None, ("row", "col")),
        P(None, ("row", "col")),
        P(None, ("row", "col"), None),
        P(None, "row", "col"),
        P(None, "row", "col"),
        P(None, "row", "col"),
        P(None, "row", "col"),
        P(None, None, "col"),
        P(None, "col"),
        P(None, ("row", "col"), None),
    )
    out_specs = (
        P(None, ("row", "col"), None),
        P(None, ("row", "col"), None),
        P(None, "row", "col"),
        P(None, "row", "col"),
        P(None, "row", "col"),
        P(None, "row", "col"),
        P(None, None, "col"),
        P(None, "col"),
    )
    local = functools.partial(shards, mesh.shape["row"], mesh.shape["col"])
    return jax.shard_map(local, mesh=mesh, in_specs=in_specs, out_specs=out_specs, check_vma=False)
```
